32 devices in a mesh: dp: 4 (over z), blk: 8 (over y, x, core).
Axes of the slice: x: 2, y: 2, z: 4, core: 2. Of those that a mesh axis runs over, the one named last changes fastest.
Arguments:
- inputs: bfloat16 [4, 1024, 768], P('dp', 'blk'), may hold values from -6 to 6
- crops: int32 [4, 1024], P('dp'), may hold values from 0 to 3, as said below
- ln1_gain: float32 [768], replicated, may hold values from 0.1 to 1.9
- ln1_bias: float32 [768], replicated, may hold values from -3 to 3
- w_qkv: bfloat16 [768, 2304], replicated, may hold values from -0.21875 to 0.21875
- w_proj: bfloat16 [768, 768], replicated, may hold values from -1.75 to 1.75
- ln2_gain: float32 [768], replicated, may hold values from 0.1 to 1.9
- ln2_bias: float32 [768], replicated, may hold values from -3 to 3
- w_fc1: bfloat16 [768, 3072], replicated, may hold values from -0.21875 to 0.21875
- w_fc2: bfloat16 [3072, 768], replicated, may hold values from -0.109375 to 0.109375
- cotangent: bfloat16 [4, 1024, 768], P('dp', 'blk'), may hold values from -6 to 6
Outputs:
- output: bfloat16 [4, 1024, 768], P('dp', 'blk')
- grad_input: bfloat16 [4, 1024, 768], P('dp', 'blk')
- grad_qkv: float32 [768, 2304], P('blk')
- grad_proj: float32 [768, 768], P('blk')
- grad_fc1: float32 [768, 3072], P('blk')
- grad_fc2: float32 [3072, 768], P('blk')
- grad_ln1_gain: float32 [768], P('blk')
- grad_ln1_bias: float32 [768], P('blk')
- grad_ln2_gain: float32 [768], P('blk')
- grad_ln2_bias: float32 [768], P('blk')
The draws below stay inside these ranges and needn't reach their ends.
Inputs may be any that keep to these rules, and one draw needn't show every extreme that they name: `crops`: crop numbers are constant on aligned runs of 128 positions, and each crop of a sequence holds 256 positions.
All inputs are finite; a program needn't handle non-finite values.
Results may differ from the reference program's by a relative error of at most 0.019.
Values may be sent and summed in bfloat16 or wider, within the bound.
A program may use at most 192 MiB of HBM per device.

```python
from functools import partial
import jax
import jax.numpy as jnp
from jax import lax

D = 768
HEADS = 12
HEAD_DIM = 64
FF = 3072
NCROP = 4
RUN = 128
BATCH = 4
L = 1024


def draw_crops(key, part):
    key = jax.random.fold_in(key, 7)
    run_count = L // RUN
    seq_keys = jax.random.split(key, BATCH)

    def one_sequence(seq_key):
        shuffled = jax.random.permutation(seq_key, run_count)
        return jnp.repeat(shuffled % NCROP, RUN)
    return jax.vmap(one_sequence)(seq_keys).astype(jnp.int32)


def block_scale(rng, extent, pieces, smallest, high):
    def one(axis_at, blocks):
        draws = jax.random.uniform(jax.random.fold_in(jax.random.fold_in(rng, 6), axis_at), (blocks,), jnp.float32, smallest / len(pieces), high / len(pieces))
        return jnp.repeat(jnp.exp(draws), extent[axis_at] // blocks).reshape((-1,) + (1,) * (len(extent) - axis_at - 1))

    gain = one(*pieces[0])
    for cut in pieces[1:]:
        gain = gain * one(*cut)
    return gain


def gaussian(own_key, shape, scale, reach, shards=(), dtype=jnp.bfloat16):
    values = jax.random.normal(own_key, shape, jnp.float32) * scale
    if len(shards) > 0:
        values = block_scale(own_key, shape, shards, -0.22, 0.18) * values
    return jnp.clip(values, min=-reach, max=reach).astype(dtype)


def setup_inputs(seed: int = 0) -> dict:
    key_list = jax.random.split(jax.random.key(seed), 12)
    inputs = gaussian(key_list[0], (BATCH, L, D), 1.0, 6.0, ((0, 4), (1, 8)))
    crops = draw_crops(jax.random.fold_in(key_list[11], 71), 0)
    ln1_gain = jnp.clip(1.0 + 0.18 * jax.random.normal(key_list[2], (D,), jnp.float32), 0.1, 1.9)
    ln1_bias = gaussian(key_list[3], (D,), 0.5, 3.0, (), jnp.float32)
    w_qkv = gaussian(key_list[4], (D, 3 * D), D ** -0.5, 0.21875)
    w_proj = gaussian(key_list[5], (D, D), (max(1, 4 * D * NCROP // L)) ** -0.5, 1.75)
    ln2_gain = jnp.clip(1.0 + 0.18 * jax.random.normal(key_list[6], (D,), jnp.float32), 0.1, 1.9)
    ln2_bias = gaussian(key_list[7], (D,), 0.5, 3.0, (), jnp.float32)
    w_fc1 = gaussian(key_list[8], (D, FF), D ** -0.5, 0.21875)
    w_fc2 = gaussian(key_list[9], (FF, D), FF ** -0.5, 0.109375)
    cotangent = gaussian(key_list[10], (BATCH, L, D), 1.0, 6.0, ((0, 4), (1, 8)))
    return dict(inputs=inputs, crops=crops, ln1_gain=ln1_gain, ln1_bias=ln1_bias, w_qkv=w_qkv, w_proj=w_proj, ln2_gain=ln2_gain, ln2_bias=ln2_bias, w_fc1=w_fc1, w_fc2=w_fc2, cotangent=cotangent)


EPSILON = 1e-05
MASKED = -1e+30
HIGH = lax.Precision.HIGHEST

@jax.custom_vjp
def low(v):
    return lax.optimization_barrier(v.astype(jnp.bfloat16)).astype(jnp.float32)

@jax.custom_vjp
def low_back(v):
    return v

def low_keep(v):
    return (low(v), None)

def low_pass(kept, grad):
    return (grad,)

def back_keep(v):
    return (v, None)

def back_low(kept, grad):
    return (low(grad),)
low.defvjp(low_keep, low_pass)
low_back.defvjp(back_keep, back_low)

def layer_norm(values_in, gain_in, shift_in):
    row_mean = lax.optimization_barrier(jnp.mean(values_in, axis=-1, keepdims=True))
    centred = values_in - row_mean
    row_var = lax.optimization_barrier(jnp.mean(centred * centred, axis=-1, keepdims=True))
    return centred * lax.rsqrt(row_var + EPSILON) * gain_in + shift_in

def attend_rows(query_rows, crop_rows, key_rows, value_rows, crop_keys):
    score_scale = HEAD_DIM ** (-0.5)
    scores = jnp.einsum('qhd,khd->hqk', query_rows, key_rows, precision=HIGH) * score_scale
    scores = low_back(scores)
    visible = crop_rows[:, None] == crop_keys[None, :]
    attn_probs = jax.nn.softmax(jnp.where(visible[None], scores, MASKED), axis=-1)
    attn_probs = low(attn_probs)
    return jnp.einsum('hqk,khd->qhd', attn_probs, value_rows, precision=HIGH)

def attend_sequence(query_seq, key_seq, value_seq, crop_seq):
    row_block = min(512, L)
    block_count = L // row_block
    query_blocks = query_seq.reshape(block_count, row_block, HEADS, HEAD_DIM)
    crop_blocks = crop_seq.reshape(block_count, row_block)

    def one_block(block_items):
        return attend_rows(block_items[0], block_items[1], key_seq, value_seq, crop_seq)
    outputs = lax.map(jax.checkpoint(one_block), (query_blocks, crop_blocks))
    return outputs.reshape(L, HEADS, HEAD_DIM)

def forward(inputs, ln1_gain, ln1_bias, w_qkv, w_proj, ln2_gain, ln2_bias, w_fc1, w_fc2, crops):
    batch_size = inputs.shape[0]
    normed_one = low(layer_norm(inputs, ln1_gain, ln1_bias))
    qkv_rows = low_back(low(jnp.einsum('bld,de->ble', normed_one, w_qkv, precision=HIGH)))
    query_all = qkv_rows[:, :, :D].reshape(batch_size, L, HEADS, HEAD_DIM)
    key_all = qkv_rows[:, :, D:2 * D].reshape(batch_size, L, HEADS, HEAD_DIM)
    value_all = qkv_rows[:, :, 2 * D:].reshape(batch_size, L, HEADS, HEAD_DIM)

    def one_sequence(seq_items):
        return attend_sequence(seq_items[0], seq_items[1], seq_items[2], seq_items[3])
    attended = lax.map(one_sequence, (query_all, key_all, value_all, crops))
    attended = low_back(low(attended.reshape(batch_size, L, D)))
    mixed_rows = inputs + low_back(jnp.einsum('bld,de->ble', attended, w_proj, precision=HIGH))
    normed_two = low(layer_norm(mixed_rows, ln2_gain, ln2_bias))
    hidden_pre = low_back(jnp.einsum('bld,df->blf', normed_two, w_fc1, precision=HIGH))
    active = low(jax.nn.gelu(hidden_pre))
    return mixed_rows + jnp.einsum('blf,fd->bld', active, w_fc2, precision=HIGH)

def reference(inputs, crops, ln1_gain, ln1_bias, w_qkv, w_proj, ln2_gain, ln2_bias, w_fc1, w_fc2, cotangent):
    primals = (inputs.astype(jnp.float32), ln1_gain.astype(jnp.float32), ln1_bias.astype(jnp.float32), w_qkv.astype(jnp.float32), w_proj.astype(jnp.float32), ln2_gain.astype(jnp.float32), ln2_bias.astype(jnp.float32), w_fc1.astype(jnp.float32), w_fc2.astype(jnp.float32))
    result, layer_back = jax.vjp(partial(forward, crops=crops), *primals)
    grads = layer_back(cotangent.astype(jnp.float32))
    return (result.astype(jnp.bfloat16), grads[0].astype(jnp.bfloat16), grads[3], grads[4], grads[7], grads[8], grads[1], grads[2], grads[5], grads[6])
```

```python
import functools
import math

import jax
import jax.numpy as jnp
from jax import lax
from jax.experimental import pallas as pl
from jax.experimental.pallas import tpu as pltpu
from jax.sharding import PartitionSpec as P

HEADS = 12


EPSILON = 1e-05
MASKED = -1e30


def layer_norm(values_in, gain_in, shift_in):
    row_mean = jnp.mean(values_in, axis=-1, keepdims=True)
    centred = values_in - row_mean
    row_var = jnp.mean(centred * centred, axis=-1, keepdims=True)
    return centred * lax.rsqrt(row_var + EPSILON) * gain_in + shift_in


def contract_rows(left_side, right_side):
    return lax.dot_general(
        left_side, right_side, (((0,), (0,)), ((), ())), preferred_element_type=jnp.float32
    )


def against_weight(grad_rows, weight_mat):
    return lax.dot_general(
        grad_rows, weight_mat, (((1,), (1,)), ((), ())), preferred_element_type=jnp.float32
    )


def head_view(matrix, head_count):
    return matrix.reshape(matrix.shape[0], head_count, matrix.shape[1] // head_count)


def scores_of(query_heads, key_heads, score_scale):
    return (
        jnp.einsum("qhd,khd->hqk", query_heads, key_heads, preferred_element_type=jnp.float32)
        * score_scale
    )


def weights_of(scores, visible, logsum):
    return jnp.where(visible[None], jnp.exp(scores - logsum[:, :, None]), 0.0)


def shards(
    inputs, crops, ln1_gain, ln1_bias, w_qkv, w_proj, ln2_gain, ln2_bias, w_fc1, w_fc2, cotangent
):
    row_count = inputs.shape[1]
    model_width = inputs.shape[2]
    head_count = HEADS
    score_scale = 1.0 / math.sqrt(model_width // head_count)
    seq_crops = crops[0]
    seq_len = seq_crops.shape[0]
    key_block = min(1024, seq_len)
    block_count = seq_len // key_block
    block_ids = jnp.arange(block_count)
    own_crops = lax.dynamic_slice_in_dim(seq_crops, lax.axis_index("blk") * row_count, row_count, 0)
    residual = inputs[0].astype(jnp.float32)
    normed_one_low = layer_norm(residual, ln1_gain, ln1_bias).astype(jnp.bfloat16)
    qkv_low = jnp.dot(normed_one_low, w_qkv, preferred_element_type=jnp.float32).astype(
        jnp.bfloat16
    )
    query_own = qkv_low[:, :model_width]
    key_own = qkv_low[:, model_width : 2 * model_width]
    value_own = qkv_low[:, 2 * model_width :]
    keys_all, values_all = (
        lax.all_gather(key_own, "blk", axis=0, tiled=True),
        lax.all_gather(value_own, "blk", axis=0, tiled=True),
    )
    query_heads = head_view(query_own, head_count)

    def block_inputs(block_index):
        key_heads = head_view(
            lax.dynamic_slice_in_dim(keys_all, block_index * key_block, key_block, 0), head_count
        )
        value_heads = head_view(
            lax.dynamic_slice_in_dim(values_all, block_index * key_block, key_block, 0), head_count
        )
        crop_block = lax.dynamic_slice_in_dim(seq_crops, block_index * key_block, key_block, 0)
        visible = own_crops[:, None] == crop_block[None, :]
        return (key_heads, value_heads, visible)

    def stats_step(carried, block_index):
        old_max, summed = carried
        key_heads, value_heads, visible = block_inputs(block_index)
        scores = jnp.where(visible[None], scores_of(query_heads, key_heads, score_scale), MASKED)
        new_max = jnp.maximum(old_max, jnp.max(scores, axis=-1))
        exp_terms = jnp.where(visible[None], jnp.exp(scores - new_max[:, :, None]), 0.0)
        return ((new_max, summed * jnp.exp(old_max - new_max) + jnp.sum(exp_terms, axis=-1)), None)

    start_max = jnp.full((head_count, row_count), MASKED, jnp.float32)
    start_sum = jnp.zeros((head_count, row_count), jnp.float32)
    (row_max, summed), _ = lax.scan(stats_step, (start_max, start_sum), block_ids)
    logsum = row_max + jnp.log(summed)

    def output_step(running, block_index):
        key_heads, value_heads, visible = block_inputs(block_index)
        attn_probs = weights_of(
            scores_of(query_heads, key_heads, score_scale), visible, logsum
        ).astype(jnp.bfloat16)
        return (
            running
            + jnp.einsum(
                "hqk,khd->qhd", attn_probs, value_heads, preferred_element_type=jnp.float32
            ),
            None,
        )

    attended, _ = lax.scan(output_step, jnp.zeros(query_heads.shape, jnp.float32), block_ids)
    attended_low = attended.reshape(row_count, model_width).astype(jnp.bfloat16)
    mixed_rows = residual + jnp.dot(attended_low, w_proj, preferred_element_type=jnp.float32)
    normed_two_low = layer_norm(mixed_rows, ln2_gain, ln2_bias).astype(jnp.bfloat16)
    hidden_pre = jnp.dot(normed_two_low, w_fc1, preferred_element_type=jnp.float32)
    active, gelu_back = jax.vjp(jax.nn.gelu, hidden_pre)
    active_low = active.astype(jnp.bfloat16)
    result = mixed_rows + jnp.dot(active_low, w_fc2, preferred_element_type=jnp.float32)
    output = result.astype(jnp.bfloat16)[None]
    grad_out_low = cotangent[0]
    grad_fc2 = contract_rows(active_low, grad_out_low)
    grad_active = against_weight(grad_out_low, w_fc2)
    grad_hidden_low = gelu_back(grad_active)[0].astype(jnp.bfloat16)
    grad_fc1 = contract_rows(normed_two_low, grad_hidden_low)
    grad_normed_two = against_weight(grad_hidden_low, w_fc1)
    _, norm_two_back = jax.vjp(layer_norm, mixed_rows, ln2_gain, ln2_bias)
    grad_mixed_part, grad_gain_two, grad_bias_two = norm_two_back(grad_normed_two)
    grad_mixed = grad_out_low.astype(jnp.float32) + grad_mixed_part
    grad_mixed_low = grad_mixed.astype(jnp.bfloat16)
    grad_proj = contract_rows(attended_low, grad_mixed_low)
    grad_attended_low = against_weight(grad_mixed_low, w_proj).astype(jnp.bfloat16)
    grad_heads = head_view(grad_attended_low, head_count)

    def delta_step(running, block_index):
        key_heads, value_heads, visible = block_inputs(block_index)
        attn_probs = weights_of(scores_of(query_heads, key_heads, score_scale), visible, logsum)
        grad_probs = jnp.einsum(
            "qhd,khd->hqk", grad_heads, value_heads, preferred_element_type=jnp.float32
        )
        return (running + jnp.sum(attn_probs * grad_probs, axis=-1), None)

    row_delta, _ = lax.scan(delta_step, jnp.zeros((head_count, row_count), jnp.float32), block_ids)

    def score_grads(
        query_part, grad_part, logsum_part, delta_part, key_heads, value_heads, visible
    ):
        attn_probs = weights_of(scores_of(query_part, key_heads, score_scale), visible, logsum_part)
        grad_probs = jnp.einsum(
            "qhd,khd->hqk", grad_part, value_heads, preferred_element_type=jnp.float32
        )
        grad_scores = (attn_probs * (grad_probs - delta_part[:, :, None])).astype(jnp.bfloat16)
        return (attn_probs, grad_scores)

    def pair_step(running, block_index):
        key_heads, value_heads, visible = block_inputs(block_index)
        attn_probs, grad_scores = score_grads(
            query_heads, grad_heads, logsum, row_delta, key_heads, value_heads, visible
        )
        key_term = (
            jnp.einsum("hqk,qhd->khd", grad_scores, query_heads, preferred_element_type=jnp.float32)
            * score_scale
        )
        value_term = jnp.einsum(
            "hqk,qhd->khd",
            attn_probs.astype(jnp.bfloat16),
            grad_heads,
            preferred_element_type=jnp.float32,
        )
        joined = jnp.concatenate(
            [key_term.reshape(key_block, model_width), value_term.reshape(key_block, model_width)],
            axis=1,
        )
        step_query = jnp.einsum(
            "hqk,khd->qhd", grad_scores, key_heads, preferred_element_type=jnp.float32
        )
        return (running + step_query, joined)

    grad_query, key_terms = lax.scan(
        pair_step, jnp.zeros(query_heads.shape, jnp.float32), block_ids
    )
    key_sums = lax.psum_scatter(
        key_terms.reshape(seq_len, 2 * model_width).astype(jnp.bfloat16),
        "blk",
        scatter_dimension=0,
        tiled=True,
    ).astype(jnp.float32)
    grad_key = key_sums[:, :model_width]
    grad_value = key_sums[:, model_width:]
    grad_query = grad_query.reshape(row_count, model_width) * score_scale
    grad_qkv_low = jnp.concatenate([grad_query, grad_key, grad_value], axis=1).astype(jnp.bfloat16)
    grad_wqkv = contract_rows(normed_one_low, grad_qkv_low)
    grad_normed_one = against_weight(grad_qkv_low, w_qkv)
    _, norm_one_back = jax.vjp(layer_norm, residual, ln1_gain, ln1_bias)
    grad_resid, grad_gain_one, grad_bias_one = norm_one_back(grad_normed_one)
    grad_input = (grad_mixed + grad_resid).astype(jnp.bfloat16)[None]
    (
        fc1_share,
        fc2_share,
        qkv_share,
        proj_share,
        gain_one_share,
        bias_one_share,
        gain_two_share,
        bias_two_share,
    ) = (
        lax.psum_scatter(
            grad_fc1.astype(jnp.bfloat16), "blk", scatter_dimension=0, tiled=True
        ).astype(jnp.float32),
        lax.psum_scatter(
            grad_fc2.astype(jnp.bfloat16), "blk", scatter_dimension=0, tiled=True
        ).astype(jnp.float32),
        lax.psum_scatter(
            grad_wqkv.astype(jnp.bfloat16), "blk", scatter_dimension=0, tiled=True
        ).astype(jnp.float32),
        lax.psum_scatter(
            grad_proj.astype(jnp.bfloat16), "blk", scatter_dimension=0, tiled=True
        ).astype(jnp.float32),
        lax.psum_scatter(
            grad_gain_one.astype(jnp.bfloat16), "blk", scatter_dimension=0, tiled=True
        ).astype(jnp.float32),
        lax.psum_scatter(
            grad_bias_one.astype(jnp.bfloat16), "blk", scatter_dimension=0, tiled=True
        ).astype(jnp.float32),
        lax.psum_scatter(
            grad_gain_two.astype(jnp.bfloat16), "blk", scatter_dimension=0, tiled=True
        ).astype(jnp.float32),
        lax.psum_scatter(
            grad_bias_two.astype(jnp.bfloat16), "blk", scatter_dimension=0, tiled=True
        ).astype(jnp.float32),
    )
    totals = (
        lax.psum(qkv_share.astype(jnp.bfloat16), "dp").astype(jnp.float32),
        lax.psum(proj_share.astype(jnp.bfloat16), "dp").astype(jnp.float32),
        lax.psum(fc1_share.astype(jnp.bfloat16), "dp").astype(jnp.float32),
        lax.psum(fc2_share.astype(jnp.bfloat16), "dp").astype(jnp.float32),
        lax.psum(gain_one_share.astype(jnp.bfloat16), "dp").astype(jnp.float32),
        lax.psum(bias_one_share.astype(jnp.bfloat16), "dp").astype(jnp.float32),
        lax.psum(gain_two_share.astype(jnp.bfloat16), "dp").astype(jnp.float32),
        lax.psum(bias_two_share.astype(jnp.bfloat16), "dp").astype(jnp.float32),
    )
    return (
        output,
        grad_input,
        totals[0],
        totals[1],
        totals[2],
        totals[3],
        totals[4],
        totals[5],
        totals[6],
        totals[7],
    )


MESH = pl.DeviceIdType.MESH
F32 = jnp.float32
BF16 = jnp.bfloat16
RUN_ROWS = 128
HEAD = 64


def mm(left, right):
    return lax.dot_general(left, right, (((1,), (0,)), ((), ())), preferred_element_type=F32)


def mm_nt(left, right):
    return lax.dot_general(left, right, (((1,), (1,)), ((), ())), preferred_element_type=F32)


def mm_tn(left, right):
    return lax.dot_general(left, right, (((0,), (0,)), ((), ())), preferred_element_type=F32)


def norm_parts(rows):
    centred = rows - jnp.mean(rows, axis=-1, keepdims=True)
    inv_std = lax.rsqrt(jnp.mean(centred * centred, axis=-1, keepdims=True) + EPSILON)
    return centred * inv_std, inv_std


def norm_back(grad_rows, hat, inv_std, gain):
    grad_hat = grad_rows * gain
    return inv_std * (
        grad_hat
        - jnp.mean(grad_hat, axis=-1, keepdims=True)
        - hat * jnp.mean(grad_hat * hat, axis=-1, keepdims=True)
    )


def gelu_pair(u):
    inner = 0.7978845608028654 * (u + 0.044715 * u * u * u)
    t = jnp.tanh(inner)
    half = 0.5 * (1.0 + t)
    slope = half + 0.5 * u * (1.0 - t * t) * (0.7978845608028654 * (1.0 + 0.134145 * u * u))
    return u * half, slope


def layer_kernel(Z, names, *refs):
    r = dict(zip(names, refs, strict=True))
    z = lax.axis_index("dp")
    b = lax.axis_index("blk")
    e = lax.rem(b, 2)
    chip = b // 2
    cx = lax.rem(chip, 2)
    cy = chip // 2
    scale = HEAD**-0.5

    def chip_at(delta):
        dx, dy = delta % 2, delta // 2
        return 2 * (cy + dy - 2 * cy * dy) + (cx + dx - 2 * cx * dx)

    def dev(delta):
        return (z, 2 * chip_at(delta) + e)

    other = (z, b + 1 - 2 * e)
    slot_other = b + 1 - 2 * e

    def remote(src, dst, send_sem, recv_sem, device):
        return pltpu.make_async_remote_copy(
            src_ref=src, dst_ref=dst, send_sem=send_sem, recv_sem=recv_sem,
            device_id=device, device_id_type=MESH,
        )

    loads = []

    def load(src, dst, at):
        copy = pltpu.make_async_copy(src, dst, r["ld_sem"].at[at])
        copy.start()
        loads.append(copy)

    load(r["x"], r["xb"].at[b], 0)
    for t in range(3):
        first = pl.multiple_of(768 * t + 384 * e, 128)
        load(r["w_qkv"].at[:, pl.ds(first, 384)], r["wf"].at[:, pl.ds(384 * t, 384)], 1 + t)
    load(r["w_proj"], r["wp"], 4)
    load(r["w_fc1"].at[:, pl.ds(pl.multiple_of(384 * b, 128), 384)], r["w1"], 5)
    load(r["w_fc2"].at[pl.ds(pl.multiple_of(384 * b, 128), 384)], r["w2"], 6)
    load(r["dy"], r["dyb"].at[b], 7)
    for t in range(3):
        first = pl.multiple_of(768 * t + 192 * chip - 64 * lax.rem(chip, 2), 128)
        load(r["w_qkv"].at[:, pl.ds(first, 256)], r["w4"].at[t], 8 + t)

    bar = pltpu.get_barrier_semaphore()
    for target in (other, dev(1), dev(2), dev(3)):
        pl.semaphore_signal(bar, inc=1, device_id=target, device_id_type=MESH)

    @pl.when(z > 0)
    def _():
        pl.semaphore_signal(bar, inc=1, device_id=(z - 1, b), device_id_type=MESH)

    @pl.when(z < Z - 1)
    def _():
        pl.semaphore_signal(bar, inc=1, device_id=(z + 1, b), device_id_type=MESH)

    pl.semaphore_wait(bar, 4 + jnp.minimum(z, 1) + jnp.minimum(Z - 1 - z, 1))

    class Gather:
        def __init__(self, buf, ss, rs):
            self.buf, self.ss, self.rs = buf, ss, rs

        def to_chip(self, delta, src):
            return remote(src, self.buf.at[b], self.ss.at[2 * delta], self.rs.at[2 * delta], dev(delta))

        def to_core(self, src):
            return remote(src, self.buf.at[b], self.ss.at[1], self.rs.at[1], other)

        def slot(self, m):
            return 2 * chip_at(m // 2) + (e if m % 2 == 0 else 1 - e)

        def send(self, src):
            for delta in (3, 2, 1):
                self.to_chip(delta, src).start()
            self.to_core(src).start()

        def forward(self, delta):
            at = self.slot(2 * delta)
            return remote(
                self.buf.at[at], self.buf.at[at], self.ss.at[2 * delta + 1],
                self.rs.at[2 * delta + 1], other,
            )

        def wait_chip(self, delta):
            at = self.slot(2 * delta)
            remote(self.buf.at[at], self.buf.at[at], self.ss.at[2 * delta], self.rs.at[2 * delta], dev(delta)).wait_recv()
            self.forward(delta).start()

        def wait_core(self, delta):
            at = self.slot(2 * delta + 1)
            remote(self.buf.at[at], self.buf.at[at], self.ss.at[2 * delta + 1], self.rs.at[2 * delta + 1], other).wait_recv()

        def finish(self, src):
            for delta in (1, 2, 3):
                self.to_chip(delta, src).wait_send()
                self.forward(delta).wait_send()
            self.to_core(src).wait_send()

    gx = Gather(r["xb"], r["gx_s"], r["gx_r"])
    gdy = Gather(r["dyb"], r["gdy_s"], r["gdy_r"])
    gdx = Gather(r["dxb"], r["gdx_s"], r["gdx_r"])
    gdo = Gather(r["dob"], r["gdo_s"], r["gdo_r"])

    class Chain:
        def __init__(self, name, K, dtype, sink):
            self.K, self.dtype, self.sink = K, dtype, sink
            for part in ("own", "rl", "rr", "tu", "td", "su", "sd", "ru", "rd"):
                setattr(self, part, r[name + "_" + part])

        def up(self, src, k):
            return remote(src, self.rl.at[k], self.su.at[k], self.ru.at[k], (z + 1, b))

        def down(self, src, k):
            return remote(src, self.rr.at[k], self.sd.at[k], self.rd.at[k], (z - 1, b))

        def prime(self, k):
            if Z == 1:
                return

            @pl.when(z == 0)
            def _():
                self.up(self.own.at[k], k).start()

            @pl.when(z == Z - 1)
            def _():
                self.down(self.own.at[k], k).start()

        def tick(self, i):
            ku = i - z

            @pl.when((z > 0) & (ku >= 0) & (ku < self.K))
            def _():
                self.up(self.own.at[ku], ku).wait_recv()

                @pl.when(z < Z - 1)
                def _():
                    self.tu[ku] = (self.own[ku].astype(F32) + self.rl[ku].astype(F32)).astype(self.dtype)
                    self.up(self.tu.at[ku], ku).start()

            kd = i - (Z - 1 - z)

            @pl.when((z < Z - 1) & (kd >= 0) & (kd < self.K))
            def _():
                self.down(self.own.at[kd], kd).wait_recv()

                @pl.when(z > 0)
                def _():
                    self.td[kd] = (self.own[kd].astype(F32) + self.rr[kd].astype(F32)).astype(self.dtype)
                    self.down(self.td.at[kd], kd).start()

            k = i - (Z - 1)
            if 0 <= k < self.K:

                @pl.when(z == 0)
                def _():
                    self.sink(k, self.own[k].astype(F32) + self.rr[k].astype(F32))

                @pl.when(z == Z - 1)
                def _():
                    self.sink(k, self.own[k].astype(F32) + self.rl[k].astype(F32))

                @pl.when((z > 0) & (z < Z - 1))
                def _():
                    self.sink(
                        k,
                        self.own[k].astype(F32) + self.rl[k].astype(F32) + self.rr[k].astype(F32),
                    )

        def finish(self):
            @pl.when(z < Z - 1)
            def _():
                for k in range(self.K):
                    self.up(self.own.at[k], k).wait_send()

            @pl.when(z > 0)
            def _():
                for k in range(self.K):
                    self.down(self.own.at[k], k).wait_send()

    def sink_a(k, total):
        low = total.astype(BF16)
        if k < 4:
            r["o_fc2"][96 * k : 96 * k + 96, 0:384] = low[0]
            r["o_fc2"][96 * k : 96 * k + 96, 384:768] = low[1]
        elif k < 8:
            src = chip_at(k - 4)
            r["o_fc1"][:, pl.ds(pl.multiple_of(768 * src, 128), 384)] = low[0]
            r["o_fc1"][:, pl.ds(pl.multiple_of(768 * src + 384, 128), 384)] = low[1]
        else:
            r["o_proj"][:, 0:384] = low[0]
            r["o_proj"][:, 384:768] = low[1]

    def sink_b(k, total):
        r["o_qkv"][chip_at(k)] = total.astype(BF16)

    def sink_c(k, total):
        r["o_ln"][...] = total

    ca = Chain("ca", 9, BF16, sink_a)
    cb = Chain("cb", 4, BF16, sink_b)
    cc = Chain("cc", 1, F32, sink_c)

    class Scatter:
        def __init__(self, name):
            for part in ("ctx", "crx", "keep", "tx", "rx", "cs", "cr", "ss", "sr"):
                setattr(self, part, r[name + "_" + part])

        def core(self, j):
            return remote(self.ctx.at[j], self.crx.at[j], self.cs.at[j], self.cr.at[j], other)

        def send(self, j):
            delta = 3 - j
            return remote(self.tx.at[j], self.rx.at[j], self.ss.at[j], self.sr.at[j], dev(delta))

        def put(self, j, mine, theirs):
            self.keep[j] = mine
            self.ctx[j] = theirs.astype(BF16)
            self.core(j).start()

        def sum_core(self, j):
            self.core(j).wait_recv()
            return self.keep[j] + self.crx[j].astype(F32)

        def result(self):
            total = self.sum_core(3)
            for j in range(3):
                self.send(j).wait_recv()
                total += self.rx[j].astype(F32)
            return total

        def finish(self):
            for j in range(4):
                self.core(j).wait_send()
            for j in range(3):
                self.send(j).wait_send()

    dn = Scatter("dn")
    ys = Scatter("ys")

    gx.send(r["x"])

    crop = [r["crops"][0, RUN_ROWS * i] for i in range(8)]
    places = []
    for i in range(8):
        place = 2 * crop[i]
        for h in range(i):
            place = place + jnp.where(crop[h] == crop[i], 1, 0)
        places.append(place)
        r["inv"][i] = place
    for s in range(8):
        run = jnp.int32(0)
        for i in range(8):
            run = run + jnp.where(places[i] == s, i, 0)
        r["perm"][s] = run

    for copy in loads[:4]:
        copy.wait()
    for copy in loads[8:]:
        copy.wait()
    odd = lax.rem(chip, 2) == 1
    for t in range(3):
        r["wo"][:, 192 * t : 192 * t + 192] = jnp.where(odd, r["w4"][t, :, 64:256], r["w4"][t, :, 0:192])

    g1, b1 = r["ln1_gain"][...], r["ln1_bias"][...]
    g2, b2 = r["ln2_gain"][...], r["ln2_bias"][...]

    for delta in range(4):
        if delta > 0:
            gx.wait_chip(delta)
            gdy.to_chip(delta, r["dy"]).start()
        else:
            gdy.to_core(r["dy"]).start()
        gx.wait_core(delta)
        pair = pl.ds(2 * chip_at(delta), 2)
        hat, _ = norm_parts(r["xb"][pair].reshape(256, 768).astype(F32))
        normed = (hat * g1 + b1).astype(BF16)
        r["n1"][pair] = normed.reshape(2, 128, 768)
        r["qkv"][pair] = mm(normed, r["wf"][...]).astype(BF16).reshape(2, 128, 1152)

    def o_core(at):
        return remote(r["ob"].at[e, pl.ds(2 * at, 2)], r["ob"].at[e, pl.ds(2 * at, 2)], r["o_s"].at[at], r["o_r"].at[at], other)

    def attend(at, carry):
        run0, run1 = r["perm"][2 * at], r["perm"][2 * at + 1]
        rows = jnp.concatenate([r["qkv"][run0], r["qkv"][run1]], axis=0)
        outs = []
        for h in range(6):
            q = rows[:, 64 * h : 64 * h + 64]
            k = rows[:, 384 + 64 * h : 384 + 64 * h + 64]
            v = rows[:, 768 + 64 * h : 768 + 64 * h + 64]
            s = mm_nt(q, k) * scale
            p = jnp.exp(s - jnp.max(s, axis=-1, keepdims=True))
            p = (p / jnp.sum(p, axis=-1, keepdims=True)).astype(BF16)
            outs.append(mm(p, v))
        low = jnp.concatenate(outs, axis=1).astype(BF16)
        r["ob"][e, pl.ds(2 * at, 2)] = low.reshape(2, 128, 384)
        o_core(at).start()
        return carry

    lax.fori_loop(0, 4, attend, 0)

    for delta in (1, 2, 3):
        gdy.wait_chip(delta)
    for delta in range(4):
        gdy.wait_core(delta)
    for copy in loads[4:8]:
        copy.wait()
    for at in range(4):
        remote(r["ob"].at[1 - e, pl.ds(2 * at, 2)], r["ob"].at[1 - e, pl.ds(2 * at, 2)], r["o_s"].at[at], r["o_r"].at[at], other).wait_recv()

    def o_rows(run):
        at = r["inv"][run]
        return jnp.concatenate([r["ob"][0, at], r["ob"][1, at]], axis=1)

    def feed(j, carry):
        delta = 3 - j
        c = chip_at(delta)
        pair = pl.ds(2 * c, 2)
        o = jnp.concatenate([o_rows(2 * c), o_rows(2 * c + 1)], axis=0)
        x1 = r["xb"][pair].reshape(256, 768).astype(F32) + mm(o, r["wp"][...])
        r["x1"][pair] = x1.reshape(2, 128, 768)
        hat, _ = norm_parts(x1)
        n2 = (hat * g2 + b2).astype(BF16)
        r["n2"][pair] = n2.reshape(2, 128, 768)
        act, slope = gelu_pair(mm(n2, r["w1"][...]))
        r["act"][pair] = act.astype(BF16).reshape(2, 128, 384)
        du = (mm_nt(r["dyb"][pair].reshape(256, 768), r["w2"][...]) * slope).astype(BF16)
        r["du"][pair] = du.reshape(2, 128, 384)
        r["part"][...] = mm_nt(du, r["w1"][...]).reshape(2, 128, 768)
        dn.put(j, r["part"][e], r["part"][1 - e])

        @pl.when(j > 0)
        def _():
            dn.tx[j - 1] = dn.sum_core(j - 1).astype(BF16)
            dn.send(j - 1).start()

        return carry

    lax.fori_loop(0, 4, feed, 0)

    grad = mm_tn(r["act"][...].reshape(1024, 384), r["dyb"][...].reshape(1024, 768)).astype(BF16)
    for k in range(4):
        ca.own[k, 0] = grad[96 * k : 96 * k + 96, 0:384]
        ca.own[k, 1] = grad[96 * k : 96 * k + 96, 384:768]
        ca.prime(k)

    grad = mm_tn(r["n2"][...].reshape(1024, 768), r["du"][...].reshape(1024, 384)).astype(BF16)
    for i in range(8):
        r["t1"][i % 2, i // 2] = grad[96 * i : 96 * i + 96]
    t1_core = remote(r["t1"].at[1 - e], r["t1x"], r["t1_cs"], r["t1_cr"], other)
    t1_core.start()

    def t1_send(delta, half):
        src = r["t1"].at[e, chip_at(delta)] if half == 0 else r["t1x"].at[chip_at(delta)]
        hidden_core = e if half == 0 else 1 - e
        at = 2 * delta + half
        return remote(src, ca.own.at[4 + delta, hidden_core], r["t1_s"].at[at], r["t1_r"].at[at], dev(delta))

    def second(j, carry):
        delta = 3 - j
        pair = pl.ds(2 * chip_at(delta), 2)
        r["part"][...] = mm(r["act"][pair].reshape(256, 384), r["w2"][...]).reshape(2, 128, 768)
        ys.put(j, r["part"][e], r["part"][1 - e])
        return carry

    lax.fori_loop(0, 4, second, 0)
    ca.tick(1)

    runs = [r["perm"][4 * e + s] for s in range(4)]
    n1s = jnp.concatenate([r["n1"][run] for run in runs], axis=0)
    r["n1s"][...] = n1s
    r["qo"][...] = mm(n1s, r["wo"][...]).astype(BF16).reshape(2, 256, 576)

    dn2 = dn.result()
    x1 = r["x1"][b]
    hat, inv_std = norm_parts(x1)
    r["lnp"][2:3] = jnp.sum(dn2 * hat, axis=0, keepdims=True)
    r["lnp"][3:4] = jnp.sum(dn2, axis=0, keepdims=True)
    dx1 = r["dyb"][b].astype(F32) + norm_back(dn2, hat, inv_std, g2)
    r["dx1"][...] = dx1
    low = dx1.astype(BF16)
    r["dxb"][b] = low
    do = mm_nt(low, r["wp"][...]).astype(BF16)
    for i in range(4):
        r["dos"][i] = do[:, 192 * i : 192 * i + 192]
    for delta in (3, 2, 1):
        gdo.to_chip(delta, r["dos"].at[chip_at(delta)]).start()
    gdo.to_core(r["dos"].at[chip]).start()
    r["dob"][b] = r["dos"][chip]
    t1_core.wait_recv()
    for delta in (3, 2, 1):
        for half in (0, 1):
            t1_send(delta, half).start()
    ca.own[4, e] = r["t1"][e, chip]
    ca.own[4, 1 - e] = r["t1x"][chip]
    ca.prime(4)
    ca.tick(2)
    gdx.send(r["dxb"].at[b])
    for delta in (1, 2, 3):
        gdo.wait_chip(delta)
    for delta in range(4):
        gdo.wait_core(delta)

    def attend_back(at, carry):
        run0, run1 = r["perm"][4 * e + 2 * at], r["perm"][4 * e + 2 * at + 1]
        do_rows = jnp.concatenate([r["dob"][run0], r["dob"][run1]], axis=0)
        rows = r["qo"][at]
        for h in range(3):
            q = rows[:, 64 * h : 64 * h + 64]
            k = rows[:, 192 + 64 * h : 192 + 64 * h + 64]
            v = rows[:, 384 + 64 * h : 384 + 64 * h + 64]
            g = do_rows[:, 64 * h : 64 * h + 64]
            s = mm_nt(q, k) * scale
            p = jnp.exp(s - jnp.max(s, axis=-1, keepdims=True))
            p = p / jnp.sum(p, axis=-1, keepdims=True)
            dp = mm_nt(g, v)
            ds = (p * (dp - jnp.sum(p * dp, axis=-1, keepdims=True))).astype(BF16)
            r["dq"][at, :, 64 * h : 64 * h + 64] = (mm(ds, k) * scale).astype(BF16)
            r["dq"][at, :, 192 + 64 * h : 192 + 64 * h + 64] = (mm_tn(ds, q) * scale).astype(BF16)
            r["dq"][at, :, 384 + 64 * h : 384 + 64 * h + 64] = mm_tn(p.astype(BF16), g).astype(BF16)
        return carry

    lax.fori_loop(0, 2, attend_back, 0)
    ca.tick(3)

    dqkv = r["dq"][...].reshape(512, 576)
    grad = mm_tn(r["n1s"][...], dqkv)
    for i in range(8):
        r["tq"][i % 2, i // 2] = grad[96 * i : 96 * i + 96].astype(BF16)
    tq_core = remote(r["tq"].at[1 - e], r["tqx"], r["tq_cs"], r["tq_cr"], other)
    tq_core.start()

    dn1_low = mm_nt(dqkv, r["wo"][...]).astype(BF16)
    r["d1"][pl.ds(4 * e, 4)] = dn1_low.reshape(4, 128, 768)
    d1_core = remote(r["d1"].at[pl.ds(4 * e, 4)], r["d1"].at[pl.ds(4 * e, 4)], r["d1_cs"], r["d1_cr"], other)
    d1_core.start()

    def tq_send(delta):
        return remote(r["tqs"].at[delta], cb.own.at[delta], r["tq_s"].at[delta], r["tq_r"].at[delta], dev(delta))

    def d1_send(delta):
        return remote(r["d1s"].at[delta], r["d1r"].at[delta], r["d1_s"].at[delta], r["d1_r"].at[delta], dev(delta))

    tq_core.wait_recv()
    for delta in (3, 2, 1, 0):
        c = chip_at(delta)
        total = (r["tq"][e, c].astype(F32) + r["tqx"][c].astype(F32)).astype(BF16)
        if delta == 0:
            cb.own[0] = total
        else:
            r["tqs"][delta] = total
            tq_send(delta).start()
    remote(r["d1"].at[pl.ds(4 - 4 * e, 4)], r["d1"].at[pl.ds(4 - 4 * e, 4)], r["d1_cs"], r["d1_cr"], other).wait_recv()
    for delta in (3, 2, 1):
        r["d1s"][delta] = r["d1"][r["inv"][2 * chip_at(delta) + e]]
        d1_send(delta).start()

    for delta in (1, 2, 3):
        for half in (0, 1):
            t1_send(delta, half).wait_recv()
        ca.prime(4 + delta)
    ca.tick(4)
    cb.prime(0)
    for delta in (1, 2, 3):
        gdx.wait_chip(delta)
    ca.tick(5)
    for delta in range(4):
        gdx.wait_core(delta)
    parts = []
    for i in range(8):
        o = r["ob"][chip // 2, r["inv"][i]]
        first = jnp.where(e == 0, o[:, 0:96], o[:, 96:192])
        second_half = jnp.where(e == 0, o[:, 192:288], o[:, 288:384])
        parts.append(jnp.where(odd, second_half, first))
    grad = mm_tn(jnp.concatenate(parts, axis=0), r["dxb"][...].reshape(1024, 768)).astype(BF16)
    ca.own[8, 0] = grad[:, 0:384]
    ca.own[8, 1] = grad[:, 384:768]
    ca.prime(8)
    ca.tick(6)
    for j in range(3):
        ys.tx[j] = ys.sum_core(j).astype(BF16)
        ys.send(j).start()
    for delta in (1, 2, 3):
        tq_send(delta).wait_recv()
        cb.prime(delta)
    ca.tick(7)
    dn1 = r["d1"][r["inv"][b]].astype(F32)
    for delta in (1, 2, 3):
        d1_send(delta).wait_recv()
        dn1 += r["d1r"][delta].astype(F32)
    hat, inv_std = norm_parts(r["xb"][b].astype(F32))
    r["lnp"][0:1] = jnp.sum(dn1 * hat, axis=0, keepdims=True)
    r["lnp"][1:2] = jnp.sum(dn1, axis=0, keepdims=True)
    r["lnp"][4:8] = jnp.zeros((4, 768), F32)
    r["o_gin"][...] = (r["dx1"][...] + norm_back(dn1, hat, inv_std, g1)).astype(BF16)
    ln_core = remote(r["lnp"], r["lnx"].at[0], r["ln_s"].at[0], r["ln_r"].at[0], other)
    ln_core.start()
    ca.tick(8)
    cb.tick(1)
    ln_core.wait_recv()
    r["lns"][...] = r["lnp"][...] + r["lnx"][0]

    def ln_send(delta):
        return remote(r["lns"], r["lnx"].at[delta], r["ln_s"].at[delta], r["ln_r"].at[delta], dev(delta))

    for delta in (3, 2, 1):
        ln_send(delta).start()
    ca.tick(9)
    cb.tick(2)
    total = r["lns"][...]
    for delta in (1, 2, 3):
        ln_send(delta).wait_recv()
        total += r["lnx"][delta]
    cc.own[0] = total
    cc.prime(0)
    ca.tick(10)
    cb.tick(3)
    cc.tick(1)
    ca.tick(11)
    cb.tick(4)
    cc.tick(2)
    r["o_y"][...] = (r["x1"][b] + ys.result()).astype(BF16)
    cb.tick(5)
    cc.tick(3)
    cb.tick(6)

    gx.finish(r["x"])
    gdy.finish(r["dy"])
    gdx.finish(r["dxb"].at[b])
    gdo.finish(r["dos"].at[chip])
    for at in range(4):
        o_core(at).wait_send()
    dn.finish()
    ys.finish()
    t1_core.wait_send()
    tq_core.wait_send()
    d1_core.wait_send()
    for delta in (1, 2, 3):
        t1_send(delta, 0).wait_send()
        t1_send(delta, 1).wait_send()
        tq_send(delta).wait_send()
        d1_send(delta).wait_send()
        ln_send(delta).wait_send()
    ln_core.wait_send()
    ca.finish()
    cb.finish()
    cc.finish()


def fast_shards(
    Z, inputs, crops, ln1_gain, ln1_bias, w_qkv, w_proj, ln2_gain, ln2_bias, w_fc1, w_fc2, cotangent
):
    V, D = pltpu.VMEM, pltpu.SemaphoreType.DMA
    anyspace = pl.BlockSpec(memory_space=pl.ANY)
    vmem = pl.BlockSpec(memory_space=pltpu.VMEM)
    smem = pl.BlockSpec(memory_space=pltpu.SMEM)
    arguments = dict(
        x=(inputs[0], anyspace),
        crops=(crops, smem),
        ln1_gain=(ln1_gain[None], vmem),
        ln1_bias=(ln1_bias[None], vmem),
        w_qkv=(w_qkv, anyspace),
        w_proj=(w_proj, anyspace),
        ln2_gain=(ln2_gain[None], vmem),
        ln2_bias=(ln2_bias[None], vmem),
        w_fc1=(w_fc1, anyspace),
        w_fc2=(w_fc2, anyspace),
        dy=(cotangent[0], anyspace),
    )
    results = dict(
        o_y=((128, 768), BF16),
        o_gin=((128, 768), BF16),
        o_qkv=((4, 96, 576), BF16),
        o_proj=((96, 768), BF16),
        o_fc1=((96, 3072), BF16),
        o_fc2=((384, 768), BF16),
        o_ln=((8, 768), F32),
    )
    scratch = dict(
        ld_sem=D((11,)),
        perm=pltpu.SMEM((8,), jnp.int32),
        inv=pltpu.SMEM((8,), jnp.int32),
        xb=V((8, 128, 768), BF16), gx_s=D((8,)), gx_r=D((8,)),
        dyb=V((8, 128, 768), BF16), gdy_s=D((8,)), gdy_r=D((8,)),
        dxb=V((8, 128, 768), BF16), gdx_s=D((8,)), gdx_r=D((8,)),
        dob=V((8, 128, 192), BF16), dos=V((4, 128, 192), BF16), gdo_s=D((8,)), gdo_r=D((8,)),
        wf=V((768, 1152), BF16), w4=V((3, 768, 256), BF16), wo=V((768, 576), BF16),
        wp=V((768, 768), BF16), w1=V((768, 384), BF16), w2=V((384, 768), BF16),
        n1=V((8, 128, 768), BF16), n1s=V((512, 768), BF16), qkv=V((8, 128, 1152), BF16),
        ob=V((2, 8, 128, 384), BF16), o_s=D((4,)), o_r=D((4,)),
        x1=V((8, 128, 768), F32), n2=V((8, 128, 768), BF16),
        act=V((8, 128, 384), BF16), du=V((8, 128, 384), BF16), part=V((2, 128, 768), F32),
        dx1=V((128, 768), F32),
        t1=V((2, 4, 96, 384), BF16), t1x=V((4, 96, 384), BF16),
        t1_cs=D, t1_cr=D, t1_s=D((8,)), t1_r=D((8,)),
        qo=V((2, 256, 576), BF16), dq=V((2, 256, 576), BF16),
        tq=V((2, 4, 96, 576), BF16), tqx=V((4, 96, 576), BF16), tqs=V((4, 96, 576), BF16),
        tq_cs=D, tq_cr=D, tq_s=D((4,)), tq_r=D((4,)),
        d1=V((8, 128, 768), BF16), d1s=V((4, 128, 768), BF16), d1r=V((4, 128, 768), BF16),
        d1_cs=D, d1_cr=D, d1_s=D((4,)), d1_r=D((4,)),
        lnp=V((8, 768), F32), lns=V((8, 768), F32), lnx=V((4, 8, 768), F32), ln_s=D((4,)), ln_r=D((4,)),
    )
    for name in ("dn", "ys"):
        scratch.update(
            {
                name + "_ctx": V((4, 128, 768), BF16), name + "_crx": V((4, 128, 768), BF16),
                name + "_keep": V((4, 128, 768), F32), name + "_tx": V((3, 128, 768), BF16),
                name + "_rx": V((3, 128, 768), BF16), name + "_cs": D((4,)), name + "_cr": D((4,)),
                name + "_ss": D((3,)), name + "_sr": D((3,)),
            }
        )
    for name, K, shape, dtype in (
        ("ca", 9, (2, 96, 384), BF16), ("cb", 4, (96, 576), BF16), ("cc", 1, (8, 768), F32)
    ):
        for part in ("own", "rl", "rr", "tu", "td"):
            scratch[name + "_" + part] = V((K, *shape), dtype)
        for part in ("su", "sd", "ru", "rd"):
            scratch[name + "_" + part] = D((K,))
    names = (*arguments, *results, *scratch)
    y, gin, gqkv, gproj, gfc1, gfc2, gln = pl.pallas_call(
        functools.partial(layer_kernel, Z, names),
        out_shape=[jax.ShapeDtypeStruct(*shape) for shape in results.values()],
        in_specs=[spec for _, spec in arguments.values()],
        out_specs=[vmem] * len(results),
        scratch_shapes=list(scratch.values()),
        compiler_params=pltpu.CompilerParams(
            collective_id=0, has_side_effects=True, vmem_limit_bytes=60 * 2**20
        ),
    )(*[array for array, _ in arguments.values()])
    gqkv = gqkv.reshape(4, 96, 3, 192).transpose(1, 2, 0, 3).reshape(96, 2304)
    mine = lax.dynamic_slice_in_dim(gln, 96 * lax.axis_index("blk"), 96, 1)
    return (
        y[None], gin[None], gqkv.astype(F32), gproj.astype(F32), gfc1.astype(F32), gfc2.astype(F32),
        mine[0], mine[1], mine[2], mine[3],
    )


def solution(mesh):
    placed = (
        P("dp", "blk", None),
        P("dp", None),
        P(),
        P(),
        P(),
        P(),
        P(),
        P(),
        P(),
        P(),
        P("dp", "blk", None),
    )
    def whole(*arrays):
        one_run = arrays[0].shape[1] == 8 * RUN_ROWS and mesh.shape["blk"] == 8
        body = functools.partial(fast_shards, mesh.shape["dp"]) if one_run else shards
        return placed_call(body)(*arrays)

    placed_call = lambda body: jax.shard_map(
        body,
        mesh=mesh,
        in_specs=placed,
        out_specs=(
            P("dp", "blk", None),
            P("dp", "blk", None),
            P("blk", None),
            P("blk", None),
            P("blk", None),
            P("blk", None),
            P("blk"),
            P("blk"),
            P("blk"),
            P("blk"),
        ),
        check_vma=False,
    )
    return whole
```

```python
import functools
import math

import jax
import jax.numpy as jnp
from jax import lax
from jax.experimental import pallas as pl
from jax.experimental.pallas import tpu as pltpu
from jax.sharding import PartitionSpec as P

HEADS = 12


EPSILON = 1e-05
MASKED = -1e30


def layer_norm(values_in, gain_in, shift_in):
    row_mean = jnp.mean(values_in, axis=-1, keepdims=True)
    centred = values_in - row_mean
    row_var = jnp.mean(centred * centred, axis=-1, keepdims=True)
    return centred * lax.rsqrt(row_var + EPSILON) * gain_in + shift_in


def contract_rows(left_side, right_side):
    return lax.dot_general(
        left_side, right_side, (((0,), (0,)), ((), ())), preferred_element_type=jnp.float32
    )


def against_weight(grad_rows, weight_mat):
    return lax.dot_general(
        grad_rows, weight_mat, (((1,), (1,)), ((), ())), preferred_element_type=jnp.float32
    )


def head_view(matrix, head_count):
    return matrix.reshape(matrix.shape[0], head_count, matrix.shape[1] // head_count)


def scores_of(query_heads, key_heads, score_scale):
    return (
        jnp.einsum("qhd,khd->hqk", query_heads, key_heads, preferred_element_type=jnp.float32)
        * score_scale
    )


def weights_of(scores, visible, logsum):
    return jnp.where(visible[None], jnp.exp(scores - logsum[:, :, None]), 0.0)


def shards(
    inputs, crops, ln1_gain, ln1_bias, w_qkv, w_proj, ln2_gain, ln2_bias, w_fc1, w_fc2, cotangent
):
    row_count = inputs.shape[1]
    model_width = inputs.shape[2]
    head_count = HEADS
    score_scale = 1.0 / math.sqrt(model_width // head_count)
    seq_crops = crops[0]
    seq_len = seq_crops.shape[0]
    key_block = min(1024, seq_len)
    block_count = seq_len // key_block
    block_ids = jnp.arange(block_count)
    own_crops = lax.dynamic_slice_in_dim(seq_crops, lax.axis_index("blk") * row_count, row_count, 0)
    residual = inputs[0].astype(jnp.float32)
    normed_one_low = layer_norm(residual, ln1_gain, ln1_bias).astype(jnp.bfloat16)
    qkv_low = jnp.dot(normed_one_low, w_qkv, preferred_element_type=jnp.float32).astype(
        jnp.bfloat16
    )
    query_own = qkv_low[:, :model_width]
    key_own = qkv_low[:, model_width : 2 * model_width]
    value_own = qkv_low[:, 2 * model_width :]
    keys_all, values_all = (
        lax.all_gather(key_own, "blk", axis=0, tiled=True),
        lax.all_gather(value_own, "blk", axis=0, tiled=True),
    )
    query_heads = head_view(query_own, head_count)

    def block_inputs(block_index):
        key_heads = head_view(
            lax.dynamic_slice_in_dim(keys_all, block_index * key_block, key_block, 0), head_count
        )
        value_heads = head_view(
            lax.dynamic_slice_in_dim(values_all, block_index * key_block, key_block, 0), head_count
        )
        crop_block = lax.dynamic_slice_in_dim(seq_crops, block_index * key_block, key_block, 0)
        visible = own_crops[:, None] == crop_block[None, :]
        return (key_heads, value_heads, visible)

    def stats_step(carried, block_index):
        old_max, summed = carried
        key_heads, value_heads, visible = block_inputs(block_index)
        scores = jnp.where(visible[None], scores_of(query_heads, key_heads, score_scale), MASKED)
        new_max = jnp.maximum(old_max, jnp.max(scores, axis=-1))
        exp_terms = jnp.where(visible[None], jnp.exp(scores - new_max[:, :, None]), 0.0)
        return ((new_max, summed * jnp.exp(old_max - new_max) + jnp.sum(exp_terms, axis=-1)), None)

    start_max = jnp.full((head_count, row_count), MASKED, jnp.float32)
    start_sum = jnp.zeros((head_count, row_count), jnp.float32)
    (row_max, summed), _ = lax.scan(stats_step, (start_max, start_sum), block_ids)
    logsum = row_max + jnp.log(summed)

    def output_step(running, block_index):
        key_heads, value_heads, visible = block_inputs(block_index)
        attn_probs = weights_of(
            scores_of(query_heads, key_heads, score_scale), visible, logsum
        ).astype(jnp.bfloat16)
        return (
            running
            + jnp.einsum(
                "hqk,khd->qhd", attn_probs, value_heads, preferred_element_type=jnp.float32
            ),
            None,
        )

    attended, _ = lax.scan(output_step, jnp.zeros(query_heads.shape, jnp.float32), block_ids)
    attended_low = attended.reshape(row_count, model_width).astype(jnp.bfloat16)
    mixed_rows = residual + jnp.dot(attended_low, w_proj, preferred_element_type=jnp.float32)
    normed_two_low = layer_norm(mixed_rows, ln2_gain, ln2_bias).astype(jnp.bfloat16)
    hidden_pre = jnp.dot(normed_two_low, w_fc1, preferred_element_type=jnp.float32)
    active, gelu_back = jax.vjp(jax.nn.gelu, hidden_pre)
    active_low = active.astype(jnp.bfloat16)
    result = mixed_rows + jnp.dot(active_low, w_fc2, preferred_element_type=jnp.float32)
    output = result.astype(jnp.bfloat16)[None]
    grad_out_low = cotangent[0]
    grad_fc2 = contract_rows(active_low, grad_out_low)
    grad_active = against_weight(grad_out_low, w_fc2)
    grad_hidden_low = gelu_back(grad_active)[0].astype(jnp.bfloat16)
    grad_fc1 = contract_rows(normed_two_low, grad_hidden_low)
    grad_normed_two = against_weight(grad_hidden_low, w_fc1)
    _, norm_two_back = jax.vjp(layer_norm, mixed_rows, ln2_gain, ln2_bias)
    grad_mixed_part, grad_gain_two, grad_bias_two = norm_two_back(grad_normed_two)
    grad_mixed = grad_out_low.astype(jnp.float32) + grad_mixed_part
    grad_mixed_low = grad_mixed.astype(jnp.bfloat16)
    grad_proj = contract_rows(attended_low, grad_mixed_low)
    grad_attended_low = against_weight(grad_mixed_low, w_proj).astype(jnp.bfloat16)
    grad_heads = head_view(grad_attended_low, head_count)

    def delta_step(running, block_index):
        key_heads, value_heads, visible = block_inputs(block_index)
        attn_probs = weights_of(scores_of(query_heads, key_heads, score_scale), visible, logsum)
        grad_probs = jnp.einsum(
            "qhd,khd->hqk", grad_heads, value_heads, preferred_element_type=jnp.float32
        )
        return (running + jnp.sum(attn_probs * grad_probs, axis=-1), None)

    row_delta, _ = lax.scan(delta_step, jnp.zeros((head_count, row_count), jnp.float32), block_ids)

    def score_grads(
        query_part, grad_part, logsum_part, delta_part, key_heads, value_heads, visible
    ):
        attn_probs = weights_of(scores_of(query_part, key_heads, score_scale), visible, logsum_part)
        grad_probs = jnp.einsum(
            "qhd,khd->hqk", grad_part, value_heads, preferred_element_type=jnp.float32
        )
        grad_scores = (attn_probs * (grad_probs - delta_part[:, :, None])).astype(jnp.bfloat16)
        return (attn_probs, grad_scores)

    def pair_step(running, block_index):
        key_heads, value_heads, visible = block_inputs(block_index)
        attn_probs, grad_scores = score_grads(
            query_heads, grad_heads, logsum, row_delta, key_heads, value_heads, visible
        )
        key_term = (
            jnp.einsum("hqk,qhd->khd", grad_scores, query_heads, preferred_element_type=jnp.float32)
            * score_scale
        )
        value_term = jnp.einsum(
            "hqk,qhd->khd",
            attn_probs.astype(jnp.bfloat16),
            grad_heads,
            preferred_element_type=jnp.float32,
        )
        joined = jnp.concatenate(
            [key_term.reshape(key_block, model_width), value_term.reshape(key_block, model_width)],
            axis=1,
        )
        step_query = jnp.einsum(
            "hqk,khd->qhd", grad_scores, key_heads, preferred_element_type=jnp.float32
        )
        return (running + step_query, joined)

    grad_query, key_terms = lax.scan(
        pair_step, jnp.zeros(query_heads.shape, jnp.float32), block_ids
    )
    key_sums = lax.psum_scatter(
        key_terms.reshape(seq_len, 2 * model_width).astype(jnp.bfloat16),
        "blk",
        scatter_dimension=0,
        tiled=True,
    ).astype(jnp.float32)
    grad_key = key_sums[:, :model_width]
    grad_value = key_sums[:, model_width:]
    grad_query = grad_query.reshape(row_count, model_width) * score_scale
    grad_qkv_low = jnp.concatenate([grad_query, grad_key, grad_value], axis=1).astype(jnp.bfloat16)
    grad_wqkv = contract_rows(normed_one_low, grad_qkv_low)
    grad_normed_one = against_weight(grad_qkv_low, w_qkv)
    _, norm_one_back = jax.vjp(layer_norm, residual, ln1_gain, ln1_bias)
    grad_resid, grad_gain_one, grad_bias_one = norm_one_back(grad_normed_one)
    grad_input = (grad_mixed + grad_resid).astype(jnp.bfloat16)[None]
    (
        fc1_share,
        fc2_share,
        qkv_share,
        proj_share,
        gain_one_share,
        bias_one_share,
        gain_two_share,
        bias_two_share,
    ) = (
        lax.psum_scatter(
            grad_fc1.astype(jnp.bfloat16), "blk", scatter_dimension=0, tiled=True
        ).astype(jnp.float32),
        lax.psum_scatter(
            grad_fc2.astype(jnp.bfloat16), "blk", scatter_dimension=0, tiled=True
        ).astype(jnp.float32),
        lax.psum_scatter(
            grad_wqkv.astype(jnp.bfloat16), "blk", scatter_dimension=0, tiled=True
        ).astype(jnp.float32),
        lax.psum_scatter(
            grad_proj.astype(jnp.bfloat16), "blk", scatter_dimension=0, tiled=True
        ).astype(jnp.float32),
        lax.psum_scatter(
            grad_gain_one.astype(jnp.bfloat16), "blk", scatter_dimension=0, tiled=True
        ).astype(jnp.float32),
        lax.psum_scatter(
            grad_bias_one.astype(jnp.bfloat16), "blk", scatter_dimension=0, tiled=True
        ).astype(jnp.float32),
        lax.psum_scatter(
            grad_gain_two.astype(jnp.bfloat16), "blk", scatter_dimension=0, tiled=True
        ).astype(jnp.float32),
        lax.psum_scatter(
            grad_bias_two.astype(jnp.bfloat16), "blk", scatter_dimension=0, tiled=True
        ).astype(jnp.float32),
    )
    totals = (
        lax.psum(qkv_share.astype(jnp.bfloat16), "dp").astype(jnp.float32),
        lax.psum(proj_share.astype(jnp.bfloat16), "dp").astype(jnp.float32),
        lax.psum(fc1_share.astype(jnp.bfloat16), "dp").astype(jnp.float32),
        lax.psum(fc2_share.astype(jnp.bfloat16), "dp").astype(jnp.float32),
        lax.psum(gain_one_share.astype(jnp.bfloat16), "dp").astype(jnp.float32),
        lax.psum(bias_one_share.astype(jnp.bfloat16), "dp").astype(jnp.float32),
        lax.psum(gain_two_share.astype(jnp.bfloat16), "dp").astype(jnp.float32),
        lax.psum(bias_two_share.astype(jnp.bfloat16), "dp").astype(jnp.float32),
    )
    return (
        output,
        grad_input,
        totals[0],
        totals[1],
        totals[2],
        totals[3],
        totals[4],
        totals[5],
        totals[6],
        totals[7],
    )


MESH = pl.DeviceIdType.MESH
F32 = jnp.float32
BF16 = jnp.bfloat16
RUN_ROWS = 128
HEAD = 64


def mm(left, right):
    return lax.dot_general(left, right, (((1,), (0,)), ((), ())), preferred_element_type=F32)


def mm_nt(left, right):
    return lax.dot_general(left, right, (((1,), (1,)), ((), ())), preferred_element_type=F32)


def mm_tn(left, right):
    return lax.dot_general(left, right, (((0,), (0,)), ((), ())), preferred_element_type=F32)


def norm_parts(rows):
    centred = rows - jnp.mean(rows, axis=-1, keepdims=True)
    inv_std = lax.rsqrt(jnp.mean(centred * centred, axis=-1, keepdims=True) + EPSILON)
    return centred * inv_std, inv_std


def norm_back(grad_rows, hat, inv_std, gain):
    grad_hat = grad_rows * gain
    return inv_std * (
        grad_hat
        - jnp.mean(grad_hat, axis=-1, keepdims=True)
        - hat * jnp.mean(grad_hat * hat, axis=-1, keepdims=True)
    )


def gelu_pair(u):
    inner = 0.7978845608028654 * (u + 0.044715 * u * u * u)
    t = jnp.tanh(inner)
    half = 0.5 * (1.0 + t)
    slope = half + 0.5 * u * (1.0 - t * t) * (0.7978845608028654 * (1.0 + 0.134145 * u * u))
    return u * half, slope


def layer_kernel(Z, names, *refs):
    r = dict(zip(names, refs, strict=True))
    z = lax.axis_index("dp")
    b = lax.axis_index("blk")
    e = lax.rem(b, 2)
    chip = b // 2
    cx = lax.rem(chip, 2)
    cy = chip // 2
    scale = HEAD**-0.5

    def chip_at(delta):
        dx, dy = delta % 2, delta // 2
        return 2 * (cy + dy - 2 * cy * dy) + (cx + dx - 2 * cx * dx)

    def dev(delta):
        return (z, 2 * chip_at(delta) + e)

    other = (z, b + 1 - 2 * e)

    def remote(src, dst, send_sem, recv_sem, device):
        sems = [s[0].at[s[1]] if isinstance(s, tuple) else s for s in (send_sem, recv_sem)]
        return pltpu.make_async_remote_copy(
            src_ref=src, dst_ref=dst, send_sem=sems[0], recv_sem=sems[1],
            device_id=device, device_id_type=MESH,
        )

    loads = {}

    def load(name, src, dst):
        loads[name] = pltpu.make_async_copy(src, dst, r["ld_sem"].at[len(loads)])
        loads[name].start()

    load("x", r["x"], r["xb"].at[b])
    load("w_qkv", r["w_qkv"], r["wq"])
    load("w_proj", r["w_proj"], r["wp"])
    load("dy", r["dy"], r["dyb"].at[b])
    load("w_fc1", r["w_fc1"], r["w1"])
    load("w_fc2", r["w_fc2"], r["w2"])

    bar = pltpu.get_barrier_semaphore()
    for target in (other, dev(1), dev(2), dev(3)):
        pl.semaphore_signal(bar, inc=1, device_id=target, device_id_type=MESH)

    @pl.when(z > 0)
    def _():
        pl.semaphore_signal(bar, inc=1, device_id=(z - 1, b), device_id_type=MESH)

    @pl.when(z < Z - 1)
    def _():
        pl.semaphore_signal(bar, inc=1, device_id=(z + 1, b), device_id_type=MESH)

    pl.semaphore_wait(bar, 4 + jnp.minimum(z, 1) + jnp.minimum(Z - 1 - z, 1))

    class Gather:
        def __init__(self, buf, ss, rs):
            self.buf, self.ss, self.rs = buf, ss, rs

        def slot(self, m):
            return 2 * chip_at(m // 2) + (e if m % 2 == 0 else 1 - e)

        def hop(self, delta, src=None):
            at = b if src is not None else self.slot(2 * delta)
            src = self.buf.at[at] if src is None else src
            return remote(src, self.buf.at[at], (self.ss, 2 * delta), (self.rs, 2 * delta), dev(delta))

        def half(self, part, delta, towards):
            at = (self.slot(2 * delta), pl.ds(64 * part, 64))
            return remote(self.buf.at[at], self.buf.at[at], (self.ss, 6 + 2 * part), (self.rs, 6 + 2 * part), dev(towards))

        def core(self, delta, src=None):
            at = b if src is not None else self.slot(2 * delta)
            src = self.buf.at[at] if src is None else src
            return remote(src, self.buf.at[at], (self.ss, 2 * delta + 1), (self.rs, 2 * delta + 1), other)

        def send(self, src):
            self.hop(1, src).start()
            self.hop(2, src).start()
            self.core(0, src).start()

        def pass_on(self):
            self.hop(1).wait_recv()
            self.half(0, 1, 2).start()
            self.hop(2).wait_recv()
            self.half(1, 2, 1).start()
            self.core(1).start()
            self.core(2).start()

        def pass_diagonal(self):
            self.half(0, 3, 2).wait_recv()
            self.half(1, 3, 1).wait_recv()
            self.core(3).start()

        def wait_core(self, delta):
            at = self.slot(2 * delta + 1)
            remote(self.buf.at[at], self.buf.at[at], (self.ss, 2 * delta + 1), (self.rs, 2 * delta + 1), other).wait_recv()

        def finish(self, src):
            self.hop(1, src).wait_send()
            self.hop(2, src).wait_send()
            self.half(0, 1, 2).wait_send()
            self.half(1, 2, 1).wait_send()
            self.core(0, src).wait_send()
            for delta in (1, 2, 3):
                self.core(delta).wait_send()

    gx = Gather(r["xb"], r["gx_s"], r["gx_r"])
    gdy = Gather(r["dyb"], r["gdy_s"], r["gdy_r"])

    class Chain:
        def __init__(self, name, K, dtype, sink):
            self.K, self.dtype, self.sink = K, dtype, sink
            for part in ("own", "rl", "rr", "tu", "td", "su", "sd", "ru", "rd"):
                setattr(self, part, r[name + "_" + part])

        def up(self, src, k):
            return remote(src, self.rl.at[k], (self.su, k), (self.ru, k), (z + 1, b))

        def down(self, src, k):
            return remote(src, self.rr.at[k], (self.sd, k), (self.rd, k), (z - 1, b))

        def prime(self, k):
            if Z == 1:
                return

            @pl.when(z == 0)
            def _():
                self.up(self.own.at[k], k).start()

            @pl.when(z == Z - 1)
            def _():
                self.down(self.own.at[k], k).start()

        def tick(self, i):
            ku = i - z

            @pl.when((z > 0) & (ku >= 0) & (ku < self.K))
            def _():
                self.up(self.own.at[ku], ku).wait_recv()

                @pl.when(z < Z - 1)
                def _():
                    self.tu[ku] = (self.own[ku].astype(F32) + self.rl[ku].astype(F32)).astype(self.dtype)
                    self.up(self.tu.at[ku], ku).start()

            kd = i - (Z - 1 - z)

            @pl.when((z < Z - 1) & (kd >= 0) & (kd < self.K))
            def _():
                self.down(self.own.at[kd], kd).wait_recv()

                @pl.when(z > 0)
                def _():
                    self.td[kd] = (self.own[kd].astype(F32) + self.rr[kd].astype(F32)).astype(self.dtype)
                    self.down(self.td.at[kd], kd).start()

            k = i - (Z - 1)
            if 0 <= k < self.K:

                @pl.when(z == 0)
                def _():
                    self.sink(k, self.own[k].astype(F32) + self.rr[k].astype(F32))

                @pl.when(z == Z - 1)
                def _():
                    self.sink(k, self.own[k].astype(F32) + self.rl[k].astype(F32))

                @pl.when((z > 0) & (z < Z - 1))
                def _():
                    self.sink(
                        k,
                        self.own[k].astype(F32) + self.rl[k].astype(F32) + self.rr[k].astype(F32),
                    )

        def finish(self):
            @pl.when(z < Z - 1)
            def _():
                for k in range(self.K):
                    self.up(self.own.at[k], k).wait_send()

            @pl.when(z > 0)
            def _():
                for k in range(self.K):
                    self.down(self.own.at[k], k).wait_send()

    def sink_a(k, total):
        low = total.astype(BF16)
        if k < 4:
            r["o_fc2"][96 * k : 96 * k + 96, 0:384] = low[0]
            r["o_fc2"][96 * k : 96 * k + 96, 384:768] = low[1]
        elif k < 8:
            src = chip_at(k - 4)
            r["o_fc1"][:, pl.ds(pl.multiple_of(768 * src, 128), 384)] = low[0]
            r["o_fc1"][:, pl.ds(pl.multiple_of(768 * src + 384, 128), 384)] = low[1]
        else:
            r["o_proj"][:, 0:384] = low[0]
            r["o_proj"][:, 384:768] = low[1]

    def sink_b(k, total):
        r["o_qkv"][chip_at(k)] = total.astype(BF16)

    def sink_c(k, total):
        for i in range(8):
            r["lnc"][i] = total[:, 96 * i : 96 * i + 96]
        r["o_ln"][...] = r["lnc"][b]

    ca = Chain("ca", 9, BF16, sink_a)
    cb = Chain("cb", 4, BF16, sink_b)
    cc = Chain("cc", 1, F32, sink_c)

    gx.send(r["x"])

    crop = [r["crops"][0, RUN_ROWS * i] for i in range(8)]
    places = []
    for i in range(8):
        place = 2 * crop[i]
        for h in range(i):
            place = place + jnp.where(crop[h] == crop[i], 1, 0)
        places.append(place)
        r["inv"][i] = place
    for s in range(8):
        run = jnp.int32(0)
        for i in range(8):
            run = run + jnp.where(places[i] == s, i, 0)
        r["perm"][s] = run

    g1, b1 = r["ln1_gain"][...].reshape(1, 768), r["ln1_bias"][...].reshape(1, 768)
    g2, b2 = r["ln2_gain"][...].reshape(1, 768), r["ln2_bias"][...].reshape(1, 768)

    loads["x"].wait()
    loads["w_qkv"].wait()
    for i in range(4):
        for t in range(3):
            first = 768 * t + 192 * i
            r["wo"][i, :, 128 * t : 128 * t + 128] = r["wq"][:, first : first + 128]
            r["wo"][i, :, 384 + 64 * t : 448 + 64 * t] = r["wq"][:, first + 128 : first + 192]

    def project(delta):
        gx.wait_core(delta)
        pair = pl.ds(2 * chip_at(delta), 2)
        hat, _ = norm_parts(r["xb"][pair].reshape(256, 768).astype(F32))
        normed = (hat * g1 + b1).astype(BF16)
        r["n1"][pair] = normed.reshape(2, 128, 768)
        for t in range(3):
            out = mm(normed, r["wq"][:, pl.ds(pl.multiple_of(768 * t + 384 * e, 128), 384)])
            out = out * scale if t == 0 else out
            r["qkv"][pair, :, 384 * t : 384 * t + 384] = out.astype(BF16).reshape(2, 128, 384)

    project(0)
    gx.pass_on()
    gdy.send(r["dy"])
    project(1)
    project(2)
    gx.pass_diagonal()
    project(3)

    low_lanes = lax.broadcasted_iota(jnp.int32, (1, 128), 1) < HEAD

    def stack(two):
        none = jnp.zeros_like(two)
        return jnp.concatenate([jnp.where(low_lanes, two, none), jnp.where(low_lanes, none, two)], axis=0)

    def o_core(at):
        place = (e, pl.ds(2 * at, 2))
        return remote(r["ob"].at[place], r["ob"].at[place], (r["o_s"], at), (r["o_r"], at), other)

    def attend(at, carry):
        run0, run1 = r["perm"][2 * at], r["perm"][2 * at + 1]
        outs = []
        for h in range(3):
            q, k, v = [
                jnp.concatenate(
                    [r["qkv"][run, :, 384 * t + 128 * h : 384 * t + 128 * h + 128] for run in (run0, run1)],
                    axis=0,
                )
                for t in range(3)
            ]
            s = mm_nt(stack(q), k)
            p = jnp.exp(s - jnp.max(s, axis=-1, keepdims=True))
            o = mm(p.astype(BF16), v) / jnp.sum(p, axis=-1, keepdims=True)
            outs.append(jnp.where(low_lanes, o[0:256], o[256:512]))
        low = jnp.concatenate(outs, axis=1).astype(BF16)
        r["ob"][e, pl.ds(2 * at, 2)] = low.reshape(2, 128, 384)
        o_core(at).start()
        return carry

    lax.fori_loop(0, 3, attend, 0)
    gdy.pass_on()
    attend(3, 0)
    for name in ("w_proj", "w_fc1", "w_fc2", "dy"):
        loads[name].wait()
    for at in range(4):
        place = (1 - e, pl.ds(2 * at, 2))
        remote(r["ob"].at[place], r["ob"].at[place], (r["o_s"], at), (r["o_r"], at), other).wait_recv()

    def o_rows(run):
        at = r["inv"][run]
        return jnp.concatenate([r["ob"][0, at], r["ob"][1, at]], axis=1)

    own_hidden = pl.ds(pl.multiple_of(384 * b, 128), 384)

    def feed(c, carry):
        pair = pl.ds(2 * c, 2)
        o = jnp.concatenate([o_rows(2 * c), o_rows(2 * c + 1)], axis=0)
        x1 = r["xb"][pair].reshape(256, 768).astype(F32) + mm(o, r["wp"][...])
        r["x1"][pair] = x1.reshape(2, 128, 768)
        hat, _ = norm_parts(x1)
        n2 = (hat * g2 + b2).astype(BF16)
        r["n2"][pair] = n2.reshape(2, 128, 768)
        act, slope = gelu_pair(mm(n2, r["w1"][:, own_hidden]))
        r["act"][pair] = act.astype(BF16).reshape(2, 128, 384)
        r["slope"][pair] = slope.reshape(2, 128, 384)
        return carry

    lax.fori_loop(0, 4, feed, 0)
    gdy.pass_diagonal()
    for delta in range(4):
        gdy.wait_core(delta)

    grad = mm_tn(r["act"][...].reshape(1024, 384), r["dyb"][...].reshape(1024, 768)).astype(BF16)
    for k in range(4):
        ca.own[k, 0] = grad[96 * k : 96 * k + 96, 0:384]
        ca.own[k, 1] = grad[96 * k : 96 * k + 96, 384:768]
        ca.prime(k)

    n2_own = r["n2"][b]
    dy_own = r["dyb"][b]
    r["y"][...] = r["x1"][b]
    r["dn2"][...] = jnp.zeros((128, 768), F32)

    def own_rows(i, carry):
        part = pl.ds(pl.multiple_of(768 * i, 128), 768)
        act, slope = gelu_pair(mm(r["n2"][b], r["w1"][:, part]))
        du = (mm_nt(r["dyb"][b], r["w2"][part]) * slope).astype(BF16)
        r["dn2"][...] += mm_nt(du, r["w1"][:, part])
        r["y"][...] += mm(act.astype(BF16), r["w2"][part])
        return carry

    lax.fori_loop(0, 4, own_rows, 0)
    r["o_y"][...] = r["y"][...].astype(BF16)

    dn2 = r["dn2"][...]
    hat, inv_std = norm_parts(r["x1"][b])
    r["lnp"][2:3] = jnp.sum(dn2 * hat, axis=0, keepdims=True)
    r["lnp"][3:4] = jnp.sum(dn2, axis=0, keepdims=True)
    dx1 = dy_own.astype(F32) + norm_back(dn2, hat, inv_std, g2)
    r["dx1"][...] = dx1
    low = dx1.astype(BF16)
    do = mm_nt(low, r["wp"][...]).astype(BF16)
    for i in range(4):
        r["dos"][i] = do[:, 192 * i : 192 * i + 192]

    def do_send(delta):
        return remote(r["dos"].at[chip_at(delta)], r["dob"].at[b], (r["do_s"], 2 * delta), (r["do_r"], 2 * delta), dev(delta))

    def do_slot(m):
        return 2 * chip_at(m // 2) + (e if m % 2 == 0 else 1 - e)

    def do_core(delta):
        src = r["dos"].at[chip] if delta == 0 else r["dob"].at[do_slot(2 * delta)]
        return remote(src, r["dob"].at[do_slot(2 * delta)], (r["do_s"], 2 * delta + 1), (r["do_r"], 2 * delta + 1), other)

    for delta in (3, 2, 1):
        do_send(delta).start()
    do_core(0).start()
    r["dob"][b] = r["dos"][chip]
    ca.tick(1)

    def back_hidden(c, carry):
        pair = pl.ds(2 * c, 2)
        da = mm_nt(r["dyb"][pair].reshape(256, 768), r["w2"][own_hidden])
        r["du"][pair] = (da * r["slope"][pair].reshape(256, 384)).astype(BF16).reshape(2, 128, 384)
        return carry

    lax.fori_loop(0, 4, back_hidden, 0)
    grad = mm_tn(r["n2"][...].reshape(1024, 768), r["du"][...].reshape(1024, 384)).astype(BF16)
    for i in range(8):
        r["t1"][i % 2, i // 2] = grad[96 * i : 96 * i + 96]
    t1_core = remote(r["t1"].at[1 - e], r["t1x"], r["t1_cs"], r["t1_cr"], other)
    t1_core.start()

    def t1_send(delta, half):
        src = r["t1"].at[e, chip_at(delta)] if half == 0 else r["t1x"].at[chip_at(delta)]
        hidden_core = e if half == 0 else 1 - e
        at = 2 * delta + half
        return remote(src, ca.own.at[4 + delta, hidden_core], (r["t1_s"], at), (r["t1_r"], at), dev(delta))

    grad = mm_tn(o_rows(b), low).astype(BF16)
    for i in range(8):
        r["tp"][i % 2, i // 2] = grad[96 * i : 96 * i + 96]
    tp_core = remote(r["tp"].at[1 - e], r["tpx"], r["tp_cs"], r["tp_cr"], other)
    tp_core.start()

    def tp_send(delta):
        return remote(r["tps"].at[delta], r["tpr"].at[delta], (r["tp_s"], delta), (r["tp_r"], delta), dev(delta))

    for s in range(4):
        r["n1s"][s] = r["n1"][r["perm"][4 * e + s]]
    r["qo"][...] = mm(r["n1s"][...].reshape(512, 768), r["wo"][chip]).astype(BF16).reshape(2, 256, 576)
    ca.tick(2)

    for delta in (1, 2, 3):
        do_send(delta).wait_recv()
        do_core(delta).start()
    t1_core.wait_recv()
    for delta in (1, 2, 3):
        for half in (0, 1):
            t1_send(delta, half).start()
    ca.own[4, e] = r["t1"][e, chip]
    ca.own[4, 1 - e] = r["t1x"][chip]
    ca.prime(4)
    for delta in range(4):
        at = do_slot(2 * delta + 1)
        remote(r["dob"].at[at], r["dob"].at[at], (r["do_s"], 2 * delta + 1), (r["do_r"], 2 * delta + 1), other).wait_recv()

    def attend_back(at, heads):
        runs = [r["perm"][4 * e + 2 * at + i] for i in range(2)]
        if heads == 2:
            g = jnp.concatenate([r["dob"][run, :, 0:128] for run in runs], axis=0)
            q, k, v = [r["qo"][at, :, 128 * t : 128 * t + 128] for t in range(3)]
            q, g = stack(q), stack(g)
        else:
            g = jnp.concatenate([r["dob"][run, :, 128:192] for run in runs], axis=0)
            q, k, v = [r["qo"][at, :, 384 + 64 * t : 448 + 64 * t] for t in range(3)]
        q = (q.astype(F32) * scale).astype(BF16)
        s = mm_nt(q, k)
        p = jnp.exp(s - jnp.max(s, axis=-1, keepdims=True))
        p = p / jnp.sum(p, axis=-1, keepdims=True)
        dp = mm_nt(g, v)
        ds = (p * (dp - jnp.sum(p * dp, axis=-1, keepdims=True))).astype(BF16)
        dq = mm(ds, k) * scale
        dk = mm_tn(ds, q)
        dv = mm_tn(p.astype(BF16), g)
        mine = pl.ds(2 * (2 * e + at), 2)
        if heads == 2:
            dq = jnp.where(low_lanes, dq[0:256], dq[256:512])
        first, wide = (0, 128) if heads == 2 else (384, 64)
        for t, part in enumerate((dq, dk, dv)):
            r["dq"][mine, :, first + wide * t : first + wide * t + wide] = part.astype(BF16).reshape(2, 128, wide)

    attend_back(0, 2)
    attend_back(0, 1)
    ca.tick(3)
    attend_back(1, 2)
    attend_back(1, 1)

    dq_core = remote(r["dq"].at[pl.ds(4 * e, 4)], r["dq"].at[pl.ds(4 * e, 4)], r["dq_cs"], r["dq_cr"], other)
    dq_core.start()
    grad = mm_tn(r["n1s"][...].reshape(512, 768), r["dq"][pl.ds(4 * e, 4)].reshape(512, 576))
    for i in range(8):
        r["tq"][i % 2, i // 2] = grad[96 * i : 96 * i + 96].astype(BF16)
    tq_core = remote(r["tq"].at[1 - e], r["tqx"], r["tq_cs"], r["tq_cr"], other)
    tq_core.start()

    def tq_send(delta):
        return remote(r["tqs"].at[delta], cb.own.at[delta], (r["tq_s"], delta), (r["tq_r"], delta), dev(delta))

    def dq_send(delta):
        return remote(r["dqs"].at[delta], r["dqr"].at[delta], (r["dq_s"], delta), (r["dq_r"], delta), dev(delta))

    ca.tick(4)
    tq_core.wait_recv()
    for delta in (3, 2, 1, 0):
        c = chip_at(delta)
        total = (r["tq"][e, c].astype(F32) + r["tqx"][c].astype(F32)).astype(BF16)
        if delta == 0:
            cb.own[0] = total
        else:
            r["tqs"][delta] = total
            tq_send(delta).start()
    at = pl.ds(4 - 4 * e, 4)
    remote(r["dq"].at[at], r["dq"].at[at], r["dq_cs"], r["dq_cr"], other).wait_recv()
    for delta in (3, 2, 1):
        r["dqs"][delta] = r["dq"][r["inv"][2 * chip_at(delta) + e]]
        dq_send(delta).start()
    tp_core.wait_recv()
    for delta in (3, 2, 1, 0):
        c = chip_at(delta)
        r["tps"][delta] = (r["tp"][e, c].astype(F32) + r["tpx"][c].astype(F32)).astype(BF16)
        if delta > 0:
            tp_send(delta).start()

    for delta in (1, 2, 3):
        for half in (0, 1):
            t1_send(delta, half).wait_recv()
        ca.prime(4 + delta)
    ca.tick(5)
    cb.prime(0)
    for delta in (1, 2, 3):
        tq_send(delta).wait_recv()
        cb.prime(delta)
    ca.tick(6)
    dn1 = mm_nt(r["dq"][r["inv"][b]], r["wo"][chip])
    for delta in (1, 2, 3):
        dq_send(delta).wait_recv()
        dn1 += mm_nt(r["dqr"][delta], r["wo"][chip_at(delta)])
    hat, inv_std = norm_parts(r["xb"][b].astype(F32))
    r["lnp"][0:1] = jnp.sum(dn1 * hat, axis=0, keepdims=True)
    r["lnp"][1:2] = jnp.sum(dn1, axis=0, keepdims=True)
    r["lnp"][4:8] = jnp.zeros((4, 768), F32)
    r["o_gin"][...] = (r["dx1"][...] + norm_back(dn1, hat, inv_std, g1)).astype(BF16)
    ln_core = remote(r["lnp"], r["lnx"].at[0], (r["ln_s"], 0), (r["ln_r"], 0), other)
    ln_core.start()
    total = r["tps"][0].astype(F32)
    for delta in (1, 2, 3):
        tp_send(delta).wait_recv()
        total += r["tpr"][delta].astype(F32)
    ca.own[8, 0] = total[:, 0:384].astype(BF16)
    ca.own[8, 1] = total[:, 384:768].astype(BF16)
    ca.prime(8)
    ca.tick(7)
    ln_core.wait_recv()
    r["lns"][...] = r["lnp"][...] + r["lnx"][0]

    def ln_send(delta):
        return remote(r["lns"], r["lnx"].at[delta], (r["ln_s"], delta), (r["ln_r"], delta), dev(delta))

    for delta in (3, 2, 1):
        ln_send(delta).start()
    ca.tick(8)
    cb.tick(1)
    total = r["lns"][...]
    for delta in (1, 2, 3):
        ln_send(delta).wait_recv()
        total += r["lnx"][delta]
    cc.own[0] = total
    cc.prime(0)
    ca.tick(9)
    cb.tick(2)
    cc.tick(1)
    ca.tick(10)
    cb.tick(3)
    cc.tick(2)
    ca.tick(11)
    cb.tick(4)
    cc.tick(3)
    cb.tick(5)
    cb.tick(6)

    gx.finish(r["x"])
    gdy.finish(r["dy"])
    for at in range(4):
        o_core(at).wait_send()
    for copy in (t1_core, tp_core, tq_core, dq_core, ln_core, do_core(0)):
        copy.wait_send()
    for delta in (1, 2, 3):
        do_send(delta).wait_send()
        do_core(delta).wait_send()
        t1_send(delta, 0).wait_send()
        t1_send(delta, 1).wait_send()
        tp_send(delta).wait_send()
        tq_send(delta).wait_send()
        dq_send(delta).wait_send()
        ln_send(delta).wait_send()
    ca.finish()
    cb.finish()
    cc.finish()


def widen_kernel(y, gin, gqkv, gproj, gfc1, gfc2, gln, o_y, o_gin, o_qkv, o_proj, o_fc1, o_fc2, *o_ln):
    o_y[...] = y[...]
    o_gin[...] = gin[...]
    o_proj[...] = gproj[...].astype(F32)
    o_fc1[...] = gfc1[...].astype(F32)
    o_fc2[...] = gfc2[...].astype(F32)
    for t in range(3):
        parts = []
        for i in range(4):
            parts.append(gqkv[i, :, 128 * t : 128 * t + 128])
            parts.append(gqkv[i, :, 384 + 64 * t : 448 + 64 * t])
        o_qkv[:, 768 * t : 768 * t + 768] = jnp.concatenate(parts, axis=1).astype(F32)
    for i in range(4):
        o_ln[i][...] = gln[i, :]


def fast_shards(
    Z, inputs, crops, ln1_gain, ln1_bias, w_qkv, w_proj, ln2_gain, ln2_bias, w_fc1, w_fc2, cotangent
):
    V, D = pltpu.VMEM, pltpu.SemaphoreType.DMA
    anyspace = pl.BlockSpec(memory_space=pl.ANY)
    vmem = pl.BlockSpec(memory_space=pltpu.VMEM)
    smem = pl.BlockSpec(memory_space=pltpu.SMEM)
    arguments = dict(
        x=(inputs[0], anyspace),
        crops=(crops, smem),
        ln1_gain=(ln1_gain, vmem),
        ln1_bias=(ln1_bias, vmem),
        w_qkv=(w_qkv, anyspace),
        w_proj=(w_proj, anyspace),
        ln2_gain=(ln2_gain, vmem),
        ln2_bias=(ln2_bias, vmem),
        w_fc1=(w_fc1, anyspace),
        w_fc2=(w_fc2, anyspace),
        dy=(cotangent[0], anyspace),
    )
    results = dict(
        o_y=((128, 768), BF16),
        o_gin=((128, 768), BF16),
        o_qkv=((4, 96, 576), BF16),
        o_proj=((96, 768), BF16),
        o_fc1=((96, 3072), BF16),
        o_fc2=((384, 768), BF16),
        o_ln=((8, 96), F32),
    )
    scratch = dict(
        ld_sem=D((6,)),
        perm=pltpu.SMEM((8,), jnp.int32),
        inv=pltpu.SMEM((8,), jnp.int32),
        xb=V((8, 128, 768), BF16), gx_s=D((9,)), gx_r=D((9,)),
        dyb=V((8, 128, 768), BF16), gdy_s=D((9,)), gdy_r=D((9,)),
        dob=V((8, 128, 192), BF16), dos=V((4, 128, 192), BF16), do_s=D((8,)), do_r=D((8,)),
        wq=V((768, 2304), BF16), wo=V((4, 768, 576), BF16), wp=V((768, 768), BF16),
        w1=V((768, 3072), BF16), w2=V((3072, 768), BF16),
        n1=V((8, 128, 768), BF16), n1s=V((4, 128, 768), BF16), qkv=V((8, 128, 1152), BF16),
        ob=V((2, 8, 128, 384), BF16), o_s=D((4,)), o_r=D((4,)),
        x1=V((8, 128, 768), F32), n2=V((8, 128, 768), BF16),
        act=V((8, 128, 384), BF16), slope=V((8, 128, 384), F32), du=V((8, 128, 384), BF16),
        y=V((128, 768), F32), dn2=V((128, 768), F32), dx1=V((128, 768), F32),
        t1=V((2, 4, 96, 384), BF16), t1x=V((4, 96, 384), BF16),
        t1_cs=D, t1_cr=D, t1_s=D((8,)), t1_r=D((8,)),
        tp=V((2, 4, 96, 768), BF16), tpx=V((4, 96, 768), BF16), tps=V((4, 96, 768), BF16), tpr=V((4, 96, 768), BF16),
        tp_cs=D, tp_cr=D, tp_s=D((4,)), tp_r=D((4,)),
        qo=V((2, 256, 576), BF16), dq=V((8, 128, 576), BF16),
        tq=V((2, 4, 96, 576), BF16), tqx=V((4, 96, 576), BF16), tqs=V((4, 96, 576), BF16),
        tq_cs=D, tq_cr=D, tq_s=D((4,)), tq_r=D((4,)),
        dqs=V((4, 128, 576), BF16), dqr=V((4, 128, 576), BF16),
        dq_cs=D, dq_cr=D, dq_s=D((4,)), dq_r=D((4,)),
        lnp=V((8, 768), F32), lns=V((8, 768), F32), lnx=V((4, 8, 768), F32), lnc=V((8, 8, 96), F32),
        ln_s=D((4,)), ln_r=D((4,)),
    )
    for name, K, shape, dtype in (
        ("ca", 9, (2, 96, 384), BF16), ("cb", 4, (96, 576), BF16), ("cc", 1, (8, 768), F32)
    ):
        for part in ("own", "rl", "rr", "tu", "td"):
            scratch[name + "_" + part] = V((K, *shape), dtype)
        for part in ("su", "sd", "ru", "rd"):
            scratch[name + "_" + part] = D((K,))
    names = (*arguments, *results, *scratch)
    narrow = pl.pallas_call(
        functools.partial(layer_kernel, Z, names),
        out_shape=[jax.ShapeDtypeStruct(*shape) for shape in results.values()],
        in_specs=[spec for _, spec in arguments.values()],
        out_specs=[vmem] * len(results),
        scratch_shapes=list(scratch.values()),
        compiler_params=pltpu.CompilerParams(
            collective_id=0, has_side_effects=True, vmem_limit_bytes=60 * 2**20
        ),
    )(*[array for array, _ in arguments.values()])
    wide = [((128, 768), BF16), ((128, 768), BF16), ((96, 2304), F32), ((96, 768), F32), ((96, 3072), F32), ((384, 768), F32)]
    wide += [((96,), F32)] * 4
    y, gin, *grads = pl.pallas_call(
        widen_kernel,
        out_shape=[jax.ShapeDtypeStruct(*shape) for shape in wide],
        in_specs=[vmem] * len(narrow),
        out_specs=[vmem] * len(wide),
        compiler_params=pltpu.CompilerParams(vmem_limit_bytes=30 * 2**20),
    )(*narrow)
    return (y[None], gin[None], *grads)


def solution(mesh):
    placed = (
        P("dp", "blk", None),
        P("dp", None),
        P(),
        P(),
        P(),
        P(),
        P(),
        P(),
        P(),
        P(),
        P("dp", "blk", None),
    )
    def whole(*arrays):
        one_run = arrays[0].shape[1] == 8 * RUN_ROWS and mesh.shape["blk"] == 8
        body = functools.partial(fast_shards, mesh.shape["dp"]) if one_run else shards
        return placed_call(body)(*arrays)

    placed_call = lambda body: jax.shard_map(
        body,
        mesh=mesh,
        in_specs=placed,
        out_specs=(
            P("dp", "blk", None),
            P("dp", "blk", None),
            P("blk", None),
            P("blk", None),
            P("blk", None),
            P("blk", None),
            P("blk"),
            P("blk"),
            P("blk"),
            P("blk"),
        ),
        check_vma=False,
    )
    return whole
```

```python
import functools
import math

import jax
import jax.numpy as jnp
from jax import lax
from jax.experimental import pallas as pl
from jax.experimental.pallas import tpu as pltpu
from jax.sharding import PartitionSpec as P

HEADS = 12


EPSILON = 1e-05
MASKED = -1e30


def layer_norm(values_in, gain_in, shift_in):
    row_mean = jnp.mean(values_in, axis=-1, keepdims=True)
    centred = values_in - row_mean
    row_var = jnp.mean(centred * centred, axis=-1, keepdims=True)
    return centred * lax.rsqrt(row_var + EPSILON) * gain_in + shift_in


def contract_rows(left_side, right_side):
    return lax.dot_general(
        left_side, right_side, (((0,), (0,)), ((), ())), preferred_element_type=jnp.float32
    )


def against_weight(grad_rows, weight_mat):
    return lax.dot_general(
        grad_rows, weight_mat, (((1,), (1,)), ((), ())), preferred_element_type=jnp.float32
    )


def head_view(matrix, head_count):
    return matrix.reshape(matrix.shape[0], head_count, matrix.shape[1] // head_count)


def scores_of(query_heads, key_heads, score_scale):
    return (
        jnp.einsum("qhd,khd->hqk", query_heads, key_heads, preferred_element_type=jnp.float32)
        * score_scale
    )


def weights_of(scores, visible, logsum):
    return jnp.where(visible[None], jnp.exp(scores - logsum[:, :, None]), 0.0)


def shards(
    inputs, crops, ln1_gain, ln1_bias, w_qkv, w_proj, ln2_gain, ln2_bias, w_fc1, w_fc2, cotangent
):
    row_count = inputs.shape[1]
    model_width = inputs.shape[2]
    head_count = HEADS
    score_scale = 1.0 / math.sqrt(model_width // head_count)
    seq_crops = crops[0]
    seq_len = seq_crops.shape[0]
    key_block = min(1024, seq_len)
    block_count = seq_len // key_block
    block_ids = jnp.arange(block_count)
    own_crops = lax.dynamic_slice_in_dim(seq_crops, lax.axis_index("blk") * row_count, row_count, 0)
    residual = inputs[0].astype(jnp.float32)
    normed_one_low = layer_norm(residual, ln1_gain, ln1_bias).astype(jnp.bfloat16)
    qkv_low = jnp.dot(normed_one_low, w_qkv, preferred_element_type=jnp.float32).astype(
        jnp.bfloat16
    )
    query_own = qkv_low[:, :model_width]
    key_own = qkv_low[:, model_width : 2 * model_width]
    value_own = qkv_low[:, 2 * model_width :]
    keys_all, values_all = (
        lax.all_gather(key_own, "blk", axis=0, tiled=True),
        lax.all_gather(value_own, "blk", axis=0, tiled=True),
    )
    query_heads = head_view(query_own, head_count)

    def block_inputs(block_index):
        key_heads = head_view(
            lax.dynamic_slice_in_dim(keys_all, block_index * key_block, key_block, 0), head_count
        )
        value_heads = head_view(
            lax.dynamic_slice_in_dim(values_all, block_index * key_block, key_block, 0), head_count
        )
        crop_block = lax.dynamic_slice_in_dim(seq_crops, block_index * key_block, key_block, 0)
        visible = own_crops[:, None] == crop_block[None, :]
        return (key_heads, value_heads, visible)

    def stats_step(carried, block_index):
        old_max, summed = carried
        key_heads, value_heads, visible = block_inputs(block_index)
        scores = jnp.where(visible[None], scores_of(query_heads, key_heads, score_scale), MASKED)
        new_max = jnp.maximum(old_max, jnp.max(scores, axis=-1))
        exp_terms = jnp.where(visible[None], jnp.exp(scores - new_max[:, :, None]), 0.0)
        return ((new_max, summed * jnp.exp(old_max - new_max) + jnp.sum(exp_terms, axis=-1)), None)

    start_max = jnp.full((head_count, row_count), MASKED, jnp.float32)
    start_sum = jnp.zeros((head_count, row_count), jnp.float32)
    (row_max, summed), _ = lax.scan(stats_step, (start_max, start_sum), block_ids)
    logsum = row_max + jnp.log(summed)

    def output_step(running, block_index):
        key_heads, value_heads, visible = block_inputs(block_index)
        attn_probs = weights_of(
            scores_of(query_heads, key_heads, score_scale), visible, logsum
        ).astype(jnp.bfloat16)
        return (
            running
            + jnp.einsum(
                "hqk,khd->qhd", attn_probs, value_heads, preferred_element_type=jnp.float32
            ),
            None,
        )

    attended, _ = lax.scan(output_step, jnp.zeros(query_heads.shape, jnp.float32), block_ids)
    attended_low = attended.reshape(row_count, model_width).astype(jnp.bfloat16)
    mixed_rows = residual + jnp.dot(attended_low, w_proj, preferred_element_type=jnp.float32)
    normed_two_low = layer_norm(mixed_rows, ln2_gain, ln2_bias).astype(jnp.bfloat16)
    hidden_pre = jnp.dot(normed_two_low, w_fc1, preferred_element_type=jnp.float32)
    active, gelu_back = jax.vjp(jax.nn.gelu, hidden_pre)
    active_low = active.astype(jnp.bfloat16)
    result = mixed_rows + jnp.dot(active_low, w_fc2, preferred_element_type=jnp.float32)
    output = result.astype(jnp.bfloat16)[None]
    grad_out_low = cotangent[0]
    grad_fc2 = contract_rows(active_low, grad_out_low)
    grad_active = against_weight(grad_out_low, w_fc2)
    grad_hidden_low = gelu_back(grad_active)[0].astype(jnp.bfloat16)
    grad_fc1 = contract_rows(normed_two_low, grad_hidden_low)
    grad_normed_two = against_weight(grad_hidden_low, w_fc1)
    _, norm_two_back = jax.vjp(layer_norm, mixed_rows, ln2_gain, ln2_bias)
    grad_mixed_part, grad_gain_two, grad_bias_two = norm_two_back(grad_normed_two)
    grad_mixed = grad_out_low.astype(jnp.float32) + grad_mixed_part
    grad_mixed_low = grad_mixed.astype(jnp.bfloat16)
    grad_proj = contract_rows(attended_low, grad_mixed_low)
    grad_attended_low = against_weight(grad_mixed_low, w_proj).astype(jnp.bfloat16)
    grad_heads = head_view(grad_attended_low, head_count)

    def delta_step(running, block_index):
        key_heads, value_heads, visible = block_inputs(block_index)
        attn_probs = weights_of(scores_of(query_heads, key_heads, score_scale), visible, logsum)
        grad_probs = jnp.einsum(
            "qhd,khd->hqk", grad_heads, value_heads, preferred_element_type=jnp.float32
        )
        return (running + jnp.sum(attn_probs * grad_probs, axis=-1), None)

    row_delta, _ = lax.scan(delta_step, jnp.zeros((head_count, row_count), jnp.float32), block_ids)

    def score_grads(
        query_part, grad_part, logsum_part, delta_part, key_heads, value_heads, visible
    ):
        attn_probs = weights_of(scores_of(query_part, key_heads, score_scale), visible, logsum_part)
        grad_probs = jnp.einsum(
            "qhd,khd->hqk", grad_part, value_heads, preferred_element_type=jnp.float32
        )
        grad_scores = (attn_probs * (grad_probs - delta_part[:, :, None])).astype(jnp.bfloat16)
        return (attn_probs, grad_scores)

    def pair_step(running, block_index):
        key_heads, value_heads, visible = block_inputs(block_index)
        attn_probs, grad_scores = score_grads(
            query_heads, grad_heads, logsum, row_delta, key_heads, value_heads, visible
        )
        key_term = (
            jnp.einsum("hqk,qhd->khd", grad_scores, query_heads, preferred_element_type=jnp.float32)
            * score_scale
        )
        value_term = jnp.einsum(
            "hqk,qhd->khd",
            attn_probs.astype(jnp.bfloat16),
            grad_heads,
            preferred_element_type=jnp.float32,
        )
        joined = jnp.concatenate(
            [key_term.reshape(key_block, model_width), value_term.reshape(key_block, model_width)],
            axis=1,
        )
        step_query = jnp.einsum(
            "hqk,khd->qhd", grad_scores, key_heads, preferred_element_type=jnp.float32
        )
        return (running + step_query, joined)

    grad_query, key_terms = lax.scan(
        pair_step, jnp.zeros(query_heads.shape, jnp.float32), block_ids
    )
    key_sums = lax.psum_scatter(
        key_terms.reshape(seq_len, 2 * model_width).astype(jnp.bfloat16),
        "blk",
        scatter_dimension=0,
        tiled=True,
    ).astype(jnp.float32)
    grad_key = key_sums[:, :model_width]
    grad_value = key_sums[:, model_width:]
    grad_query = grad_query.reshape(row_count, model_width) * score_scale
    grad_qkv_low = jnp.concatenate([grad_query, grad_key, grad_value], axis=1).astype(jnp.bfloat16)
    grad_wqkv = contract_rows(normed_one_low, grad_qkv_low)
    grad_normed_one = against_weight(grad_qkv_low, w_qkv)
    _, norm_one_back = jax.vjp(layer_norm, residual, ln1_gain, ln1_bias)
    grad_resid, grad_gain_one, grad_bias_one = norm_one_back(grad_normed_one)
    grad_input = (grad_mixed + grad_resid).astype(jnp.bfloat16)[None]
    (
        fc1_share,
        fc2_share,
        qkv_share,
        proj_share,
        gain_one_share,
        bias_one_share,
        gain_two_share,
        bias_two_share,
    ) = (
        lax.psum_scatter(
            grad_fc1.astype(jnp.bfloat16), "blk", scatter_dimension=0, tiled=True
        ).astype(jnp.float32),
        lax.psum_scatter(
            grad_fc2.astype(jnp.bfloat16), "blk", scatter_dimension=0, tiled=True
        ).astype(jnp.float32),
        lax.psum_scatter(
            grad_wqkv.astype(jnp.bfloat16), "blk", scatter_dimension=0, tiled=True
        ).astype(jnp.float32),
        lax.psum_scatter(
            grad_proj.astype(jnp.bfloat16), "blk", scatter_dimension=0, tiled=True
        ).astype(jnp.float32),
        lax.psum_scatter(
            grad_gain_one.astype(jnp.bfloat16), "blk", scatter_dimension=0, tiled=True
        ).astype(jnp.float32),
        lax.psum_scatter(
            grad_bias_one.astype(jnp.bfloat16), "blk", scatter_dimension=0, tiled=True
        ).astype(jnp.float32),
        lax.psum_scatter(
            grad_gain_two.astype(jnp.bfloat16), "blk", scatter_dimension=0, tiled=True
        ).astype(jnp.float32),
        lax.psum_scatter(
            grad_bias_two.astype(jnp.bfloat16), "blk", scatter_dimension=0, tiled=True
        ).astype(jnp.float32),
    )
    totals = (
        lax.psum(qkv_share.astype(jnp.bfloat16), "dp").astype(jnp.float32),
        lax.psum(proj_share.astype(jnp.bfloat16), "dp").astype(jnp.float32),
        lax.psum(fc1_share.astype(jnp.bfloat16), "dp").astype(jnp.float32),
        lax.psum(fc2_share.astype(jnp.bfloat16), "dp").astype(jnp.float32),
        lax.psum(gain_one_share.astype(jnp.bfloat16), "dp").astype(jnp.float32),
        lax.psum(bias_one_share.astype(jnp.bfloat16), "dp").astype(jnp.float32),
        lax.psum(gain_two_share.astype(jnp.bfloat16), "dp").astype(jnp.float32),
        lax.psum(bias_two_share.astype(jnp.bfloat16), "dp").astype(jnp.float32),
    )
    return (
        output,
        grad_input,
        totals[0],
        totals[1],
        totals[2],
        totals[3],
        totals[4],
        totals[5],
        totals[6],
        totals[7],
    )


MESH = pl.DeviceIdType.MESH
F32 = jnp.float32
BF16 = jnp.bfloat16
RUN_ROWS = 128
HEAD = 64
SKEW = 3


def mm(left, right):
    return lax.dot_general(left, right, (((1,), (0,)), ((), ())), preferred_element_type=F32)


def mm_nt(left, right):
    return lax.dot_general(left, right, (((1,), (1,)), ((), ())), preferred_element_type=F32)


def mm_tn(left, right):
    return lax.dot_general(left, right, (((0,), (0,)), ((), ())), preferred_element_type=F32)


def norm_parts(rows):
    centred = rows - jnp.mean(rows, axis=-1, keepdims=True)
    inv_std = lax.rsqrt(jnp.mean(centred * centred, axis=-1, keepdims=True) + EPSILON)
    return centred * inv_std, inv_std


def norm_back(grad_rows, hat, inv_std, gain):
    grad_hat = grad_rows * gain
    return inv_std * (
        grad_hat
        - jnp.mean(grad_hat, axis=-1, keepdims=True)
        - hat * jnp.mean(grad_hat * hat, axis=-1, keepdims=True)
    )


def gelu_pair(u):
    inner = 0.7978845608028654 * (u + 0.044715 * u * u * u)
    t = jnp.tanh(inner)
    half = 0.5 * (1.0 + t)
    slope = half + 0.5 * u * (1.0 - t * t) * (0.7978845608028654 * (1.0 + 0.134145 * u * u))
    return u * half, slope


def layer_kernel(Z, names, *refs):
    r = dict(zip(names, refs, strict=True))
    z = lax.axis_index("dp")
    b = lax.axis_index("blk")
    e = lax.rem(b, 2)
    chip = b // 2
    cx = lax.rem(chip, 2)
    cy = chip // 2
    scale = HEAD**-0.5

    def chip_at(delta):
        dx, dy = delta % 2, delta // 2
        return 2 * (cy + dy - 2 * cy * dy) + (cx + dx - 2 * cx * dx)

    def dev(delta):
        return (z, 2 * chip_at(delta) + e)

    other = (z, b + 1 - 2 * e)

    def remote(src, dst, send_sem, recv_sem, device):
        sems = [s[0].at[s[1]] if isinstance(s, tuple) else s for s in (send_sem, recv_sem)]
        return pltpu.make_async_remote_copy(
            src_ref=src, dst_ref=dst, send_sem=sems[0], recv_sem=sems[1],
            device_id=device, device_id_type=MESH,
        )

    loads = {}

    def load(name, src, dst):
        loads[name] = pltpu.make_async_copy(src, dst, r["ld_sem"].at[len(loads)])
        loads[name].start()

    load("x", r["x"], r["xb"].at[b])
    load("w_qkv", r["w_qkv"], r["wq"])
    load("w_proj", r["w_proj"], r["wp"])
    load("dy", r["dy"], r["dyb"].at[b])
    load("w_fc1", r["w_fc1"], r["w1"])
    load("w_fc2", r["w_fc2"], r["w2"])

    bar = pltpu.get_barrier_semaphore()
    for target in (other, dev(1), dev(2), dev(3)):
        pl.semaphore_signal(bar, inc=1, device_id=target, device_id_type=MESH)

    @pl.when(z > 0)
    def _():
        pl.semaphore_signal(bar, inc=1, device_id=(z - 1, b), device_id_type=MESH)

    @pl.when(z < Z - 1)
    def _():
        pl.semaphore_signal(bar, inc=1, device_id=(z + 1, b), device_id_type=MESH)

    pl.semaphore_wait(bar, 4 + jnp.minimum(z, 1) + jnp.minimum(Z - 1 - z, 1))

    class Gather:
        def __init__(self, buf, ss, rs):
            self.buf, self.ss, self.rs = buf, ss, rs

        def slot(self, m):
            return 2 * chip_at(m // 2) + (e if m % 2 == 0 else 1 - e)

        def hop(self, delta, src=None):
            at = b if src is not None else self.slot(2 * delta)
            src = self.buf.at[at] if src is None else src
            return remote(src, self.buf.at[at], (self.ss, 2 * delta), (self.rs, 2 * delta), dev(delta))

        def half(self, part, delta, towards):
            at = (self.slot(2 * delta), pl.ds(64 * part, 64))
            return remote(self.buf.at[at], self.buf.at[at], (self.ss, 6 + 2 * part), (self.rs, 6 + 2 * part), dev(towards))

        def core(self, delta, src=None):
            at = b if src is not None else self.slot(2 * delta)
            src = self.buf.at[at] if src is None else src
            return remote(src, self.buf.at[at], (self.ss, 2 * delta + 1), (self.rs, 2 * delta + 1), other)

        def send(self, src):
            self.hop(1, src).start()
            self.hop(2, src).start()
            self.core(0, src).start()

        def pass_on(self):
            self.hop(1).wait_recv()
            self.half(0, 1, 2).start()
            self.hop(2).wait_recv()
            self.half(1, 2, 1).start()
            self.core(1).start()
            self.core(2).start()

        def pass_diagonal(self):
            self.half(0, 3, 2).wait_recv()
            self.half(1, 3, 1).wait_recv()
            self.core(3).start()

        def wait_core(self, delta):
            at = self.slot(2 * delta + 1)
            remote(self.buf.at[at], self.buf.at[at], (self.ss, 2 * delta + 1), (self.rs, 2 * delta + 1), other).wait_recv()

        def finish(self, src):
            self.hop(1, src).wait_send()
            self.hop(2, src).wait_send()
            self.half(0, 1, 2).wait_send()
            self.half(1, 2, 1).wait_send()
            self.core(0, src).wait_send()
            for delta in (1, 2, 3):
                self.core(delta).wait_send()

    gx = Gather(r["xb"], r["gx_s"], r["gx_r"])
    gdy = Gather(r["dyb"], r["gdy_s"], r["gdy_r"])

    class Chain:
        def __init__(self, name, K, dtype, sink):
            self.K, self.dtype, self.sink = K, dtype, sink
            for part in ("own", "rl", "rr", "tu", "td", "su", "sd", "ru", "rd"):
                setattr(self, part, r[name + "_" + part])

        def up(self, src, k):
            return remote(src, self.rl.at[k], (self.su, k), (self.ru, k), (z + 1, b))

        def down(self, src, k):
            return remote(src, self.rr.at[k], (self.sd, k), (self.rd, k), (z - 1, b))

        def prime(self, k):
            if Z == 1:
                return

            @pl.when(z == 0)
            def _():
                self.up(self.own.at[k], k).start()

            @pl.when(z == Z - 1)
            def _():
                self.down(self.own.at[k], k).start()

        def tick(self, i):
            ku = i - 1 - SKEW * (z - 1)

            @pl.when((z > 0) & (z < Z - 1) & (ku >= 0) & (ku < self.K))
            def _():
                self.up(self.own.at[ku], ku).wait_recv()
                self.tu[ku] = (self.own[ku].astype(F32) + self.rl[ku].astype(F32)).astype(self.dtype)
                self.up(self.tu.at[ku], ku).start()

            kd = i - 1 - SKEW * (Z - 2 - z)

            @pl.when((z > 0) & (z < Z - 1) & (kd >= 0) & (kd < self.K))
            def _():
                self.down(self.own.at[kd], kd).wait_recv()
                self.td[kd] = (self.own[kd].astype(F32) + self.rr[kd].astype(F32)).astype(self.dtype)
                self.down(self.td.at[kd], kd).start()

            k = i - 1 - SKEW * max(Z - 2, 0)
            if 0 <= k < self.K:

                @pl.when(z == 0)
                def _():
                    if Z > 1:
                        self.down(self.own.at[k], k).wait_recv()
                    self.sink(k, self.own[k].astype(F32) + self.rr[k].astype(F32))

                @pl.when((z == Z - 1) & (z > 0))
                def _():
                    self.up(self.own.at[k], k).wait_recv()
                    self.sink(k, self.own[k].astype(F32) + self.rl[k].astype(F32))

                @pl.when((z > 0) & (z < Z - 1))
                def _():
                    self.sink(
                        k,
                        self.own[k].astype(F32) + self.rl[k].astype(F32) + self.rr[k].astype(F32),
                    )

        def finish(self):
            @pl.when(z < Z - 1)
            def _():
                for k in range(self.K):
                    self.up(self.own.at[k], k).wait_send()

            @pl.when(z > 0)
            def _():
                for k in range(self.K):
                    self.down(self.own.at[k], k).wait_send()

    def sink_a(k, total):
        low = total.astype(BF16)
        if k < 8:
            r["o_fc2"][96 * (k // 2) : 96 * (k // 2) + 96, 384 * (k % 2) : 384 * (k % 2) + 384] = low
        else:
            src = chip_at((k - 8) // 2)
            r["o_fc1"][:, pl.ds(pl.multiple_of(768 * src + 384 * (k % 2), 128), 384)] = low

    def sink_b(k, total):
        r["o_qkv"][chip_at(k)] = total.astype(BF16)

    def sink_p(k, total):
        r["o_proj"][:, 384 * k : 384 * k + 384] = total.astype(BF16)

    def sink_c(k, total):
        for i in range(8):
            r["lnc"][i] = total[:, 96 * i : 96 * i + 96]
        r["o_ln"][...] = r["lnc"][b]

    ca = Chain("ca", 16, BF16, sink_a)
    cb = Chain("cb", 4, BF16, sink_b)
    cp = Chain("cp", 2, BF16, sink_p)
    cc = Chain("cc", 1, F32, sink_c)
    line = ((ca, 0), (cb, 16), (cp, 20), (cc, 22))
    beats = [0]

    def beat(count=1):
        for _ in range(count):
            beats[0] += 1
            for chain, first in line:
                if 1 <= beats[0] - first <= chain.K + SKEW * max(Z - 2, 0):
                    chain.tick(beats[0] - first)

    gx.send(r["x"])

    crop = [r["crops"][0, RUN_ROWS * i] for i in range(8)]
    places = []
    for i in range(8):
        place = 2 * crop[i]
        for h in range(i):
            place = place + jnp.where(crop[h] == crop[i], 1, 0)
        places.append(place)
        r["inv"][i] = place
    for s in range(8):
        run = jnp.int32(0)
        for i in range(8):
            run = run + jnp.where(places[i] == s, i, 0)
        r["perm"][s] = run

    g1, b1 = r["ln1_gain"][...].reshape(1, 768), r["ln1_bias"][...].reshape(1, 768)
    g2, b2 = r["ln2_gain"][...].reshape(1, 768), r["ln2_bias"][...].reshape(1, 768)

    loads["x"].wait()
    loads["w_qkv"].wait()
    for i in range(4):
        for t in range(3):
            first = 768 * t + 192 * i
            r["wo"][i, :, 128 * t : 128 * t + 128] = r["wq"][:, first : first + 128]
            r["wo"][i, :, 384 + 64 * t : 448 + 64 * t] = r["wq"][:, first + 128 : first + 192]

    def project(delta):
        gx.wait_core(delta)
        pair = pl.ds(2 * chip_at(delta), 2)
        hat, _ = norm_parts(r["xb"][pair].reshape(256, 768).astype(F32))
        normed = (hat * g1 + b1).astype(BF16)
        r["n1"][pair] = normed.reshape(2, 128, 768)
        for t in range(3):
            out = mm(normed, r["wq"][:, pl.ds(pl.multiple_of(768 * t + 384 * e, 128), 384)])
            out = out * scale if t == 0 else out
            r["qkv"][pair, :, 384 * t : 384 * t + 384] = out.astype(BF16).reshape(2, 128, 384)

    project(0)
    gx.pass_on()
    gdy.send(r["dy"])
    project(1)
    project(2)
    gx.pass_diagonal()
    project(3)

    low_lanes = lax.broadcasted_iota(jnp.int32, (1, 128), 1) < HEAD

    def stack(two):
        none = jnp.zeros_like(two)
        return jnp.concatenate([jnp.where(low_lanes, two, none), jnp.where(low_lanes, none, two)], axis=0)

    def o_core(at):
        place = (e, pl.ds(2 * at, 2))
        return remote(r["ob"].at[place], r["ob"].at[place], (r["o_s"], at), (r["o_r"], at), other)

    def attend(at, carry):
        run0, run1 = r["perm"][2 * at], r["perm"][2 * at + 1]
        outs = []
        for h in range(3):
            q, k, v = [
                jnp.concatenate(
                    [r["qkv"][run, :, 384 * t + 128 * h : 384 * t + 128 * h + 128] for run in (run0, run1)],
                    axis=0,
                )
                for t in range(3)
            ]
            s = mm_nt(stack(q), k)
            p = jnp.exp(s - jnp.max(s, axis=-1, keepdims=True))
            o = mm(p.astype(BF16), v) / jnp.sum(p, axis=-1, keepdims=True)
            outs.append(jnp.where(low_lanes, o[0:256], o[256:512]))
        low = jnp.concatenate(outs, axis=1).astype(BF16)
        r["ob"][e, pl.ds(2 * at, 2)] = low.reshape(2, 128, 384)
        o_core(at).start()
        return carry

    lax.fori_loop(0, 3, attend, 0)
    gdy.pass_on()
    attend(3, 0)
    for name in ("w_proj", "w_fc1", "w_fc2", "dy"):
        loads[name].wait()
    for at in range(4):
        place = (1 - e, pl.ds(2 * at, 2))
        remote(r["ob"].at[place], r["ob"].at[place], (r["o_s"], at), (r["o_r"], at), other).wait_recv()

    def o_rows(run):
        at = r["inv"][run]
        return jnp.concatenate([r["ob"][0, at], r["ob"][1, at]], axis=1)

    own_hidden = pl.ds(pl.multiple_of(384 * b, 128), 384)

    def feed(c, carry):
        pair = pl.ds(2 * c, 2)
        o = jnp.concatenate([o_rows(2 * c), o_rows(2 * c + 1)], axis=0)
        x1 = r["xb"][pair].reshape(256, 768).astype(F32) + mm(o, r["wp"][...])
        r["x1"][pair] = x1.reshape(2, 128, 768)
        hat, _ = norm_parts(x1)
        n2 = (hat * g2 + b2).astype(BF16)
        r["n2"][pair] = n2.reshape(2, 128, 768)
        act, slope = gelu_pair(mm(n2, r["w1"][:, own_hidden]))
        r["act"][pair] = act.astype(BF16).reshape(2, 128, 384)
        r["slope"][pair] = slope.reshape(2, 128, 384)
        return carry

    for c in range(4):
        feed(c, 0)
    gdy.pass_diagonal()
    for delta in range(4):
        gdy.wait_core(delta)

    grad = mm_tn(r["act"][...].reshape(1024, 384), r["dyb"][...].reshape(1024, 768)).astype(BF16)
    for k in range(8):
        ca.own[k] = grad[96 * (k // 2) : 96 * (k // 2) + 96, 384 * (k % 2) : 384 * (k % 2) + 384]
        ca.prime(k)

    n2_own = r["n2"][b]
    dy_own = r["dyb"][b]
    r["y"][...] = r["x1"][b]
    r["dn2"][...] = jnp.zeros((128, 768), F32)

    def own_rows(i, carry):
        part = pl.ds(768 * i, 768)
        act, slope = gelu_pair(mm(r["n2"][b], r["w1"][:, part]))
        du = (mm_nt(r["dyb"][b], r["w2"][part]) * slope).astype(BF16)
        r["dn2"][...] += mm_nt(du, r["w1"][:, part])
        r["y"][...] += mm(act.astype(BF16), r["w2"][part])
        return carry

    for i in range(4):
        own_rows(i, 0)
        if i == 3:
            beat()
    r["o_y"][...] = r["y"][...].astype(BF16)

    dn2 = r["dn2"][...]
    hat, inv_std = norm_parts(r["x1"][b])
    r["lnp"][2:3] = jnp.sum(dn2 * hat, axis=0, keepdims=True)
    r["lnp"][3:4] = jnp.sum(dn2, axis=0, keepdims=True)
    dx1 = dy_own.astype(F32) + norm_back(dn2, hat, inv_std, g2)
    r["dx1"][...] = dx1
    low = dx1.astype(BF16)
    do = mm_nt(low, r["wp"][...]).astype(BF16)
    for i in range(4):
        r["dos"][i] = do[:, 192 * i : 192 * i + 192]

    def do_send(delta):
        return remote(r["dos"].at[chip_at(delta)], r["dob"].at[b], (r["do_s"], 2 * delta), (r["do_r"], 2 * delta), dev(delta))

    def do_slot(m):
        return 2 * chip_at(m // 2) + (e if m % 2 == 0 else 1 - e)

    def do_core(delta):
        src = r["dos"].at[chip] if delta == 0 else r["dob"].at[do_slot(2 * delta)]
        return remote(src, r["dob"].at[do_slot(2 * delta)], (r["do_s"], 2 * delta + 1), (r["do_r"], 2 * delta + 1), other)

    for delta in (3, 2, 1):
        do_send(delta).start()
    do_core(0).start()
    r["dob"][b] = r["dos"][chip]

    def back_hidden(c, carry):
        pair = pl.ds(2 * c, 2)
        da = mm_nt(r["dyb"][pair].reshape(256, 768), r["w2"][own_hidden])
        r["du"][pair] = (da * r["slope"][pair].reshape(256, 384)).astype(BF16).reshape(2, 128, 384)
        return carry

    for c in range(4):
        back_hidden(c, 0)
    grad = mm_tn(r["n2"][...].reshape(1024, 768), r["du"][...].reshape(1024, 384)).astype(BF16)
    for i in range(8):
        r["t1"][i % 2, i // 2] = grad[96 * i : 96 * i + 96]
    t1_core = remote(r["t1"].at[1 - e], r["t1x"], r["t1_cs"], r["t1_cr"], other)
    t1_core.start()
    beat()

    def t1_send(delta, half):
        src = r["t1"].at[e, chip_at(delta)] if half == 0 else r["t1x"].at[chip_at(delta)]
        hidden_core = e if half == 0 else 1 - e
        at = 2 * delta + half
        return remote(src, ca.own.at[8 + 2 * delta + hidden_core], (r["t1_s"], at), (r["t1_r"], at), dev(delta))

    grad = mm_tn(o_rows(b), low).astype(BF16)
    for i in range(8):
        r["tp"][i % 2, i // 2] = grad[96 * i : 96 * i + 96]
    tp_core = remote(r["tp"].at[1 - e], r["tpx"], r["tp_cs"], r["tp_cr"], other)
    tp_core.start()

    def tp_send(delta):
        return remote(r["tps"].at[delta], r["tpr"].at[delta], (r["tp_s"], delta), (r["tp_r"], delta), dev(delta))

    for s in range(4):
        r["n1s"][s] = r["n1"][r["perm"][4 * e + s]]
    r["qo"][...] = mm(r["n1s"][...].reshape(512, 768), r["wo"][chip]).astype(BF16).reshape(2, 256, 576)

    for delta in (1, 2, 3):
        do_send(delta).wait_recv()
        do_core(delta).start()
    t1_core.wait_recv()
    for delta in (1, 2, 3):
        for half in (0, 1):
            t1_send(delta, half).start()
    ca.own[8 + e] = r["t1"][e, chip]
    ca.own[9 - e] = r["t1x"][chip]
    ca.prime(8)
    ca.prime(9)
    beat()
    for delta in range(4):
        at = do_slot(2 * delta + 1)
        remote(r["dob"].at[at], r["dob"].at[at], (r["do_s"], 2 * delta + 1), (r["do_r"], 2 * delta + 1), other).wait_recv()

    def attend_back(at, heads):
        runs = [r["perm"][4 * e + 2 * at + i] for i in range(2)]
        if heads == 2:
            g = jnp.concatenate([r["dob"][run, :, 0:128] for run in runs], axis=0)
            q, k, v = [r["qo"][at, :, 128 * t : 128 * t + 128] for t in range(3)]
            q, g = stack(q), stack(g)
        else:
            g = jnp.concatenate([r["dob"][run, :, 128:192] for run in runs], axis=0)
            q, k, v = [r["qo"][at, :, 384 + 64 * t : 448 + 64 * t] for t in range(3)]
        q = (q.astype(F32) * scale).astype(BF16)
        s = mm_nt(q, k)
        p = jnp.exp(s - jnp.max(s, axis=-1, keepdims=True))
        p = p / jnp.sum(p, axis=-1, keepdims=True)
        dp = mm_nt(g, v)
        ds = (p * (dp - jnp.sum(p * dp, axis=-1, keepdims=True))).astype(BF16)
        dq = mm(ds, k) * scale
        dk = mm_tn(ds, q)
        dv = mm_tn(p.astype(BF16), g)
        mine = pl.ds(2 * (2 * e + at), 2)
        if heads == 2:
            dq = jnp.where(low_lanes, dq[0:256], dq[256:512])
        first, wide = (0, 128) if heads == 2 else (384, 64)
        for t, part in enumerate((dq, dk, dv)):
            r["dq"][mine, :, first + wide * t : first + wide * t + wide] = part.astype(BF16).reshape(2, 128, wide)

    attend_back(0, 2)
    beat()
    attend_back(0, 1)
    beat()
    attend_back(1, 2)
    beat()
    attend_back(1, 1)

    dq_core = remote(r["dq"].at[pl.ds(4 * e, 4)], r["dq"].at[pl.ds(4 * e, 4)], r["dq_cs"], r["dq_cr"], other)
    dq_core.start()
    grad = mm_tn(r["n1s"][...].reshape(512, 768), r["dq"][pl.ds(4 * e, 4)].reshape(512, 576))
    for i in range(8):
        r["tq"][i % 2, i // 2] = grad[96 * i : 96 * i + 96].astype(BF16)
    tq_core = remote(r["tq"].at[1 - e], r["tqx"], r["tq_cs"], r["tq_cr"], other)
    tq_core.start()

    def tq_send(delta):
        return remote(r["tqs"].at[delta], cb.own.at[delta], (r["tq_s"], delta), (r["tq_r"], delta), dev(delta))

    def dq_send(delta):
        return remote(r["dqs"].at[delta], r["dqr"].at[delta], (r["dq_s"], delta), (r["dq_r"], delta), dev(delta))

    beat()

    def t1_arrive(delta):
        for half in (0, 1):
            t1_send(delta, half).wait_recv()
        ca.prime(8 + 2 * delta)
        ca.prime(9 + 2 * delta)

    tq_core.wait_recv()
    for delta in (3, 2, 1, 0):
        c = chip_at(delta)
        total = (r["tq"][e, c].astype(F32) + r["tqx"][c].astype(F32)).astype(BF16)
        if delta == 0:
            cb.own[0] = total
        else:
            r["tqs"][delta] = total
            tq_send(delta).start()
    beat()
    t1_arrive(1)
    at = pl.ds(4 - 4 * e, 4)
    remote(r["dq"].at[at], r["dq"].at[at], r["dq_cs"], r["dq_cr"], other).wait_recv()
    for delta in (3, 2, 1):
        r["dqs"][delta] = r["dq"][r["inv"][2 * chip_at(delta) + e]]
        dq_send(delta).start()
    t1_arrive(2)
    beat()
    t1_arrive(3)
    cb.prime(0)
    tp_core.wait_recv()
    for delta in (3, 2, 1, 0):
        c = chip_at(delta)
        r["tps"][delta] = (r["tp"][e, c].astype(F32) + r["tpx"][c].astype(F32)).astype(BF16)
        if delta > 0:
            tp_send(delta).start()

    def beat_to(count):
        beat(count - beats[0])

    beat_to(14)
    for delta in (1, 2, 3):
        tq_send(delta).wait_recv()
        cb.prime(delta)
    beat_to(18)
    dn1 = mm_nt(r["dq"][r["inv"][b]], r["wo"][chip])
    for delta in (1, 2, 3):
        dq_send(delta).wait_recv()
        dn1 += mm_nt(r["dqr"][delta], r["wo"][chip_at(delta)])
    hat, inv_std = norm_parts(r["xb"][b].astype(F32))
    r["lnp"][0:1] = jnp.sum(dn1 * hat, axis=0, keepdims=True)
    r["lnp"][1:2] = jnp.sum(dn1, axis=0, keepdims=True)
    r["lnp"][4:8] = jnp.zeros((4, 768), F32)
    r["o_gin"][...] = (r["dx1"][...] + norm_back(dn1, hat, inv_std, g1)).astype(BF16)
    ln_core = remote(r["lnp"], r["lnx"].at[0], (r["ln_s"], 0), (r["ln_r"], 0), other)
    ln_core.start()
    total = r["tps"][0].astype(F32)
    for delta in (1, 2, 3):
        tp_send(delta).wait_recv()
        total += r["tpr"][delta].astype(F32)
    for k in range(2):
        cp.own[k] = total[:, 384 * k : 384 * k + 384].astype(BF16)
        cp.prime(k)
    ln_core.wait_recv()
    r["lns"][...] = r["lnp"][...] + r["lnx"][0]

    def ln_send(delta):
        return remote(r["lns"], r["lnx"].at[delta], (r["ln_s"], delta), (r["ln_r"], delta), dev(delta))

    for delta in (3, 2, 1):
        ln_send(delta).start()
    beat_to(20)
    total = r["lns"][...]
    for delta in (1, 2, 3):
        ln_send(delta).wait_recv()
        total += r["lnx"][delta]
    cc.own[0] = total
    cc.prime(0)
    beat_to(23 + SKEW * max(Z - 2, 0))

    gx.finish(r["x"])
    gdy.finish(r["dy"])
    for at in range(4):
        o_core(at).wait_send()
    for copy in (t1_core, tp_core, tq_core, dq_core, ln_core, do_core(0)):
        copy.wait_send()
    for delta in (1, 2, 3):
        do_send(delta).wait_send()
        do_core(delta).wait_send()
        t1_send(delta, 0).wait_send()
        t1_send(delta, 1).wait_send()
        tp_send(delta).wait_send()
        tq_send(delta).wait_send()
        dq_send(delta).wait_send()
        ln_send(delta).wait_send()
    ca.finish()
    cb.finish()
    cp.finish()
    cc.finish()


def widen_kernel(*refs):
    sources, results, held, wide = refs[:7], refs[7:17], refs[17:24], refs[24:32]
    sem_in, sem_out = refs[32:]
    order = (4, 5, 2, 3, 6, 0, 1)
    copies = {i: pltpu.make_async_copy(sources[i], held[i], sem_in.at[i]) for i in order}
    for copy in copies.values():
        copy.start()
    leaving = []

    def leave(src, at):
        copy = pltpu.make_async_copy(src, results[at], sem_out.at[at])
        copy.start()
        leaving.append(copy)

    for i in order:
        copies[i].wait()
        part = held[i]
        if i < 2:
            leave(part, i)
        elif i == 2:
            for t in range(3):
                parts = []
                for c in range(4):
                    parts.append(part[c, :, 128 * t : 128 * t + 128])
                    parts.append(part[c, :, 384 + 64 * t : 448 + 64 * t])
                wide[0][:, 768 * t : 768 * t + 768] = jnp.concatenate(parts, axis=1).astype(F32)
            leave(wide[0], 2)
        elif i < 6:
            wide[i - 2][...] = part[...].astype(F32)
            leave(wide[i - 2], i)
        else:
            for t in range(4):
                wide[4 + t][...] = part[t, :]
                leave(wide[4 + t], 6 + t)
    for copy in leaving:
        copy.wait()


def fast_shards(
    Z, inputs, crops, ln1_gain, ln1_bias, w_qkv, w_proj, ln2_gain, ln2_bias, w_fc1, w_fc2, cotangent
):
    V, D = pltpu.VMEM, pltpu.SemaphoreType.DMA
    anyspace = pl.BlockSpec(memory_space=pl.ANY)
    vmem = pl.BlockSpec(memory_space=pltpu.VMEM)
    smem = pl.BlockSpec(memory_space=pltpu.SMEM)
    arguments = dict(
        x=(inputs[0], anyspace),
        crops=(crops, smem),
        ln1_gain=(ln1_gain, vmem),
        ln1_bias=(ln1_bias, vmem),
        w_qkv=(w_qkv, anyspace),
        w_proj=(w_proj, anyspace),
        ln2_gain=(ln2_gain, vmem),
        ln2_bias=(ln2_bias, vmem),
        w_fc1=(w_fc1, anyspace),
        w_fc2=(w_fc2, anyspace),
        dy=(cotangent[0], anyspace),
    )
    results = dict(
        o_y=((128, 768), BF16),
        o_gin=((128, 768), BF16),
        o_qkv=((4, 96, 576), BF16),
        o_proj=((96, 768), BF16),
        o_fc1=((96, 3072), BF16),
        o_fc2=((384, 768), BF16),
        o_ln=((8, 96), F32),
    )
    scratch = dict(
        ld_sem=D((6,)),
        perm=pltpu.SMEM((8,), jnp.int32),
        inv=pltpu.SMEM((8,), jnp.int32),
        xb=V((8, 128, 768), BF16), gx_s=D((9,)), gx_r=D((9,)),
        dyb=V((8, 128, 768), BF16), gdy_s=D((9,)), gdy_r=D((9,)),
        dob=V((8, 128, 192), BF16), dos=V((4, 128, 192), BF16), do_s=D((8,)), do_r=D((8,)),
        wq=V((768, 2304), BF16), wo=V((4, 768, 576), BF16), wp=V((768, 768), BF16),
        w1=V((768, 3072), BF16), w2=V((3072, 768), BF16),
        n1=V((8, 128, 768), BF16), n1s=V((4, 128, 768), BF16), qkv=V((8, 128, 1152), BF16),
        ob=V((2, 8, 128, 384), BF16), o_s=D((4,)), o_r=D((4,)),
        x1=V((8, 128, 768), F32), n2=V((8, 128, 768), BF16),
        act=V((8, 128, 384), BF16), slope=V((8, 128, 384), F32), du=V((8, 128, 384), BF16),
        y=V((128, 768), F32), dn2=V((128, 768), F32), dx1=V((128, 768), F32),
        t1=V((2, 4, 96, 384), BF16), t1x=V((4, 96, 384), BF16),
        t1_cs=D, t1_cr=D, t1_s=D((8,)), t1_r=D((8,)),
        tp=V((2, 4, 96, 768), BF16), tpx=V((4, 96, 768), BF16), tps=V((4, 96, 768), BF16), tpr=V((4, 96, 768), BF16),
        tp_cs=D, tp_cr=D, tp_s=D((4,)), tp_r=D((4,)),
        qo=V((2, 256, 576), BF16), dq=V((8, 128, 576), BF16),
        tq=V((2, 4, 96, 576), BF16), tqx=V((4, 96, 576), BF16), tqs=V((4, 96, 576), BF16),
        tq_cs=D, tq_cr=D, tq_s=D((4,)), tq_r=D((4,)),
        dqs=V((4, 128, 576), BF16), dqr=V((4, 128, 576), BF16),
        dq_cs=D, dq_cr=D, dq_s=D((4,)), dq_r=D((4,)),
        lnp=V((8, 768), F32), lns=V((8, 768), F32), lnx=V((4, 8, 768), F32), lnc=V((8, 8, 96), F32),
        ln_s=D((4,)), ln_r=D((4,)),
    )
    for name, K, shape, dtype in (
        ("ca", 16, (96, 384), BF16), ("cb", 4, (96, 576), BF16), ("cp", 2, (96, 384), BF16), ("cc", 1, (8, 768), F32)
    ):
        for part in ("own", "rl", "rr", "tu", "td"):
            scratch[name + "_" + part] = V((K, *shape), dtype)
        for part in ("su", "sd", "ru", "rd"):
            scratch[name + "_" + part] = D((K,))
    names = (*arguments, *results, *scratch)
    narrow = pl.pallas_call(
        functools.partial(layer_kernel, Z, names),
        out_shape=[jax.ShapeDtypeStruct(*shape) for shape in results.values()],
        in_specs=[spec for _, spec in arguments.values()],
        out_specs=[vmem] * len(results),
        scratch_shapes=list(scratch.values()),
        compiler_params=pltpu.CompilerParams(
            collective_id=0, has_side_effects=True, vmem_limit_bytes=60 * 2**20
        ),
    )(*[array for array, _ in arguments.values()])
    wide = [((128, 768), BF16), ((128, 768), BF16), ((96, 2304), F32), ((96, 768), F32), ((96, 3072), F32), ((384, 768), F32)]
    wide += [((96,), F32)] * 4
    y, gin, *grads = pl.pallas_call(
        widen_kernel,
        out_shape=[jax.ShapeDtypeStruct(*shape) for shape in wide],
        in_specs=[anyspace] * len(narrow),
        out_specs=[anyspace] * len(wide),
        scratch_shapes=[V(*shape) for shape in results.values()]
        + [V(*shape) for shape in wide[2:6]]
        + [V((96,), F32)] * 4
        + [D((len(narrow),)), D((len(wide),))],
        compiler_params=pltpu.CompilerParams(vmem_limit_bytes=62 * 2**20),
    )(*narrow)
    return (y[None], gin[None], *grads)


def solution(mesh):
    placed = (
        P("dp", "blk", None),
        P("dp", None),
        P(),
        P(),
        P(),
        P(),
        P(),
        P(),
        P(),
        P(),
        P("dp", "blk", None),
    )
    def whole(*arrays):
        one_run = arrays[0].shape[1] == 8 * RUN_ROWS and mesh.shape["blk"] == 8
        body = functools.partial(fast_shards, mesh.shape["dp"]) if one_run else shards
        return placed_call(body)(*arrays)

    placed_call = lambda body: jax.shard_map(
        body,
        mesh=mesh,
        in_specs=placed,
        out_specs=(
            P("dp", "blk", None),
            P("dp", "blk", None),
            P("blk", None),
            P("blk", None),
            P("blk", None),
            P("blk", None),
            P("blk"),
            P("blk"),
            P("blk"),
            P("blk"),
        ),
        check_vma=False,
    )
    return whole
```

```python
import functools
import math

import jax
import jax.numpy as jnp
from jax import lax
from jax.experimental import pallas as pl
from jax.experimental.pallas import tpu as pltpu
from jax.sharding import PartitionSpec as P

HEADS = 12


EPSILON = 1e-05
MASKED = -1e30


def layer_norm(values_in, gain_in, shift_in):
    row_mean = jnp.mean(values_in, axis=-1, keepdims=True)
    centred = values_in - row_mean
    row_var = jnp.mean(centred * centred, axis=-1, keepdims=True)
    return centred * lax.rsqrt(row_var + EPSILON) * gain_in + shift_in


def contract_rows(left_side, right_side):
    return lax.dot_general(
        left_side, right_side, (((0,), (0,)), ((), ())), preferred_element_type=jnp.float32
    )


def against_weight(grad_rows, weight_mat):
    return lax.dot_general(
        grad_rows, weight_mat, (((1,), (1,)), ((), ())), preferred_element_type=jnp.float32
    )


def head_view(matrix, head_count):
    return matrix.reshape(matrix.shape[0], head_count, matrix.shape[1] // head_count)


def scores_of(query_heads, key_heads, score_scale):
    return (
        jnp.einsum("qhd,khd->hqk", query_heads, key_heads, preferred_element_type=jnp.float32)
        * score_scale
    )


def weights_of(scores, visible, logsum):
    return jnp.where(visible[None], jnp.exp(scores - logsum[:, :, None]), 0.0)


def shards(
    inputs, crops, ln1_gain, ln1_bias, w_qkv, w_proj, ln2_gain, ln2_bias, w_fc1, w_fc2, cotangent
):
    row_count = inputs.shape[1]
    model_width = inputs.shape[2]
    head_count = HEADS
    score_scale = 1.0 / math.sqrt(model_width // head_count)
    seq_crops = crops[0]
    seq_len = seq_crops.shape[0]
    key_block = min(1024, seq_len)
    block_count = seq_len // key_block
    block_ids = jnp.arange(block_count)
    own_crops = lax.dynamic_slice_in_dim(seq_crops, lax.axis_index("blk") * row_count, row_count, 0)
    residual = inputs[0].astype(jnp.float32)
    normed_one_low = layer_norm(residual, ln1_gain, ln1_bias).astype(jnp.bfloat16)
    qkv_low = jnp.dot(normed_one_low, w_qkv, preferred_element_type=jnp.float32).astype(
        jnp.bfloat16
    )
    query_own = qkv_low[:, :model_width]
    key_own = qkv_low[:, model_width : 2 * model_width]
    value_own = qkv_low[:, 2 * model_width :]
    keys_all, values_all = (
        lax.all_gather(key_own, "blk", axis=0, tiled=True),
        lax.all_gather(value_own, "blk", axis=0, tiled=True),
    )
    query_heads = head_view(query_own, head_count)

    def block_inputs(block_index):
        key_heads = head_view(
            lax.dynamic_slice_in_dim(keys_all, block_index * key_block, key_block, 0), head_count
        )
        value_heads = head_view(
            lax.dynamic_slice_in_dim(values_all, block_index * key_block, key_block, 0), head_count
        )
        crop_block = lax.dynamic_slice_in_dim(seq_crops, block_index * key_block, key_block, 0)
        visible = own_crops[:, None] == crop_block[None, :]
        return (key_heads, value_heads, visible)

    def stats_step(carried, block_index):
        old_max, summed = carried
        key_heads, value_heads, visible = block_inputs(block_index)
        scores = jnp.where(visible[None], scores_of(query_heads, key_heads, score_scale), MASKED)
        new_max = jnp.maximum(old_max, jnp.max(scores, axis=-1))
        exp_terms = jnp.where(visible[None], jnp.exp(scores - new_max[:, :, None]), 0.0)
        return ((new_max, summed * jnp.exp(old_max - new_max) + jnp.sum(exp_terms, axis=-1)), None)

    start_max = jnp.full((head_count, row_count), MASKED, jnp.float32)
    start_sum = jnp.zeros((head_count, row_count), jnp.float32)
    (row_max, summed), _ = lax.scan(stats_step, (start_max, start_sum), block_ids)
    logsum = row_max + jnp.log(summed)

    def output_step(running, block_index):
        key_heads, value_heads, visible = block_inputs(block_index)
        attn_probs = weights_of(
            scores_of(query_heads, key_heads, score_scale), visible, logsum
        ).astype(jnp.bfloat16)
        return (
            running
            + jnp.einsum(
                "hqk,khd->qhd", attn_probs, value_heads, preferred_element_type=jnp.float32
            ),
            None,
        )

    attended, _ = lax.scan(output_step, jnp.zeros(query_heads.shape, jnp.float32), block_ids)
    attended_low = attended.reshape(row_count, model_width).astype(jnp.bfloat16)
    mixed_rows = residual + jnp.dot(attended_low, w_proj, preferred_element_type=jnp.float32)
    normed_two_low = layer_norm(mixed_rows, ln2_gain, ln2_bias).astype(jnp.bfloat16)
    hidden_pre = jnp.dot(normed_two_low, w_fc1, preferred_element_type=jnp.float32)
    active, gelu_back = jax.vjp(jax.nn.gelu, hidden_pre)
    active_low = active.astype(jnp.bfloat16)
    result = mixed_rows + jnp.dot(active_low, w_fc2, preferred_element_type=jnp.float32)
    output = result.astype(jnp.bfloat16)[None]
    grad_out_low = cotangent[0]
    grad_fc2 = contract_rows(active_low, grad_out_low)
    grad_active = against_weight(grad_out_low, w_fc2)
    grad_hidden_low = gelu_back(grad_active)[0].astype(jnp.bfloat16)
    grad_fc1 = contract_rows(normed_two_low, grad_hidden_low)
    grad_normed_two = against_weight(grad_hidden_low, w_fc1)
    _, norm_two_back = jax.vjp(layer_norm, mixed_rows, ln2_gain, ln2_bias)
    grad_mixed_part, grad_gain_two, grad_bias_two = norm_two_back(grad_normed_two)
    grad_mixed = grad_out_low.astype(jnp.float32) + grad_mixed_part
    grad_mixed_low = grad_mixed.astype(jnp.bfloat16)
    grad_proj = contract_rows(attended_low, grad_mixed_low)
    grad_attended_low = against_weight(grad_mixed_low, w_proj).astype(jnp.bfloat16)
    grad_heads = head_view(grad_attended_low, head_count)

    def delta_step(running, block_index):
        key_heads, value_heads, visible = block_inputs(block_index)
        attn_probs = weights_of(scores_of(query_heads, key_heads, score_scale), visible, logsum)
        grad_probs = jnp.einsum(
            "qhd,khd->hqk", grad_heads, value_heads, preferred_element_type=jnp.float32
        )
        return (running + jnp.sum(attn_probs * grad_probs, axis=-1), None)

    row_delta, _ = lax.scan(delta_step, jnp.zeros((head_count, row_count), jnp.float32), block_ids)

    def score_grads(
        query_part, grad_part, logsum_part, delta_part, key_heads, value_heads, visible
    ):
        attn_probs = weights_of(scores_of(query_part, key_heads, score_scale), visible, logsum_part)
        grad_probs = jnp.einsum(
            "qhd,khd->hqk", grad_part, value_heads, preferred_element_type=jnp.float32
        )
        grad_scores = (attn_probs * (grad_probs - delta_part[:, :, None])).astype(jnp.bfloat16)
        return (attn_probs, grad_scores)

    def pair_step(running, block_index):
        key_heads, value_heads, visible = block_inputs(block_index)
        attn_probs, grad_scores = score_grads(
            query_heads, grad_heads, logsum, row_delta, key_heads, value_heads, visible
        )
        key_term = (
            jnp.einsum("hqk,qhd->khd", grad_scores, query_heads, preferred_element_type=jnp.float32)
            * score_scale
        )
        value_term = jnp.einsum(
            "hqk,qhd->khd",
            attn_probs.astype(jnp.bfloat16),
            grad_heads,
            preferred_element_type=jnp.float32,
        )
        joined = jnp.concatenate(
            [key_term.reshape(key_block, model_width), value_term.reshape(key_block, model_width)],
            axis=1,
        )
        step_query = jnp.einsum(
            "hqk,khd->qhd", grad_scores, key_heads, preferred_element_type=jnp.float32
        )
        return (running + step_query, joined)

    grad_query, key_terms = lax.scan(
        pair_step, jnp.zeros(query_heads.shape, jnp.float32), block_ids
    )
    key_sums = lax.psum_scatter(
        key_terms.reshape(seq_len, 2 * model_width).astype(jnp.bfloat16),
        "blk",
        scatter_dimension=0,
        tiled=True,
    ).astype(jnp.float32)
    grad_key = key_sums[:, :model_width]
    grad_value = key_sums[:, model_width:]
    grad_query = grad_query.reshape(row_count, model_width) * score_scale
    grad_qkv_low = jnp.concatenate([grad_query, grad_key, grad_value], axis=1).astype(jnp.bfloat16)
    grad_wqkv = contract_rows(normed_one_low, grad_qkv_low)
    grad_normed_one = against_weight(grad_qkv_low, w_qkv)
    _, norm_one_back = jax.vjp(layer_norm, residual, ln1_gain, ln1_bias)
    grad_resid, grad_gain_one, grad_bias_one = norm_one_back(grad_normed_one)
    grad_input = (grad_mixed + grad_resid).astype(jnp.bfloat16)[None]
    (
        fc1_share,
        fc2_share,
        qkv_share,
        proj_share,
        gain_one_share,
        bias_one_share,
        gain_two_share,
        bias_two_share,
    ) = (
        lax.psum_scatter(
            grad_fc1.astype(jnp.bfloat16), "blk", scatter_dimension=0, tiled=True
        ).astype(jnp.float32),
        lax.psum_scatter(
            grad_fc2.astype(jnp.bfloat16), "blk", scatter_dimension=0, tiled=True
        ).astype(jnp.float32),
        lax.psum_scatter(
            grad_wqkv.astype(jnp.bfloat16), "blk", scatter_dimension=0, tiled=True
        ).astype(jnp.float32),
        lax.psum_scatter(
            grad_proj.astype(jnp.bfloat16), "blk", scatter_dimension=0, tiled=True
        ).astype(jnp.float32),
        lax.psum_scatter(
            grad_gain_one.astype(jnp.bfloat16), "blk", scatter_dimension=0, tiled=True
        ).astype(jnp.float32),
        lax.psum_scatter(
            grad_bias_one.astype(jnp.bfloat16), "blk", scatter_dimension=0, tiled=True
        ).astype(jnp.float32),
        lax.psum_scatter(
            grad_gain_two.astype(jnp.bfloat16), "blk", scatter_dimension=0, tiled=True
        ).astype(jnp.float32),
        lax.psum_scatter(
            grad_bias_two.astype(jnp.bfloat16), "blk", scatter_dimension=0, tiled=True
        ).astype(jnp.float32),
    )
    totals = (
        lax.psum(qkv_share.astype(jnp.bfloat16), "dp").astype(jnp.float32),
        lax.psum(proj_share.astype(jnp.bfloat16), "dp").astype(jnp.float32),
        lax.psum(fc1_share.astype(jnp.bfloat16), "dp").astype(jnp.float32),
        lax.psum(fc2_share.astype(jnp.bfloat16), "dp").astype(jnp.float32),
        lax.psum(gain_one_share.astype(jnp.bfloat16), "dp").astype(jnp.float32),
        lax.psum(bias_one_share.astype(jnp.bfloat16), "dp").astype(jnp.float32),
        lax.psum(gain_two_share.astype(jnp.bfloat16), "dp").astype(jnp.float32),
        lax.psum(bias_two_share.astype(jnp.bfloat16), "dp").astype(jnp.float32),
    )
    return (
        output,
        grad_input,
        totals[0],
        totals[1],
        totals[2],
        totals[3],
        totals[4],
        totals[5],
        totals[6],
        totals[7],
    )


MESH = pl.DeviceIdType.MESH
F32 = jnp.float32
BF16 = jnp.bfloat16
RUN_ROWS = 128
HEAD = 64
SKEW = 3


def mm(left, right):
    return lax.dot_general(left, right, (((1,), (0,)), ((), ())), preferred_element_type=F32)


def mm_nt(left, right):
    return lax.dot_general(left, right, (((1,), (1,)), ((), ())), preferred_element_type=F32)


def mm_tn(left, right):
    return lax.dot_general(left, right, (((0,), (0,)), ((), ())), preferred_element_type=F32)


def norm_parts(rows):
    centred = rows - jnp.mean(rows, axis=-1, keepdims=True)
    inv_std = lax.rsqrt(jnp.mean(centred * centred, axis=-1, keepdims=True) + EPSILON)
    return centred * inv_std, inv_std


def norm_back(grad_rows, hat, inv_std, gain):
    grad_hat = grad_rows * gain
    return inv_std * (
        grad_hat
        - jnp.mean(grad_hat, axis=-1, keepdims=True)
        - hat * jnp.mean(grad_hat * hat, axis=-1, keepdims=True)
    )


def gelu_pair(u):
    inner = 0.7978845608028654 * (u + 0.044715 * u * u * u)
    t = jnp.tanh(inner)
    half = 0.5 * (1.0 + t)
    slope = half + 0.5 * u * (1.0 - t * t) * (0.7978845608028654 * (1.0 + 0.134145 * u * u))
    return u * half, slope


def layer_kernel(Z, names, *refs):
    r = dict(zip(names, refs, strict=True))
    z = lax.axis_index("dp")
    b = lax.axis_index("blk")
    e = lax.rem(b, 2)
    chip = b // 2
    cx = lax.rem(chip, 2)
    cy = chip // 2
    scale = HEAD**-0.5

    def chip_at(delta):
        dx, dy = delta % 2, delta // 2
        return 2 * (cy + dy - 2 * cy * dy) + (cx + dx - 2 * cx * dx)

    def dev(delta):
        return (z, 2 * chip_at(delta) + e)

    other = (z, b + 1 - 2 * e)

    def remote(src, dst, send_sem, recv_sem, device):
        sems = [s[0].at[s[1]] if isinstance(s, tuple) else s for s in (send_sem, recv_sem)]
        return pltpu.make_async_remote_copy(
            src_ref=src, dst_ref=dst, send_sem=sems[0], recv_sem=sems[1],
            device_id=device, device_id_type=MESH,
        )

    loads = {}

    def load(name, src, dst):
        loads[name] = pltpu.make_async_copy(src, dst, r["ld_sem"].at[len(loads)])
        loads[name].start()

    load("x", r["x"], r["xb"].at[b])

    bar = pltpu.get_barrier_semaphore()
    for target in (other, dev(1), dev(2), dev(3)):
        pl.semaphore_signal(bar, inc=1, device_id=target, device_id_type=MESH)

    @pl.when(z > 0)
    def _():
        pl.semaphore_signal(bar, inc=1, device_id=(z - 1, b), device_id_type=MESH)

    @pl.when(z < Z - 1)
    def _():
        pl.semaphore_signal(bar, inc=1, device_id=(z + 1, b), device_id_type=MESH)

    pl.semaphore_wait(bar, 4 + jnp.minimum(z, 1) + jnp.minimum(Z - 1 - z, 1))

    class Gather:
        def __init__(self, buf, ss, rs):
            self.buf, self.ss, self.rs = buf, ss, rs

        def slot(self, m):
            return 2 * chip_at(m // 2) + (e if m % 2 == 0 else 1 - e)

        def copy(self, src, at, place, device):
            return remote(src, self.buf.at[at], (self.ss, place), (self.rs, place), device)

        def hop(self, delta, part, src=None):
            rows = pl.ds(64 * part, 64)
            at = (self.slot(2 * delta) if src is None else b, rows)
            return self.copy(self.buf.at[at] if src is None else src.at[rows], at, 2 * delta + part, dev(delta))

        def turn(self, part, delta):
            at = (self.slot(2 * delta), pl.ds(64 * part, 64))
            return self.copy(self.buf.at[at], at, 6 + part, dev(2 - part))

        def core(self, delta, src=None):
            at = self.slot(2 * delta) if src is None else b
            return self.copy(self.buf.at[at] if src is None else src, at, (0, 8, 9)[delta], other)

        def core_half(self, part):
            at = (self.slot(6), pl.ds(64 * part, 64))
            return self.copy(self.buf.at[at], at, 10 + part, other)

        def send(self, src):
            for part in (0, 1):
                self.hop(1, part, src).start()
                self.hop(2, 1 - part, src).start()
            self.core(0, src).start()

        def pass_on(self):
            self.hop(1, 0).wait_recv()
            self.turn(0, 1).start()
            self.hop(2, 1).wait_recv()
            self.turn(1, 2).start()
            self.hop(1, 1).wait_recv()
            self.core(1).start()
            self.hop(2, 0).wait_recv()
            self.core(2).start()

        def pass_diagonal(self):
            for part in (0, 1):
                self.turn(part, 3).wait_recv()
                self.core_half(part).start()

        def wait_core(self, delta):
            at = self.slot(2 * delta + 1)
            if delta < 3:
                self.copy(self.buf.at[at], at, (0, 8, 9)[delta], other).wait_recv()
            else:
                for part in (0, 1):
                    half = (at, pl.ds(64 * part, 64))
                    self.copy(self.buf.at[half], half, 10 + part, other).wait_recv()

        def finish(self, src):
            self.core(0, src).wait_send()
            for part in (0, 1):
                self.hop(1, part, src).wait_send()
                self.hop(2, part, src).wait_send()
                self.turn(part, 1 + part).wait_send()
                self.core(1 + part).wait_send()
                self.core_half(part).wait_send()

    gx = Gather(r["xb"], r["gx_s"], r["gx_r"])
    gdy = Gather(r["dyb"], r["gdy_s"], r["gdy_r"])

    class Chain:
        def __init__(self, name, K, dtype, sink):
            self.K, self.dtype, self.sink = K, dtype, sink
            for part in ("own", "rl", "rr", "tu", "td", "su", "sd", "ru", "rd"):
                setattr(self, part, r[name + "_" + part])

        def up(self, src, k):
            return remote(src, self.rl.at[k], (self.su, k), (self.ru, k), (z + 1, b))

        def down(self, src, k):
            return remote(src, self.rr.at[k], (self.sd, k), (self.rd, k), (z - 1, b))

        def prime(self, k):
            if Z == 1:
                return

            @pl.when(z == 0)
            def _():
                self.up(self.own.at[k], k).start()

            @pl.when(z == Z - 1)
            def _():
                self.down(self.own.at[k], k).start()

        def tick(self, i):
            ku = i - 1 - SKEW * (z - 1)

            @pl.when((z > 0) & (z < Z - 1) & (ku >= 0) & (ku < self.K))
            def _():
                self.up(self.own.at[ku], ku).wait_recv()
                self.tu[ku] = (self.own[ku].astype(F32) + self.rl[ku].astype(F32)).astype(self.dtype)
                self.up(self.tu.at[ku], ku).start()

            kd = i - 1 - SKEW * (Z - 2 - z)

            @pl.when((z > 0) & (z < Z - 1) & (kd >= 0) & (kd < self.K))
            def _():
                self.down(self.own.at[kd], kd).wait_recv()
                self.td[kd] = (self.own[kd].astype(F32) + self.rr[kd].astype(F32)).astype(self.dtype)
                self.down(self.td.at[kd], kd).start()

            k = i - 1 - SKEW * max(Z - 2, 0)
            if 0 <= k < self.K:

                @pl.when(z == 0)
                def _():
                    if Z > 1:
                        self.down(self.own.at[k], k).wait_recv()
                    self.sink(k, self.own[k].astype(F32) + self.rr[k].astype(F32))

                @pl.when((z == Z - 1) & (z > 0))
                def _():
                    self.up(self.own.at[k], k).wait_recv()
                    self.sink(k, self.own[k].astype(F32) + self.rl[k].astype(F32))

                @pl.when((z > 0) & (z < Z - 1))
                def _():
                    self.sink(
                        k,
                        self.own[k].astype(F32) + self.rl[k].astype(F32) + self.rr[k].astype(F32),
                    )

        def finish(self):
            @pl.when(z < Z - 1)
            def _():
                for k in range(self.K):
                    self.up(self.own.at[k], k).wait_send()

            @pl.when(z > 0)
            def _():
                for k in range(self.K):
                    self.down(self.own.at[k], k).wait_send()

    def sink_a(k, total):
        low = total.astype(BF16)
        if k < 8:
            r["o_fc2"][96 * (k // 2) : 96 * (k // 2) + 96, 384 * (k % 2) : 384 * (k % 2) + 384] = low
        else:
            src = chip_at((k - 8) // 2)
            r["o_fc1"][:, pl.ds(pl.multiple_of(768 * src + 384 * (k % 2), 128), 384)] = low

    def sink_b(k, total):
        r["o_qkv"][chip_at(k)] = total.astype(BF16)

    def sink_p(k, total):
        r["o_proj"][:, 384 * k : 384 * k + 384] = total.astype(BF16)

    def sink_c(k, total):
        for i in range(8):
            r["lnc"][i] = total[:, 96 * i : 96 * i + 96]
        r["o_ln"][...] = r["lnc"][b]

    ca = Chain("ca", 16, BF16, sink_a)
    cb = Chain("cb", 4, BF16, sink_b)
    cp = Chain("cp", 2, BF16, sink_p)
    cc = Chain("cc", 1, F32, sink_c)
    line = ((ca, 0), (cb, 16), (cp, 20), (cc, 22))
    beats = [0]

    def beat(count=1):
        for _ in range(count):
            beats[0] += 1
            for chain, first in line:
                if 1 <= beats[0] - first <= chain.K + SKEW * max(Z - 2, 0):
                    chain.tick(beats[0] - first)

    gx.send(r["x"])
    load("w_qkv", r["w_qkv"], r["wq"])
    load("w_proj", r["w_proj"], r["wp"])
    load("dy", r["dy"], r["dyb"].at[b])
    load("w_fc1", r["w_fc1"], r["w1"])
    load("w_fc2", r["w_fc2"], r["w2"])

    crop = [r["crops"][0, RUN_ROWS * i] for i in range(8)]
    places = []
    for i in range(8):
        place = 2 * crop[i]
        for h in range(i):
            place = place + jnp.where(crop[h] == crop[i], 1, 0)
        places.append(place)
        r["inv"][i] = place
    for s in range(8):
        run = jnp.int32(0)
        for i in range(8):
            run = run + jnp.where(places[i] == s, i, 0)
        r["perm"][s] = run

    g1, b1 = r["ln1_gain"][...].reshape(1, 768), r["ln1_bias"][...].reshape(1, 768)
    g2, b2 = r["ln2_gain"][...].reshape(1, 768), r["ln2_bias"][...].reshape(1, 768)

    loads["x"].wait()
    loads["w_qkv"].wait()
    for i in range(4):
        for t in range(3):
            first = 768 * t + 192 * i
            r["wo"][i, :, 128 * t : 128 * t + 128] = r["wq"][:, first : first + 128]
            r["wo"][i, :, 384 + 64 * t : 448 + 64 * t] = r["wq"][:, first + 128 : first + 192]

    def project(delta):
        gx.wait_core(delta)
        pair = pl.ds(2 * chip_at(delta), 2)
        hat, _ = norm_parts(r["xb"][pair].reshape(256, 768).astype(F32))
        normed = (hat * g1 + b1).astype(BF16)
        r["n1"][pair] = normed.reshape(2, 128, 768)
        for t in range(3):
            out = mm(normed, r["wq"][:, pl.ds(pl.multiple_of(768 * t + 384 * e, 128), 384)])
            out = out * scale if t == 0 else out
            r["qkv"][pair, :, 384 * t : 384 * t + 384] = out.astype(BF16).reshape(2, 128, 384)

    project(0)
    gx.pass_on()
    gdy.send(r["dy"])
    project(1)
    project(2)
    gx.pass_diagonal()
    project(3)

    low_lanes = lax.broadcasted_iota(jnp.int32, (1, 128), 1) < HEAD

    def stack(two):
        none = jnp.zeros_like(two)
        return jnp.concatenate([jnp.where(low_lanes, two, none), jnp.where(low_lanes, none, two)], axis=0)

    def o_core(at):
        place = (e, pl.ds(2 * at, 2))
        return remote(r["ob"].at[place], r["ob"].at[place], (r["o_s"], at), (r["o_r"], at), other)

    def attend(at, carry):
        run0, run1 = r["perm"][2 * at], r["perm"][2 * at + 1]
        outs = []
        for h in range(3):
            q, k, v = [
                jnp.concatenate(
                    [r["qkv"][run, :, 384 * t + 128 * h : 384 * t + 128 * h + 128] for run in (run0, run1)],
                    axis=0,
                )
                for t in range(3)
            ]
            s = mm_nt(stack(q), k)
            p = jnp.exp(s - jnp.max(s, axis=-1, keepdims=True))
            o = mm(p.astype(BF16), jnp.concatenate([v, jnp.ones_like(v)], axis=1))
            o = o[:, 0:128] / o[:, 128:256]
            outs.append(jnp.where(low_lanes, o[0:256], o[256:512]))
        low = jnp.concatenate(outs, axis=1).astype(BF16)
        r["ob"][e, pl.ds(2 * at, 2)] = low.reshape(2, 128, 384)
        o_core(at).start()
        return carry

    def by_perm(buf, first, count):
        return jnp.concatenate([buf[r["perm"][first + i]] for i in range(count)], axis=0)

    own_hidden = pl.ds(pl.multiple_of(384 * b, 128), 384)

    def feed(at):
        place = (1 - e, pl.ds(2 * at, 2))
        remote(r["ob"].at[place], r["ob"].at[place], (r["o_s"], at), (r["o_r"], at), other).wait_recv()
        pair = pl.ds(2 * at, 2)
        o = jnp.concatenate([r["ob"][i, pair].reshape(256, 384) for i in range(2)], axis=1)
        x1 = by_perm(r["xb"], 2 * at, 2).astype(F32) + mm(o, r["wp"][...])
        r["x1"][pair] = x1.reshape(2, 128, 768)
        hat, _ = norm_parts(x1)
        n2 = (hat * g2 + b2).astype(BF16)
        r["n2"][pair] = n2.reshape(2, 128, 768)
        u = mm(n2, r["w1"][:, own_hidden])
        r["u"][pair] = u.reshape(2, 128, 384)
        r["act"][pair] = gelu_pair(u)[0].astype(BF16).reshape(2, 128, 384)

    attend(0, 0)
    attend(1, 0)
    for name in ("w_proj", "w_fc1", "w_fc2", "dy"):
        loads[name].wait()
    gdy.pass_on()
    feed(0)
    attend(2, 0)
    feed(1)
    attend(3, 0)
    gdy.pass_diagonal()
    feed(2)
    for delta in range(4):
        gdy.wait_core(delta)
    feed(3)

    grad = mm_tn(r["act"][...].reshape(1024, 384), by_perm(r["dyb"], 0, 8)).astype(BF16)
    for k in range(8):
        ca.own[k] = grad[96 * (k // 2) : 96 * (k // 2) + 96, 384 * (k % 2) : 384 * (k % 2) + 384]
        ca.prime(k)

    place_own = r["inv"][b]
    dy_own = r["dyb"][b]
    r["y"][...] = r["x1"][place_own]
    r["dn2"][...] = jnp.zeros((128, 768), F32)

    def own_rows(i, carry):
        part = pl.ds(768 * i, 768)
        act, slope = gelu_pair(mm(r["n2"][place_own], r["w1"][:, part]))
        du = (mm_nt(r["dyb"][b], r["w2"][part]) * slope).astype(BF16)
        r["dn2"][...] += mm_nt(du, r["w1"][:, part])
        r["y"][...] += mm(act.astype(BF16), r["w2"][part])
        return carry

    for i in range(4):
        own_rows(i, 0)
        if i == 3:
            beat()
    r["o_y"][...] = r["y"][...].astype(BF16)

    dn2 = r["dn2"][...]
    hat, inv_std = norm_parts(r["x1"][place_own])
    r["lnp"][2:3] = jnp.sum(dn2 * hat, axis=0, keepdims=True)
    r["lnp"][3:4] = jnp.sum(dn2, axis=0, keepdims=True)
    dx1 = dy_own.astype(F32) + norm_back(dn2, hat, inv_std, g2)
    r["dx1"][...] = dx1
    low = dx1.astype(BF16)
    do = mm_nt(low, r["wp"][...]).astype(BF16)
    for i in range(4):
        r["dos"][i] = do[:, 192 * i : 192 * i + 192]

    def do_send(delta):
        return remote(r["dos"].at[chip_at(delta)], r["dob"].at[b], (r["do_s"], 2 * delta), (r["do_r"], 2 * delta), dev(delta))

    def do_slot(m):
        return 2 * chip_at(m // 2) + (e if m % 2 == 0 else 1 - e)

    def do_core(delta):
        src = r["dos"].at[chip] if delta == 0 else r["dob"].at[do_slot(2 * delta)]
        return remote(src, r["dob"].at[do_slot(2 * delta)], (r["do_s"], 2 * delta + 1), (r["do_r"], 2 * delta + 1), other)

    for delta in (3, 2, 1):
        do_send(delta).start()
    do_core(0).start()
    r["dob"][b] = r["dos"][chip]
    beat()

    def back_hidden(c, carry):
        pair = pl.ds(2 * c, 2)
        da = mm_nt(by_perm(r["dyb"], 2 * c, 2), r["w2"][own_hidden])
        slope = gelu_pair(r["u"][pair].reshape(256, 384))[1]
        r["du"][pair] = (da * slope).astype(BF16).reshape(2, 128, 384)
        return carry

    for c in range(4):
        back_hidden(c, 0)
    beat()
    grad = mm_tn(r["n2"][...].reshape(1024, 768), r["du"][...].reshape(1024, 384)).astype(BF16)
    for i in range(8):
        r["t1"][i % 2, i // 2] = grad[96 * i : 96 * i + 96]
    t1_core = remote(r["t1"].at[1 - e], r["t1x"], r["t1_cs"], r["t1_cr"], other)
    t1_core.start()
    beat()

    def t1_send(delta, half):
        src = r["t1"].at[e, chip_at(delta)] if half == 0 else r["t1x"].at[chip_at(delta)]
        hidden_core = e if half == 0 else 1 - e
        at = 2 * delta + half
        return remote(src, ca.own.at[8 + 2 * delta + hidden_core], (r["t1_s"], at), (r["t1_r"], at), dev(delta))

    o = jnp.concatenate([r["ob"][i, place_own] for i in range(2)], axis=1)
    grad = mm_tn(o, low).astype(BF16)
    for i in range(8):
        r["tp"][i % 2, i // 2] = grad[96 * i : 96 * i + 96]
    tp_core = remote(r["tp"].at[1 - e], r["tpx"], r["tp_cs"], r["tp_cr"], other)
    tp_core.start()

    def tp_send(delta):
        return remote(r["tps"].at[delta], r["tpr"].at[delta], (r["tp_s"], delta), (r["tp_r"], delta), dev(delta))

    t1_core.wait_recv()
    for delta in (1, 2, 3):
        for half in (0, 1):
            t1_send(delta, half).start()
    ca.own[8 + e] = r["t1"][e, chip]
    ca.own[9 - e] = r["t1x"][chip]
    ca.prime(8)
    ca.prime(9)
    beat()

    for s in range(4):
        r["n1s"][s] = r["n1"][r["perm"][4 * e + s]]
    r["qo"][...] = mm(r["n1s"][...].reshape(512, 768), r["wo"][chip]).astype(BF16).reshape(2, 256, 576)

    for delta in (1, 2, 3):
        do_send(delta).wait_recv()
        do_core(delta).start()
    for delta in range(4):
        at = do_slot(2 * delta + 1)
        remote(r["dob"].at[at], r["dob"].at[at], (r["do_s"], 2 * delta + 1), (r["do_r"], 2 * delta + 1), other).wait_recv()

    beat()

    def attend_back(at, heads):
        runs = [r["perm"][4 * e + 2 * at + i] for i in range(2)]
        if heads == 2:
            g = jnp.concatenate([r["dob"][run, :, 0:128] for run in runs], axis=0)
            q, k, v = [r["qo"][at, :, 128 * t : 128 * t + 128] for t in range(3)]
            q, g = stack(q), stack(g)
        else:
            g = jnp.concatenate([r["dob"][run, :, 128:192] for run in runs], axis=0)
            q, k, v = [r["qo"][at, :, 384 + 64 * t : 448 + 64 * t] for t in range(3)]
        q = (q.astype(F32) * scale).astype(BF16)
        s = mm_nt(q, k)
        p = jnp.exp(s - jnp.max(s, axis=-1, keepdims=True))
        p = p / jnp.sum(p, axis=-1, keepdims=True)
        dp = mm_nt(g, v)
        ds = (p * (dp - jnp.sum(p * dp, axis=-1, keepdims=True))).astype(BF16)
        dq = mm(ds, k) * scale
        dk = mm_tn(ds, q)
        dv = mm_tn(p.astype(BF16), g)
        mine = pl.ds(2 * (2 * e + at), 2)
        if heads == 2:
            dq = jnp.where(low_lanes, dq[0:256], dq[256:512])
        first, wide = (0, 128) if heads == 2 else (384, 64)
        for t, part in enumerate((dq, dk, dv)):
            r["dq"][mine, :, first + wide * t : first + wide * t + wide] = part.astype(BF16).reshape(2, 128, wide)

    attend_back(0, 2)
    beat()
    attend_back(0, 1)
    beat()
    attend_back(1, 2)
    beat()
    attend_back(1, 1)

    dq_core = remote(r["dq"].at[pl.ds(4 * e, 4)], r["dq"].at[pl.ds(4 * e, 4)], r["dq_cs"], r["dq_cr"], other)
    dq_core.start()
    grad = mm_tn(r["n1s"][...].reshape(512, 768), r["dq"][pl.ds(4 * e, 4)].reshape(512, 576))
    for i in range(8):
        r["tq"][i % 2, i // 2] = grad[96 * i : 96 * i + 96].astype(BF16)
    tq_core = remote(r["tq"].at[1 - e], r["tqx"], r["tq_cs"], r["tq_cr"], other)
    tq_core.start()

    def tq_send(delta):
        return remote(r["tqs"].at[delta], cb.own.at[delta], (r["tq_s"], delta), (r["tq_r"], delta), dev(delta))

    def dq_send(delta):
        return remote(r["dqs"].at[delta], r["dqr"].at[delta], (r["dq_s"], delta), (r["dq_r"], delta), dev(delta))

    beat()

    def t1_arrive(delta):
        for half in (0, 1):
            t1_send(delta, half).wait_recv()
        ca.prime(8 + 2 * delta)
        ca.prime(9 + 2 * delta)

    t1_arrive(1)
    tq_core.wait_recv()
    for delta in (3, 2, 1, 0):
        c = chip_at(delta)
        total = (r["tq"][e, c].astype(F32) + r["tqx"][c].astype(F32)).astype(BF16)
        if delta == 0:
            cb.own[0] = total
        else:
            r["tqs"][delta] = total
            tq_send(delta).start()
    beat()
    at = pl.ds(4 - 4 * e, 4)
    remote(r["dq"].at[at], r["dq"].at[at], r["dq_cs"], r["dq_cr"], other).wait_recv()
    for delta in (3, 2, 1):
        r["dqs"][delta] = r["dq"][r["inv"][2 * chip_at(delta) + e]]
        dq_send(delta).start()
    tp_core.wait_recv()
    for delta in (3, 2, 1, 0):
        c = chip_at(delta)
        r["tps"][delta] = (r["tp"][e, c].astype(F32) + r["tpx"][c].astype(F32)).astype(BF16)
        if delta > 0:
            tp_send(delta).start()

    def beat_to(count):
        beat(count - beats[0])

    t1_arrive(2)
    beat_to(13)
    t1_arrive(3)
    cb.prime(0)
    beat_to(15)
    for delta in (1, 2, 3):
        tq_send(delta).wait_recv()
        cb.prime(delta)
    beat_to(18)
    dn1 = mm_nt(r["dq"][r["inv"][b]], r["wo"][chip])
    for delta in (1, 2, 3):
        dq_send(delta).wait_recv()
        dn1 += mm_nt(r["dqr"][delta], r["wo"][chip_at(delta)])
    hat, inv_std = norm_parts(r["xb"][b].astype(F32))
    r["lnp"][0:1] = jnp.sum(dn1 * hat, axis=0, keepdims=True)
    r["lnp"][1:2] = jnp.sum(dn1, axis=0, keepdims=True)
    r["lnp"][4:8] = jnp.zeros((4, 768), F32)
    r["o_gin"][...] = (r["dx1"][...] + norm_back(dn1, hat, inv_std, g1)).astype(BF16)
    ln_core = remote(r["lnp"], r["lnx"].at[0], (r["ln_s"], 0), (r["ln_r"], 0), other)
    ln_core.start()
    beat_to(19)
    ln_core.wait_recv()
    r["lns"][...] = r["lnp"][...] + r["lnx"][0]

    def ln_send(delta):
        return remote(r["lns"], r["lnx"].at[delta], (r["ln_s"], delta), (r["ln_r"], delta), dev(delta))

    for delta in (3, 2, 1):
        ln_send(delta).start()
    total = r["tps"][0].astype(F32)
    for delta in (1, 2, 3):
        tp_send(delta).wait_recv()
        total += r["tpr"][delta].astype(F32)
    for k in range(2):
        cp.own[k] = total[:, 384 * k : 384 * k + 384].astype(BF16)
        cp.prime(k)
    beat_to(20)
    total = r["lns"][...]
    for delta in (1, 2, 3):
        ln_send(delta).wait_recv()
        total += r["lnx"][delta]
    cc.own[0] = total
    cc.prime(0)
    beat_to(23 + SKEW * max(Z - 2, 0))

    gx.finish(r["x"])
    gdy.finish(r["dy"])
    for at in range(4):
        o_core(at).wait_send()
    for copy in (t1_core, tp_core, tq_core, dq_core, ln_core, do_core(0)):
        copy.wait_send()
    for delta in (1, 2, 3):
        do_send(delta).wait_send()
        do_core(delta).wait_send()
        t1_send(delta, 0).wait_send()
        t1_send(delta, 1).wait_send()
        tp_send(delta).wait_send()
        tq_send(delta).wait_send()
        dq_send(delta).wait_send()
        ln_send(delta).wait_send()
    ca.finish()
    cb.finish()
    cp.finish()
    cc.finish()


def widen_kernel(*refs):
    sources, results, held, wide = refs[:7], refs[7:17], refs[17:24], refs[24:32]
    sem_in, sem_out = refs[32:]
    order = (4, 5, 2, 3, 6, 0, 1)
    copies = {i: pltpu.make_async_copy(sources[i], held[i], sem_in.at[i]) for i in order}
    for copy in copies.values():
        copy.start()
    leaving = []

    def leave(src, at):
        copy = pltpu.make_async_copy(src, results[at], sem_out.at[at])
        copy.start()
        leaving.append(copy)

    for i in order:
        copies[i].wait()
        part = held[i]
        if i < 2:
            leave(part, i)
        elif i == 2:
            for t in range(3):
                parts = []
                for c in range(4):
                    parts.append(part[c, :, 128 * t : 128 * t + 128])
                    parts.append(part[c, :, 384 + 64 * t : 448 + 64 * t])
                wide[0][:, 768 * t : 768 * t + 768] = jnp.concatenate(parts, axis=1).astype(F32)
            leave(wide[0], 2)
        elif i < 6:
            wide[i - 2][...] = part[...].astype(F32)
            leave(wide[i - 2], i)
        else:
            for t in range(4):
                wide[4 + t][...] = part[t, :]
                leave(wide[4 + t], 6 + t)
    for copy in leaving:
        copy.wait()


def fast_shards(
    Z, inputs, crops, ln1_gain, ln1_bias, w_qkv, w_proj, ln2_gain, ln2_bias, w_fc1, w_fc2, cotangent
):
    V, D = pltpu.VMEM, pltpu.SemaphoreType.DMA
    anyspace = pl.BlockSpec(memory_space=pl.ANY)
    vmem = pl.BlockSpec(memory_space=pltpu.VMEM)
    smem = pl.BlockSpec(memory_space=pltpu.SMEM)
    arguments = dict(
        x=(inputs[0], anyspace),
        crops=(crops, smem),
        ln1_gain=(ln1_gain, vmem),
        ln1_bias=(ln1_bias, vmem),
        w_qkv=(w_qkv, anyspace),
        w_proj=(w_proj, anyspace),
        ln2_gain=(ln2_gain, vmem),
        ln2_bias=(ln2_bias, vmem),
        w_fc1=(w_fc1, anyspace),
        w_fc2=(w_fc2, anyspace),
        dy=(cotangent[0], anyspace),
    )
    results = dict(
        o_y=((128, 768), BF16),
        o_gin=((128, 768), BF16),
        o_qkv=((4, 96, 576), BF16),
        o_proj=((96, 768), BF16),
        o_fc1=((96, 3072), BF16),
        o_fc2=((384, 768), BF16),
        o_ln=((8, 96), F32),
    )
    scratch = dict(
        ld_sem=D((6,)),
        perm=pltpu.SMEM((8,), jnp.int32),
        inv=pltpu.SMEM((8,), jnp.int32),
        xb=V((8, 128, 768), BF16), gx_s=D((12,)), gx_r=D((12,)),
        dyb=V((8, 128, 768), BF16), gdy_s=D((12,)), gdy_r=D((12,)),
        dob=V((8, 128, 192), BF16), dos=V((4, 128, 192), BF16), do_s=D((8,)), do_r=D((8,)),
        wq=V((768, 2304), BF16), wo=V((4, 768, 576), BF16), wp=V((768, 768), BF16),
        w1=V((768, 3072), BF16), w2=V((3072, 768), BF16),
        n1=V((8, 128, 768), BF16), n1s=V((4, 128, 768), BF16), qkv=V((8, 128, 1152), BF16),
        ob=V((2, 8, 128, 384), BF16), o_s=D((4,)), o_r=D((4,)),
        x1=V((8, 128, 768), F32), n2=V((8, 128, 768), BF16),
        act=V((8, 128, 384), BF16), u=V((8, 128, 384), F32), du=V((8, 128, 384), BF16),
        y=V((128, 768), F32), dn2=V((128, 768), F32), dx1=V((128, 768), F32),
        t1=V((2, 4, 96, 384), BF16), t1x=V((4, 96, 384), BF16),
        t1_cs=D, t1_cr=D, t1_s=D((8,)), t1_r=D((8,)),
        tp=V((2, 4, 96, 768), BF16), tpx=V((4, 96, 768), BF16), tps=V((4, 96, 768), BF16), tpr=V((4, 96, 768), BF16),
        tp_cs=D, tp_cr=D, tp_s=D((4,)), tp_r=D((4,)),
        qo=V((2, 256, 576), BF16), dq=V((8, 128, 576), BF16),
        tq=V((2, 4, 96, 576), BF16), tqx=V((4, 96, 576), BF16), tqs=V((4, 96, 576), BF16),
        tq_cs=D, tq_cr=D, tq_s=D((4,)), tq_r=D((4,)),
        dqs=V((4, 128, 576), BF16), dqr=V((4, 128, 576), BF16),
        dq_cs=D, dq_cr=D, dq_s=D((4,)), dq_r=D((4,)),
        lnp=V((8, 768), F32), lns=V((8, 768), F32), lnx=V((4, 8, 768), F32), lnc=V((8, 8, 96), F32),
        ln_s=D((4,)), ln_r=D((4,)),
    )
    for name, K, shape, dtype in (
        ("ca", 16, (96, 384), BF16), ("cb", 4, (96, 576), BF16), ("cp", 2, (96, 384), BF16), ("cc", 1, (8, 768), F32)
    ):
        for part in ("own", "rl", "rr", "tu", "td"):
            scratch[name + "_" + part] = V((K, *shape), dtype)
        for part in ("su", "sd", "ru", "rd"):
            scratch[name + "_" + part] = D((K,))
    names = (*arguments, *results, *scratch)
    narrow = pl.pallas_call(
        functools.partial(layer_kernel, Z, names),
        out_shape=[jax.ShapeDtypeStruct(*shape) for shape in results.values()],
        in_specs=[spec for _, spec in arguments.values()],
        out_specs=[vmem] * len(results),
        scratch_shapes=list(scratch.values()),
        compiler_params=pltpu.CompilerParams(
            collective_id=0, has_side_effects=True, vmem_limit_bytes=60 * 2**20
        ),
    )(*[array for array, _ in arguments.values()])
    wide = [((128, 768), BF16), ((128, 768), BF16), ((96, 2304), F32), ((96, 768), F32), ((96, 3072), F32), ((384, 768), F32)]
    wide += [((96,), F32)] * 4
    y, gin, *grads = pl.pallas_call(
        widen_kernel,
        out_shape=[jax.ShapeDtypeStruct(*shape) for shape in wide],
        in_specs=[anyspace] * len(narrow),
        out_specs=[anyspace] * len(wide),
        scratch_shapes=[V(*shape) for shape in results.values()]
        + [V(*shape) for shape in wide[2:6]]
        + [V((96,), F32)] * 4
        + [D((len(narrow),)), D((len(wide),))],
        compiler_params=pltpu.CompilerParams(vmem_limit_bytes=62 * 2**20),
    )(*narrow)
    return (y[None], gin[None], *grads)


def solution(mesh):
    placed = (
        P("dp", "blk", None),
        P("dp", None),
        P(),
        P(),
        P(),
        P(),
        P(),
        P(),
        P(),
        P(),
        P("dp", "blk", None),
    )
    def whole(*arrays):
        one_run = arrays[0].shape[1] == 8 * RUN_ROWS and mesh.shape["blk"] == 8
        body = functools.partial(fast_shards, mesh.shape["dp"]) if one_run else shards
        return placed_call(body)(*arrays)

    placed_call = lambda body: jax.shard_map(
        body,
        mesh=mesh,
        in_specs=placed,
        out_specs=(
            P("dp", "blk", None),
            P("dp", "blk", None),
            P("blk", None),
            P("blk", None),
            P("blk", None),
            P("blk", None),
            P("blk"),
            P("blk"),
            P("blk"),
            P("blk"),
        ),
        check_vma=False,
    )
    return whole
```

```python
import functools
import math

import jax
import jax.numpy as jnp
from jax import lax
from jax.experimental import pallas as pl
from jax.experimental.pallas import tpu as pltpu
from jax.sharding import PartitionSpec as P

HEADS = 12


EPSILON = 1e-05
MASKED = -1e30


def layer_norm(values_in, gain_in, shift_in):
    row_mean = jnp.mean(values_in, axis=-1, keepdims=True)
    centred = values_in - row_mean
    row_var = jnp.mean(centred * centred, axis=-1, keepdims=True)
    return centred * lax.rsqrt(row_var + EPSILON) * gain_in + shift_in


def contract_rows(left_side, right_side):
    return lax.dot_general(
        left_side, right_side, (((0,), (0,)), ((), ())), preferred_element_type=jnp.float32
    )


def against_weight(grad_rows, weight_mat):
    return lax.dot_general(
        grad_rows, weight_mat, (((1,), (1,)), ((), ())), preferred_element_type=jnp.float32
    )


def head_view(matrix, head_count):
    return matrix.reshape(matrix.shape[0], head_count, matrix.shape[1] // head_count)


def scores_of(query_heads, key_heads, score_scale):
    return (
        jnp.einsum("qhd,khd->hqk", query_heads, key_heads, preferred_element_type=jnp.float32)
        * score_scale
    )


def weights_of(scores, visible, logsum):
    return jnp.where(visible[None], jnp.exp(scores - logsum[:, :, None]), 0.0)


def shards(
    inputs, crops, ln1_gain, ln1_bias, w_qkv, w_proj, ln2_gain, ln2_bias, w_fc1, w_fc2, cotangent
):
    row_count = inputs.shape[1]
    model_width = inputs.shape[2]
    head_count = HEADS
    score_scale = 1.0 / math.sqrt(model_width // head_count)
    seq_crops = crops[0]
    seq_len = seq_crops.shape[0]
    key_block = min(1024, seq_len)
    block_count = seq_len // key_block
    block_ids = jnp.arange(block_count)
    own_crops = lax.dynamic_slice_in_dim(seq_crops, lax.axis_index("blk") * row_count, row_count, 0)
    residual = inputs[0].astype(jnp.float32)
    normed_one_low = layer_norm(residual, ln1_gain, ln1_bias).astype(jnp.bfloat16)
    qkv_low = jnp.dot(normed_one_low, w_qkv, preferred_element_type=jnp.float32).astype(
        jnp.bfloat16
    )
    query_own = qkv_low[:, :model_width]
    key_own = qkv_low[:, model_width : 2 * model_width]
    value_own = qkv_low[:, 2 * model_width :]
    keys_all, values_all = (
        lax.all_gather(key_own, "blk", axis=0, tiled=True),
        lax.all_gather(value_own, "blk", axis=0, tiled=True),
    )
    query_heads = head_view(query_own, head_count)

    def block_inputs(block_index):
        key_heads = head_view(
            lax.dynamic_slice_in_dim(keys_all, block_index * key_block, key_block, 0), head_count
        )
        value_heads = head_view(
            lax.dynamic_slice_in_dim(values_all, block_index * key_block, key_block, 0), head_count
        )
        crop_block = lax.dynamic_slice_in_dim(seq_crops, block_index * key_block, key_block, 0)
        visible = own_crops[:, None] == crop_block[None, :]
        return (key_heads, value_heads, visible)

    def stats_step(carried, block_index):
        old_max, summed = carried
        key_heads, value_heads, visible = block_inputs(block_index)
        scores = jnp.where(visible[None], scores_of(query_heads, key_heads, score_scale), MASKED)
        new_max = jnp.maximum(old_max, jnp.max(scores, axis=-1))
        exp_terms = jnp.where(visible[None], jnp.exp(scores - new_max[:, :, None]), 0.0)
        return ((new_max, summed * jnp.exp(old_max - new_max) + jnp.sum(exp_terms, axis=-1)), None)

    start_max = jnp.full((head_count, row_count), MASKED, jnp.float32)
    start_sum = jnp.zeros((head_count, row_count), jnp.float32)
    (row_max, summed), _ = lax.scan(stats_step, (start_max, start_sum), block_ids)
    logsum = row_max + jnp.log(summed)

    def output_step(running, block_index):
        key_heads, value_heads, visible = block_inputs(block_index)
        attn_probs = weights_of(
            scores_of(query_heads, key_heads, score_scale), visible, logsum
        ).astype(jnp.bfloat16)
        return (
            running
            + jnp.einsum(
                "hqk,khd->qhd", attn_probs, value_heads, preferred_element_type=jnp.float32
            ),
            None,
        )

    attended, _ = lax.scan(output_step, jnp.zeros(query_heads.shape, jnp.float32), block_ids)
    attended_low = attended.reshape(row_count, model_width).astype(jnp.bfloat16)
    mixed_rows = residual + jnp.dot(attended_low, w_proj, preferred_element_type=jnp.float32)
    normed_two_low = layer_norm(mixed_rows, ln2_gain, ln2_bias).astype(jnp.bfloat16)
    hidden_pre = jnp.dot(normed_two_low, w_fc1, preferred_element_type=jnp.float32)
    active, gelu_back = jax.vjp(jax.nn.gelu, hidden_pre)
    active_low = active.astype(jnp.bfloat16)
    result = mixed_rows + jnp.dot(active_low, w_fc2, preferred_element_type=jnp.float32)
    output = result.astype(jnp.bfloat16)[None]
    grad_out_low = cotangent[0]
    grad_fc2 = contract_rows(active_low, grad_out_low)
    grad_active = against_weight(grad_out_low, w_fc2)
    grad_hidden_low = gelu_back(grad_active)[0].astype(jnp.bfloat16)
    grad_fc1 = contract_rows(normed_two_low, grad_hidden_low)
    grad_normed_two = against_weight(grad_hidden_low, w_fc1)
    _, norm_two_back = jax.vjp(layer_norm, mixed_rows, ln2_gain, ln2_bias)
    grad_mixed_part, grad_gain_two, grad_bias_two = norm_two_back(grad_normed_two)
    grad_mixed = grad_out_low.astype(jnp.float32) + grad_mixed_part
    grad_mixed_low = grad_mixed.astype(jnp.bfloat16)
    grad_proj = contract_rows(attended_low, grad_mixed_low)
    grad_attended_low = against_weight(grad_mixed_low, w_proj).astype(jnp.bfloat16)
    grad_heads = head_view(grad_attended_low, head_count)

    def delta_step(running, block_index):
        key_heads, value_heads, visible = block_inputs(block_index)
        attn_probs = weights_of(scores_of(query_heads, key_heads, score_scale), visible, logsum)
        grad_probs = jnp.einsum(
            "qhd,khd->hqk", grad_heads, value_heads, preferred_element_type=jnp.float32
        )
        return (running + jnp.sum(attn_probs * grad_probs, axis=-1), None)

    row_delta, _ = lax.scan(delta_step, jnp.zeros((head_count, row_count), jnp.float32), block_ids)

    def score_grads(
        query_part, grad_part, logsum_part, delta_part, key_heads, value_heads, visible
    ):
        attn_probs = weights_of(scores_of(query_part, key_heads, score_scale), visible, logsum_part)
        grad_probs = jnp.einsum(
            "qhd,khd->hqk", grad_part, value_heads, preferred_element_type=jnp.float32
        )
        grad_scores = (attn_probs * (grad_probs - delta_part[:, :, None])).astype(jnp.bfloat16)
        return (attn_probs, grad_scores)

    def pair_step(running, block_index):
        key_heads, value_heads, visible = block_inputs(block_index)
        attn_probs, grad_scores = score_grads(
            query_heads, grad_heads, logsum, row_delta, key_heads, value_heads, visible
        )
        key_term = (
            jnp.einsum("hqk,qhd->khd", grad_scores, query_heads, preferred_element_type=jnp.float32)
            * score_scale
        )
        value_term = jnp.einsum(
            "hqk,qhd->khd",
            attn_probs.astype(jnp.bfloat16),
            grad_heads,
            preferred_element_type=jnp.float32,
        )
        joined = jnp.concatenate(
            [key_term.reshape(key_block, model_width), value_term.reshape(key_block, model_width)],
            axis=1,
        )
        step_query = jnp.einsum(
            "hqk,khd->qhd", grad_scores, key_heads, preferred_element_type=jnp.float32
        )
        return (running + step_query, joined)

    grad_query, key_terms = lax.scan(
        pair_step, jnp.zeros(query_heads.shape, jnp.float32), block_ids
    )
    key_sums = lax.psum_scatter(
        key_terms.reshape(seq_len, 2 * model_width).astype(jnp.bfloat16),
        "blk",
        scatter_dimension=0,
        tiled=True,
    ).astype(jnp.float32)
    grad_key = key_sums[:, :model_width]
    grad_value = key_sums[:, model_width:]
    grad_query = grad_query.reshape(row_count, model_width) * score_scale
    grad_qkv_low = jnp.concatenate([grad_query, grad_key, grad_value], axis=1).astype(jnp.bfloat16)
    grad_wqkv = contract_rows(normed_one_low, grad_qkv_low)
    grad_normed_one = against_weight(grad_qkv_low, w_qkv)
    _, norm_one_back = jax.vjp(layer_norm, residual, ln1_gain, ln1_bias)
    grad_resid, grad_gain_one, grad_bias_one = norm_one_back(grad_normed_one)
    grad_input = (grad_mixed + grad_resid).astype(jnp.bfloat16)[None]
    (
        fc1_share,
        fc2_share,
        qkv_share,
        proj_share,
        gain_one_share,
        bias_one_share,
        gain_two_share,
        bias_two_share,
    ) = (
        lax.psum_scatter(
            grad_fc1.astype(jnp.bfloat16), "blk", scatter_dimension=0, tiled=True
        ).astype(jnp.float32),
        lax.psum_scatter(
            grad_fc2.astype(jnp.bfloat16), "blk", scatter_dimension=0, tiled=True
        ).astype(jnp.float32),
        lax.psum_scatter(
            grad_wqkv.astype(jnp.bfloat16), "blk", scatter_dimension=0, tiled=True
        ).astype(jnp.float32),
        lax.psum_scatter(
            grad_proj.astype(jnp.bfloat16), "blk", scatter_dimension=0, tiled=True
        ).astype(jnp.float32),
        lax.psum_scatter(
            grad_gain_one.astype(jnp.bfloat16), "blk", scatter_dimension=0, tiled=True
        ).astype(jnp.float32),
        lax.psum_scatter(
            grad_bias_one.astype(jnp.bfloat16), "blk", scatter_dimension=0, tiled=True
        ).astype(jnp.float32),
        lax.psum_scatter(
            grad_gain_two.astype(jnp.bfloat16), "blk", scatter_dimension=0, tiled=True
        ).astype(jnp.float32),
        lax.psum_scatter(
            grad_bias_two.astype(jnp.bfloat16), "blk", scatter_dimension=0, tiled=True
        ).astype(jnp.float32),
    )
    totals = (
        lax.psum(qkv_share.astype(jnp.bfloat16), "dp").astype(jnp.float32),
        lax.psum(proj_share.astype(jnp.bfloat16), "dp").astype(jnp.float32),
        lax.psum(fc1_share.astype(jnp.bfloat16), "dp").astype(jnp.float32),
        lax.psum(fc2_share.astype(jnp.bfloat16), "dp").astype(jnp.float32),
        lax.psum(gain_one_share.astype(jnp.bfloat16), "dp").astype(jnp.float32),
        lax.psum(bias_one_share.astype(jnp.bfloat16), "dp").astype(jnp.float32),
        lax.psum(gain_two_share.astype(jnp.bfloat16), "dp").astype(jnp.float32),
        lax.psum(bias_two_share.astype(jnp.bfloat16), "dp").astype(jnp.float32),
    )
    return (
        output,
        grad_input,
        totals[0],
        totals[1],
        totals[2],
        totals[3],
        totals[4],
        totals[5],
        totals[6],
        totals[7],
    )


MESH = pl.DeviceIdType.MESH
F32 = jnp.float32
BF16 = jnp.bfloat16
RUN_ROWS = 128
HEAD = 64
SKEW = 2


def mm(left, right):
    return lax.dot_general(left, right, (((1,), (0,)), ((), ())), preferred_element_type=F32)


def mm_nt(left, right):
    return lax.dot_general(left, right, (((1,), (1,)), ((), ())), preferred_element_type=F32)


def mm_tn(left, right):
    return lax.dot_general(left, right, (((0,), (0,)), ((), ())), preferred_element_type=F32)


def norm_parts(rows):
    centred = rows - jnp.mean(rows, axis=-1, keepdims=True)
    inv_std = lax.rsqrt(jnp.mean(centred * centred, axis=-1, keepdims=True) + EPSILON)
    return centred * inv_std, inv_std


def norm_back(grad_rows, hat, inv_std, gain):
    grad_hat = grad_rows * gain
    return inv_std * (
        grad_hat
        - jnp.mean(grad_hat, axis=-1, keepdims=True)
        - hat * jnp.mean(grad_hat * hat, axis=-1, keepdims=True)
    )


def gelu_pair(u):
    inner = 0.7978845608028654 * (u + 0.044715 * u * u * u)
    t = jnp.tanh(inner)
    half = 0.5 * (1.0 + t)
    slope = half + 0.5 * u * (1.0 - t * t) * (0.7978845608028654 * (1.0 + 0.134145 * u * u))
    return u * half, slope


def layer_kernel(Z, names, *refs):
    r = dict(zip(names, refs, strict=True))
    z = lax.axis_index("dp")
    b = lax.axis_index("blk")
    e = lax.rem(b, 2)
    chip = b // 2
    cx = lax.rem(chip, 2)
    cy = chip // 2
    scale = HEAD**-0.5

    def chip_at(delta):
        dx, dy = delta % 2, delta // 2
        return 2 * (cy + dy - 2 * cy * dy) + (cx + dx - 2 * cx * dx)

    def dev(delta):
        return (z, 2 * chip_at(delta) + e)

    other = (z, b + 1 - 2 * e)

    def remote(src, dst, send_sem, recv_sem, device):
        sems = [s[0].at[s[1]] if isinstance(s, tuple) else s for s in (send_sem, recv_sem)]
        return pltpu.make_async_remote_copy(
            src_ref=src, dst_ref=dst, send_sem=sems[0], recv_sem=sems[1],
            device_id=device, device_id_type=MESH,
        )

    loads = {}

    def load(name, src, dst):
        loads[name] = pltpu.make_async_copy(src, dst, r["ld_sem"].at[len(loads)])
        loads[name].start()

    load("x", r["x"], r["xb"].at[b])

    bar = pltpu.get_barrier_semaphore()
    for target in (other, dev(1), dev(2), dev(3)):
        pl.semaphore_signal(bar, inc=1, device_id=target, device_id_type=MESH)

    @pl.when(z > 0)
    def _():
        pl.semaphore_signal(bar, inc=1, device_id=(z - 1, b), device_id_type=MESH)

    @pl.when(z < Z - 1)
    def _():
        pl.semaphore_signal(bar, inc=1, device_id=(z + 1, b), device_id_type=MESH)

    pl.semaphore_wait(bar, 4 + jnp.minimum(z, 1) + jnp.minimum(Z - 1 - z, 1))

    class Gather:
        def __init__(self, buf, ss, rs):
            self.buf, self.ss, self.rs = buf, ss, rs

        def slot(self, m):
            return 2 * chip_at(m // 2) + (e if m % 2 == 0 else 1 - e)

        def copy(self, src, at, place, device):
            return remote(src, self.buf.at[at], (self.ss, place), (self.rs, place), device)

        def hop(self, delta, part, src=None):
            rows = pl.ds(64 * part, 64)
            at = (self.slot(2 * delta) if src is None else b, rows)
            return self.copy(self.buf.at[at] if src is None else src.at[rows], at, 2 * delta + part, dev(delta))

        def turn(self, part, delta):
            at = (self.slot(2 * delta), pl.ds(64 * part, 64))
            return self.copy(self.buf.at[at], at, 6 + part, dev(2 - part))

        def core(self, delta, src=None):
            at = self.slot(2 * delta) if src is None else b
            return self.copy(self.buf.at[at] if src is None else src, at, (0, 8, 9)[delta], other)

        def core_half(self, part):
            at = (self.slot(6), pl.ds(64 * part, 64))
            return self.copy(self.buf.at[at], at, 10 + part, other)

        def send(self, src):
            for part in (0, 1):
                self.hop(1, part, src).start()
                self.hop(2, 1 - part, src).start()
            self.core(0, src).start()

        def pass_first(self):
            self.hop(1, 0).wait_recv()
            self.turn(0, 1).start()
            self.hop(2, 1).wait_recv()
            self.turn(1, 2).start()

        def pass_second(self):
            self.hop(1, 1).wait_recv()
            self.core(1).start()
            self.hop(2, 0).wait_recv()
            self.core(2).start()

        def pass_diagonal(self):
            for part in (0, 1):
                self.turn(part, 3).wait_recv()
                self.core_half(part).start()

        def wait_core(self, delta):
            at = self.slot(2 * delta + 1)
            if delta < 3:
                self.copy(self.buf.at[at], at, (0, 8, 9)[delta], other).wait_recv()
            else:
                for part in (0, 1):
                    half = (at, pl.ds(64 * part, 64))
                    self.copy(self.buf.at[half], half, 10 + part, other).wait_recv()

        def finish(self, src):
            self.core(0, src).wait_send()
            for part in (0, 1):
                self.hop(1, part, src).wait_send()
                self.hop(2, part, src).wait_send()
                self.turn(part, 1 + part).wait_send()
                self.core(1 + part).wait_send()
                self.core_half(part).wait_send()

    gx = Gather(r["xb"], r["gx_s"], r["gx_r"])
    gdy = Gather(r["dyb"], r["gdy_s"], r["gdy_r"])

    class Chain:
        def __init__(self, name, K, dtype, sink, place):
            self.K, self.dtype, self.sink, self.place = K, dtype, sink, place
            for part in ("own", "rl", "rr", "tu", "td", "su", "sd", "ru", "rd"):
                setattr(self, part, r[name + "_" + part])

        def up(self, src, k):
            return remote(src, self.rl.at[k], (self.su, k), (self.ru, k), (z + 1, b))

        def down(self, src, k):
            return remote(src, self.rr.at[k], (self.sd, k), (self.rd, k), (z - 1, b))

        def prime(self, k):
            if Z == 1:
                return

            @pl.when(z == 0)
            def _():
                self.up(self.own.at[k], k).start()

            @pl.when(z == Z - 1)
            def _():
                self.down(self.own.at[k], k).start()

        def tick(self, i):
            ku = i - 1 - SKEW * (z - 1)

            @pl.when((z > 0) & (z < Z - 1) & (ku >= 0) & (ku < self.K))
            def _():
                self.up(self.own.at[ku], ku).wait_recv()
                self.tu[ku] = (self.own[ku].astype(F32) + self.rl[ku].astype(F32)).astype(self.dtype)
                self.up(self.tu.at[ku], ku).start()

            kd = i - 1 - SKEW * (Z - 2 - z)

            @pl.when((z > 0) & (z < Z - 1) & (kd >= 0) & (kd < self.K))
            def _():
                self.down(self.own.at[kd], kd).wait_recv()
                self.td[kd] = (self.own[kd].astype(F32) + self.rr[kd].astype(F32)).astype(self.dtype)
                self.down(self.td.at[kd], kd).start()

            k = i - 1 - SKEW * max(Z - 2, 0)
            if 0 <= k < self.K:

                @pl.when(z == 0)
                def _():
                    if Z > 1:
                        self.down(self.own.at[k], k).wait_recv()
                    self.sink(k, self.own[k].astype(F32) + self.rr[k].astype(F32))

                @pl.when((z == Z - 1) & (z > 0))
                def _():
                    self.up(self.own.at[k], k).wait_recv()
                    self.sink(k, self.own[k].astype(F32) + self.rl[k].astype(F32))

                @pl.when((z > 0) & (z < Z - 1))
                def _():
                    self.sink(
                        k,
                        self.own[k].astype(F32) + self.rl[k].astype(F32) + self.rr[k].astype(F32),
                    )

                leave(*self.place(k))

        def finish(self):
            @pl.when(z < Z - 1)
            def _():
                for k in range(self.K):
                    self.up(self.own.at[k], k).wait_send()

            @pl.when(z > 0)
            def _():
                for k in range(self.K):
                    self.down(self.own.at[k], k).wait_send()

    leaving = []

    def leave(name, at):
        copy = pltpu.make_async_copy(r["s_" + name].at[at], r["o_" + name].at[at], r["out_sem"].at[len(leaving)])
        copy.start()
        leaving.append(copy)

    def place_a(k):
        if k < 8:
            return "fc2", (pl.ds(96 * (k // 2), 96), pl.ds(384 * (k % 2), 384))
        src = chip_at((k - 8) // 2)
        return "fc1", (slice(None), pl.ds(pl.multiple_of(768 * src + 384 * (k % 2), 128), 384))

    def place_b(k):
        return "qkv", (chip_at(k),)

    def place_p(k):
        return "proj", (slice(None), pl.ds(384 * k, 384))

    def sink_to(place):
        def sink(k, total):
            name, at = place(k)
            r["s_" + name][at] = total.astype(BF16)

        return sink

    def place_c(k):
        return "ln", (slice(None),)

    def sink_c(k, total):
        for i in range(8):
            r["lnc"][i] = total[:, 96 * i : 96 * i + 96]
        r["s_ln"][...] = r["lnc"][b]

    ca = Chain("ca", 16, BF16, sink_to(place_a), place_a)
    cb = Chain("cb", 4, BF16, sink_to(place_b), place_b)
    cp = Chain("cp", 2, BF16, sink_to(place_p), place_p)
    cc = Chain("cc", 1, F32, sink_c, place_c)
    line = ((ca, 0), (cb, 16), (cp, 20))
    beats = [0]

    def beat(count=1):
        for _ in range(count):
            beats[0] += 1
            for chain, first in line:
                if 1 <= beats[0] - first <= chain.K + SKEW * max(Z - 2, 0):
                    chain.tick(beats[0] - first)

    gx.send(r["x"])
    load("w_qkv", r["w_qkv"], r["wq"])
    load("w_proj", r["w_proj"], r["wp"])
    load("dy", r["dy"], r["dyb"].at[b])
    load("w_fc1", r["w_fc1"], r["w1"])
    load("w_fc2", r["w_fc2"], r["w2"])

    crop = [r["crops"][0, RUN_ROWS * i] for i in range(8)]
    places = []
    for i in range(8):
        place = 2 * crop[i]
        for h in range(i):
            place = place + jnp.where(crop[h] == crop[i], 1, 0)
        places.append(place)
        r["inv"][i] = place
    for s in range(8):
        run = jnp.int32(0)
        for i in range(8):
            run = run + jnp.where(places[i] == s, i, 0)
        r["perm"][s] = run

    g1, b1 = r["ln1_gain"][...].reshape(1, 768), r["ln1_bias"][...].reshape(1, 768)
    g2, b2 = r["ln2_gain"][...].reshape(1, 768), r["ln2_bias"][...].reshape(1, 768)

    loads["x"].wait()
    loads["w_qkv"].wait()

    def project(delta):
        gx.wait_core(delta)
        pair = pl.ds(2 * chip_at(delta), 2)
        hat, _ = norm_parts(r["xb"][pair].reshape(256, 768).astype(F32))
        normed = (hat * g1 + b1).astype(BF16)
        r["n1"][pair] = normed.reshape(2, 128, 768)
        for t in range(3):
            out = mm(normed, r["wq"][:, pl.ds(pl.multiple_of(768 * t + 384 * e, 128), 384)])
            out = out * scale if t == 0 else out
            r["qkv"][pair, :, 384 * t : 384 * t + 384] = out.astype(BF16).reshape(2, 128, 384)

    project(0)
    gx.pass_first()
    gdy.send(r["dy"])
    gx.pass_second()
    project(1)
    project(2)
    gx.pass_diagonal()
    project(3)

    low_lanes = lax.broadcasted_iota(jnp.int32, (1, 128), 1) < HEAD

    def stack(two):
        none = jnp.zeros_like(two)
        return jnp.concatenate([jnp.where(low_lanes, two, none), jnp.where(low_lanes, none, two)], axis=0)

    def o_core(at):
        place = (e, pl.ds(2 * at, 2))
        return remote(r["ob"].at[place], r["ob"].at[place], (r["o_s"], at), (r["o_r"], at), other)

    def attend(at, carry):
        run0, run1 = r["perm"][2 * at], r["perm"][2 * at + 1]
        outs = []
        for h in range(3):
            q, k, v = [
                jnp.concatenate(
                    [r["qkv"][run, :, 384 * t + 128 * h : 384 * t + 128 * h + 128] for run in (run0, run1)],
                    axis=0,
                )
                for t in range(3)
            ]
            s = mm_nt(stack(q), k)
            p = jnp.exp(s - jnp.max(s, axis=-1, keepdims=True))
            o = mm(p.astype(BF16), jnp.concatenate([v, jnp.ones_like(v)], axis=1))
            o = o[:, 0:128] / o[:, 128:256]
            outs.append(jnp.where(low_lanes, o[0:256], o[256:512]))
        low = jnp.concatenate(outs, axis=1).astype(BF16)
        r["ob"][e, pl.ds(2 * at, 2)] = low.reshape(2, 128, 384)
        o_core(at).start()
        return carry

    def by_perm(buf, first, count):
        return jnp.concatenate([buf[r["perm"][first + i]] for i in range(count)], axis=0)

    own_hidden = pl.ds(pl.multiple_of(384 * b, 128), 384)

    def feed(at):
        place = (1 - e, pl.ds(2 * at, 2))
        remote(r["ob"].at[place], r["ob"].at[place], (r["o_s"], at), (r["o_r"], at), other).wait_recv()
        pair = pl.ds(2 * at, 2)
        o = jnp.concatenate([r["ob"][i, pair].reshape(256, 384) for i in range(2)], axis=1)
        x1 = by_perm(r["xb"], 2 * at, 2).astype(F32) + mm(o, r["wp"][...])
        r["x1"][pair] = x1.reshape(2, 128, 768)
        hat, _ = norm_parts(x1)
        n2 = (hat * g2 + b2).astype(BF16)
        r["n2"][pair] = n2.reshape(2, 128, 768)
        u = mm(n2, r["w1"][:, own_hidden])
        r["u"][pair] = u.reshape(2, 128, 384)
        r["act"][pair] = gelu_pair(u)[0].astype(BF16).reshape(2, 128, 384)

    attend(0, 0)
    gdy.pass_first()
    attend(1, 0)
    for name in ("w_proj", "w_fc1", "w_fc2", "dy"):
        loads[name].wait()
    feed(0)
    gdy.pass_second()
    attend(2, 0)
    feed(1)
    attend(3, 0)
    feed(2)
    gdy.pass_diagonal()
    feed(3)
    for delta in range(4):
        gdy.wait_core(delta)

    grad = mm_tn(r["act"][...].reshape(1024, 384), by_perm(r["dyb"], 0, 8)).astype(BF16)
    for k in range(8):
        ca.own[k] = grad[96 * (k // 2) : 96 * (k // 2) + 96, 384 * (k % 2) : 384 * (k % 2) + 384]
        ca.prime(k)

    place_own = r["inv"][b]
    dy_own = r["dyb"][b]
    r["y"][...] = r["x1"][place_own]
    r["dn2"][...] = jnp.zeros((128, 768), F32)

    def own_rows(i, carry):
        part = pl.ds(768 * i, 768)
        act, slope = gelu_pair(mm(r["n2"][place_own], r["w1"][:, part]))
        du = (mm_nt(r["dyb"][b], r["w2"][part]) * slope).astype(BF16)
        r["dn2"][...] += mm_nt(du, r["w1"][:, part])
        r["y"][...] += mm(act.astype(BF16), r["w2"][part])
        return carry

    for i in range(4):
        own_rows(i, 0)
        if i == 3:
            beat()
    r["s_y"][...] = r["y"][...].astype(BF16)
    leave("y", (slice(None),))

    dn2 = r["dn2"][...]
    hat, inv_std = norm_parts(r["x1"][place_own])
    r["lnp"][2:3] = jnp.sum(dn2 * hat, axis=0, keepdims=True)
    r["lnp"][3:4] = jnp.sum(dn2, axis=0, keepdims=True)
    dx1 = dy_own.astype(F32) + norm_back(dn2, hat, inv_std, g2)
    r["dx1"][...] = dx1
    low = dx1.astype(BF16)
    do = mm_nt(low, r["wp"][...]).astype(BF16)
    for i in range(4):
        r["dos"][i] = do[:, 192 * i : 192 * i + 192]

    def do_send(delta):
        return remote(r["dos"].at[chip_at(delta)], r["dob"].at[b], (r["do_s"], 2 * delta), (r["do_r"], 2 * delta), dev(delta))

    def do_slot(m):
        return 2 * chip_at(m // 2) + (e if m % 2 == 0 else 1 - e)

    def do_core(delta):
        src = r["dos"].at[chip] if delta == 0 else r["dob"].at[do_slot(2 * delta)]
        return remote(src, r["dob"].at[do_slot(2 * delta)], (r["do_s"], 2 * delta + 1), (r["do_r"], 2 * delta + 1), other)

    for delta in (3, 2, 1):
        do_send(delta).start()
    do_core(0).start()
    r["dob"][b] = r["dos"][chip]
    beat()

    def back_hidden(c, carry):
        pair = pl.ds(2 * c, 2)
        da = mm_nt(by_perm(r["dyb"], 2 * c, 2), r["w2"][own_hidden])
        slope = gelu_pair(r["u"][pair].reshape(256, 384))[1]
        r["du"][pair] = (da * slope).astype(BF16).reshape(2, 128, 384)
        return carry

    for c in range(4):
        back_hidden(c, 0)
    beat()
    grad = mm_tn(r["n2"][...].reshape(1024, 768), r["du"][...].reshape(1024, 384)).astype(BF16)
    for i in range(8):
        r["t1"][i % 2, i // 2] = grad[96 * i : 96 * i + 96]
    t1_core = remote(r["t1"].at[1 - e], r["t1x"], r["t1_cs"], r["t1_cr"], other)
    t1_core.start()
    beat()

    def t1_send(delta, half):
        src = r["t1"].at[e, chip_at(delta)] if half == 0 else r["t1x"].at[chip_at(delta)]
        hidden_core = e if half == 0 else 1 - e
        at = 2 * delta + half
        return remote(src, ca.own.at[8 + 2 * delta + hidden_core], (r["t1_s"], at), (r["t1_r"], at), dev(delta))

    o = jnp.concatenate([r["ob"][i, place_own] for i in range(2)], axis=1)
    grad = mm_tn(o, low).astype(BF16)
    for i in range(8):
        r["tp"][i % 2, i // 2] = grad[96 * i : 96 * i + 96]
    tp_core = remote(r["tp"].at[1 - e], r["tpx"], r["tp_cs"], r["tp_cr"], other)
    tp_core.start()

    def tp_send(delta):
        return remote(r["tps"].at[delta], r["tpr"].at[delta], (r["tp_s"], delta), (r["tp_r"], delta), dev(delta))

    t1_core.wait_recv()
    for delta in (1, 2, 3):
        for half in (0, 1):
            t1_send(delta, half).start()
    ca.own[8 + e] = r["t1"][e, chip]
    ca.own[9 - e] = r["t1x"][chip]
    ca.prime(8)
    ca.prime(9)
    beat()

    for s in range(4):
        r["n1s"][s] = r["n1"][r["perm"][4 * e + s]]
    odd = lax.rem(chip, 2) == 1
    for t in range(3):
        first = pl.multiple_of(768 * t + 192 * chip - 64 * lax.rem(chip, 2), 128)
        four = mm(r["n1s"][...].reshape(512, 768), r["wq"][:, pl.ds(first, 256)])
        three = jnp.where(odd, four[:, 64:256], four[:, 0:192]).astype(BF16)
        r["qo"][:, :, 128 * t : 128 * t + 128] = three[:, 0:128].reshape(2, 256, 128)
        r["qo"][:, :, 384 + 64 * t : 448 + 64 * t] = three[:, 128:192].reshape(2, 256, 64)

    for delta in (1, 2, 3):
        do_send(delta).wait_recv()
        do_core(delta).start()
    for delta in range(4):
        at = do_slot(2 * delta + 1)
        remote(r["dob"].at[at], r["dob"].at[at], (r["do_s"], 2 * delta + 1), (r["do_r"], 2 * delta + 1), other).wait_recv()

    beat()

    def t1_arrive(delta):
        for half in (0, 1):
            t1_send(delta, half).wait_recv()
        ca.prime(8 + 2 * delta)
        ca.prime(9 + 2 * delta)

    def attend_back(at, heads):
        runs = [r["perm"][4 * e + 2 * at + i] for i in range(2)]
        if heads == 2:
            g = jnp.concatenate([r["dob"][run, :, 0:128] for run in runs], axis=0)
            q, k, v = [r["qo"][at, :, 128 * t : 128 * t + 128] for t in range(3)]
            q, g = stack(q), stack(g)
        else:
            g = jnp.concatenate([r["dob"][run, :, 128:192] for run in runs], axis=0)
            q, k, v = [r["qo"][at, :, 384 + 64 * t : 448 + 64 * t] for t in range(3)]
        q = (q.astype(F32) * scale).astype(BF16)
        s = mm_nt(q, k)
        p = jnp.exp(s - jnp.max(s, axis=-1, keepdims=True))
        p = p / jnp.sum(p, axis=-1, keepdims=True)
        dp = mm_nt(g, v)
        ds = (p * (dp - jnp.sum(p * dp, axis=-1, keepdims=True))).astype(BF16)
        dq = mm(ds, k) * scale
        dk = mm_tn(ds, q)
        dv = mm_tn(p.astype(BF16), g)
        mine = pl.ds(2 * (2 * e + at), 2)
        if heads == 2:
            dq = jnp.where(low_lanes, dq[0:256], dq[256:512])
        first, wide = (0, 128) if heads == 2 else (384, 64)
        for t, part in enumerate((dq, dk, dv)):
            r["dq"][mine, :, first + wide * t : first + wide * t + wide] = part.astype(BF16).reshape(2, 128, wide)

    attend_back(0, 2)
    beat()
    attend_back(0, 1)
    t1_arrive(1)
    beat()
    attend_back(1, 2)
    t1_arrive(2)
    attend_back(1, 1)

    dq_core = remote(r["dq"].at[pl.ds(4 * e, 4)], r["dq"].at[pl.ds(4 * e, 4)], r["dq_cs"], r["dq_cr"], other)
    dq_core.start()
    grad = mm_tn(r["n1s"][...].reshape(512, 768), r["dq"][pl.ds(4 * e, 4)].reshape(512, 576))
    for i in range(8):
        r["tq"][i % 2, i // 2] = grad[96 * i : 96 * i + 96].astype(BF16)
    tq_core = remote(r["tq"].at[1 - e], r["tqx"], r["tq_cs"], r["tq_cr"], other)
    tq_core.start()

    def tq_send(delta):
        return remote(r["tqs"].at[delta], cb.own.at[delta], (r["tq_s"], delta), (r["tq_r"], delta), dev(delta))

    def dq_send(delta, landing=None):
        landing = chip if landing is None else landing
        return remote(r["dqs"].at[delta], r["dqr"].at[landing], (r["dq_s"], delta), (r["dq_r"], delta), dev(delta))

    beat()

    t1_arrive(3)
    tq_core.wait_recv()
    for delta in (3, 2, 1, 0):
        c = chip_at(delta)
        total = (r["tq"][e, c].astype(F32) + r["tqx"][c].astype(F32)).astype(BF16)
        if delta == 0:
            cb.own[0] = total
        else:
            r["tqs"][delta] = total
            tq_send(delta).start()
    beat()
    at = pl.ds(4 - 4 * e, 4)
    remote(r["dq"].at[at], r["dq"].at[at], r["dq_cs"], r["dq_cr"], other).wait_recv()
    for delta in (3, 2, 1):
        r["dqs"][delta] = r["dq"][r["inv"][2 * chip_at(delta) + e]]
        dq_send(delta).start()
    tp_core.wait_recv()
    for delta in (3, 2, 1, 0):
        c = chip_at(delta)
        r["tps"][delta] = (r["tp"][e, c].astype(F32) + r["tpx"][c].astype(F32)).astype(BF16)
        if delta > 0:
            tp_send(delta).start()

    def beat_to(count):
        beat(count - beats[0])

    beat_to(12)
    cb.prime(0)
    beat_to(15)
    for delta in (1, 2, 3):
        tq_send(delta).wait_recv()
        cb.prime(delta)
    beat_to(18)
    r["dqr"][chip] = r["dq"][r["inv"][b]]
    for delta in (1, 2, 3):
        dq_send(delta, chip_at(delta)).wait_recv()
    for i in range(4):
        for t in range(3):
            first = 768 * t + 192 * i
            r["dnat"][:, first : first + 128] = r["dqr"][i, :, 128 * t : 128 * t + 128]
            r["dnat"][:, first + 128 : first + 192] = r["dqr"][i, :, 384 + 64 * t : 448 + 64 * t]
    dn1 = mm_nt(r["dnat"][...], r["wq"][...])
    hat, inv_std = norm_parts(r["xb"][b].astype(F32))
    r["lnp"][0:1] = jnp.sum(dn1 * hat, axis=0, keepdims=True)
    r["lnp"][1:2] = jnp.sum(dn1, axis=0, keepdims=True)
    r["lnp"][4:8] = jnp.zeros((4, 768), F32)
    r["s_gin"][...] = (r["dx1"][...] + norm_back(dn1, hat, inv_std, g1)).astype(BF16)
    leave("gin", (slice(None),))
    ln_core = remote(r["lnp"], r["lnx"].at[0], (r["ln_s"], 0), (r["ln_r"], 0), other)
    ln_core.start()
    beat_to(19)
    ln_core.wait_recv()
    r["lns"][...] = r["lnp"][...] + r["lnx"][0]

    def ln_send(delta):
        return remote(r["lns"], r["lnx"].at[delta], (r["ln_s"], delta), (r["ln_r"], delta), dev(delta))

    for delta in (3, 2, 1):
        ln_send(delta).start()
    beat_to(20)
    total = r["tps"][0].astype(F32)
    for delta in (1, 2, 3):
        tp_send(delta).wait_recv()
        total += r["tpr"][delta].astype(F32)
    for k in range(2):
        cp.own[k] = total[:, 384 * k : 384 * k + 384].astype(BF16)
        cp.prime(k)
    total = r["lns"][...]
    for delta in (1, 2, 3):
        ln_send(delta).wait_recv()
        total += r["lnx"][delta]
    cc.own[0] = total
    cc.prime(0)
    beat_to(22)
    cc.tick(1)
    beat_to(22 + SKEW)
    cc.tick(1 + SKEW)
    beat_to(22 + SKEW * max(Z - 2, 0))
    for hop in range(2, max(Z - 2, 0) + 1):
        cc.tick(1 + SKEW * hop)

    gx.finish(r["x"])
    gdy.finish(r["dy"])
    for at in range(4):
        o_core(at).wait_send()
    for copy in (t1_core, tp_core, tq_core, dq_core, ln_core, do_core(0)):
        copy.wait_send()
    for delta in (1, 2, 3):
        do_send(delta).wait_send()
        do_core(delta).wait_send()
        t1_send(delta, 0).wait_send()
        t1_send(delta, 1).wait_send()
        tp_send(delta).wait_send()
        tq_send(delta).wait_send()
        dq_send(delta).wait_send()
        ln_send(delta).wait_send()
    ca.finish()
    cb.finish()
    cp.finish()
    cc.finish()
    for copy in leaving:
        copy.wait()


def widen_kernel(*refs):
    sources, results, held, wide = refs[:7], refs[7:17], refs[17:24], refs[24:32]
    sem_in, sem_out = refs[32:]
    every = slice(None)
    pieces = [(4, (every, pl.ds(1024 * i, 1024))) for i in range(3)]
    pieces += [(5, (pl.ds(128 * i, 128), every)) for i in range(3)]
    pieces += [(2, (every,)), (3, (every,)), (6, (every,)), (0, (every,)), (1, (every,))]
    copies = []
    for n, (i, at) in enumerate(pieces):
        copies.append(pltpu.make_async_copy(sources[i].at[at], held[i].at[at], sem_in.at[n]))
        copies[-1].start()
    leaving = []

    def leave(src, dst):
        copy = pltpu.make_async_copy(src, dst, sem_out.at[len(leaving)])
        copy.start()
        leaving.append(copy)

    for (i, at), copy in zip(pieces, copies):
        copy.wait()
        part = held[i]
        if i < 2:
            leave(part, results[i])
        elif i == 2:
            for t in range(3):
                parts = []
                for c in range(4):
                    parts.append(part[c, :, 128 * t : 128 * t + 128])
                    parts.append(part[c, :, 384 + 64 * t : 448 + 64 * t])
                cols = (every, pl.ds(768 * t, 768))
                wide[0][cols] = jnp.concatenate(parts, axis=1).astype(F32)
                leave(wide[0].at[cols], results[2].at[cols])
        elif i < 6:
            wide[i - 2][at] = part[at].astype(F32)
            leave(wide[i - 2].at[at], results[i].at[at])
        else:
            for t in range(4):
                wide[4 + t][...] = part[t, :]
                leave(wide[4 + t], results[6 + t])
    for copy in leaving:
        copy.wait()


def fast_shards(
    Z, inputs, crops, ln1_gain, ln1_bias, w_qkv, w_proj, ln2_gain, ln2_bias, w_fc1, w_fc2, cotangent
):
    V, D = pltpu.VMEM, pltpu.SemaphoreType.DMA
    anyspace = pl.BlockSpec(memory_space=pl.ANY)
    vmem = pl.BlockSpec(memory_space=pltpu.VMEM)
    smem = pl.BlockSpec(memory_space=pltpu.SMEM)
    arguments = dict(
        x=(inputs[0], anyspace),
        crops=(crops, smem),
        ln1_gain=(ln1_gain, vmem),
        ln1_bias=(ln1_bias, vmem),
        w_qkv=(w_qkv, anyspace),
        w_proj=(w_proj, anyspace),
        ln2_gain=(ln2_gain, vmem),
        ln2_bias=(ln2_bias, vmem),
        w_fc1=(w_fc1, anyspace),
        w_fc2=(w_fc2, anyspace),
        dy=(cotangent[0], anyspace),
    )
    results = dict(
        o_y=((128, 768), BF16),
        o_gin=((128, 768), BF16),
        o_qkv=((4, 96, 576), BF16),
        o_proj=((96, 768), BF16),
        o_fc1=((96, 3072), BF16),
        o_fc2=((384, 768), BF16),
        o_ln=((8, 96), F32),
    )
    scratch = dict(
        ld_sem=D((6,)),
        perm=pltpu.SMEM((8,), jnp.int32),
        inv=pltpu.SMEM((8,), jnp.int32),
        xb=V((8, 128, 768), BF16), gx_s=D((12,)), gx_r=D((12,)),
        dyb=V((8, 128, 768), BF16), gdy_s=D((12,)), gdy_r=D((12,)),
        dob=V((8, 128, 192), BF16), dos=V((4, 128, 192), BF16), do_s=D((8,)), do_r=D((8,)),
        wq=V((768, 2304), BF16), dnat=V((128, 2304), BF16), wp=V((768, 768), BF16),
        w1=V((768, 3072), BF16), w2=V((3072, 768), BF16),
        n1=V((8, 128, 768), BF16), n1s=V((4, 128, 768), BF16), qkv=V((8, 128, 1152), BF16),
        ob=V((2, 8, 128, 384), BF16), o_s=D((4,)), o_r=D((4,)),
        x1=V((8, 128, 768), F32), n2=V((8, 128, 768), BF16),
        act=V((8, 128, 384), BF16), u=V((8, 128, 384), F32), du=V((8, 128, 384), BF16),
        y=V((128, 768), F32), dn2=V((128, 768), F32), dx1=V((128, 768), F32),
        t1=V((2, 4, 96, 384), BF16), t1x=V((4, 96, 384), BF16),
        t1_cs=D, t1_cr=D, t1_s=D((8,)), t1_r=D((8,)),
        tp=V((2, 4, 96, 768), BF16), tpx=V((4, 96, 768), BF16), tps=V((4, 96, 768), BF16), tpr=V((4, 96, 768), BF16),
        tp_cs=D, tp_cr=D, tp_s=D((4,)), tp_r=D((4,)),
        qo=V((2, 256, 576), BF16), dq=V((8, 128, 576), BF16),
        tq=V((2, 4, 96, 576), BF16), tqx=V((4, 96, 576), BF16), tqs=V((4, 96, 576), BF16),
        tq_cs=D, tq_cr=D, tq_s=D((4,)), tq_r=D((4,)),
        dqs=V((4, 128, 576), BF16), dqr=V((4, 128, 576), BF16),
        dq_cs=D, dq_cr=D, dq_s=D((4,)), dq_r=D((4,)),
        lnp=V((8, 768), F32), lns=V((8, 768), F32), lnx=V((4, 8, 768), F32), lnc=V((8, 8, 96), F32),
        ln_s=D((4,)), ln_r=D((4,)),
    )
    for name, K, shape, dtype in (
        ("ca", 16, (96, 384), BF16), ("cb", 4, (96, 576), BF16), ("cp", 2, (96, 384), BF16), ("cc", 1, (8, 768), F32)
    ):
        for part in ("own", "rl", "rr", "tu", "td"):
            scratch[name + "_" + part] = V((K, *shape), dtype)
        for part in ("su", "sd", "ru", "rd"):
            scratch[name + "_" + part] = D((K,))
    scratch.update({"s" + name[1:]: V(*shape) for name, shape in results.items()}, out_sem=D((25,)))
    names = (*arguments, *results, *scratch)
    narrow = pl.pallas_call(
        functools.partial(layer_kernel, Z, names),
        out_shape=[jax.ShapeDtypeStruct(*shape) for shape in results.values()],
        in_specs=[spec for _, spec in arguments.values()],
        out_specs=[anyspace] * len(results),
        scratch_shapes=list(scratch.values()),
        compiler_params=pltpu.CompilerParams(
            collective_id=0, has_side_effects=True, vmem_limit_bytes=60 * 2**20
        ),
    )(*[array for array, _ in arguments.values()])
    wide = [((128, 768), BF16), ((128, 768), BF16), ((96, 2304), F32), ((96, 768), F32), ((96, 3072), F32), ((384, 768), F32)]
    wide += [((96,), F32)] * 4
    y, gin, *grads = pl.pallas_call(
        widen_kernel,
        out_shape=[jax.ShapeDtypeStruct(*shape) for shape in wide],
        in_specs=[anyspace] * len(narrow),
        out_specs=[anyspace] * len(wide),
        scratch_shapes=[V(*shape) for shape in results.values()]
        + [V(*shape) for shape in wide[2:6]]
        + [V((96,), F32)] * 4
        + [D((11,)), D((16,))],
        compiler_params=pltpu.CompilerParams(vmem_limit_bytes=62 * 2**20),
    )(*narrow)
    return (y[None], gin[None], *grads)


def solution(mesh):
    placed = (
        P("dp", "blk", None),
        P("dp", None),
        P(),
        P(),
        P(),
        P(),
        P(),
        P(),
        P(),
        P(),
        P("dp", "blk", None),
    )
    def whole(*arrays):
        one_run = arrays[0].shape[1] == 8 * RUN_ROWS and mesh.shape["blk"] == 8
        body = functools.partial(fast_shards, mesh.shape["dp"]) if one_run else shards
        return placed_call(body)(*arrays)

    placed_call = lambda body: jax.shard_map(
        body,
        mesh=mesh,
        in_specs=placed,
        out_specs=(
            P("dp", "blk", None),
            P("dp", "blk", None),
            P("blk", None),
            P("blk", None),
            P("blk", None),
            P("blk", None),
            P("blk"),
            P("blk"),
            P("blk"),
            P("blk"),
        ),
        check_vma=False,
    )
    return whole
```

```python
import functools
import math

import jax
import jax.numpy as jnp
from jax import lax
from jax.experimental import pallas as pl
from jax.experimental.pallas import tpu as pltpu
from jax.sharding import PartitionSpec as P

HEADS = 12


EPSILON = 1e-05
MASKED = -1e30


def layer_norm(values_in, gain_in, shift_in):
    row_mean = jnp.mean(values_in, axis=-1, keepdims=True)
    centred = values_in - row_mean
    row_var = jnp.mean(centred * centred, axis=-1, keepdims=True)
    return centred * lax.rsqrt(row_var + EPSILON) * gain_in + shift_in


def contract_rows(left_side, right_side):
    return lax.dot_general(
        left_side, right_side, (((0,), (0,)), ((), ())), preferred_element_type=jnp.float32
    )


def against_weight(grad_rows, weight_mat):
    return lax.dot_general(
        grad_rows, weight_mat, (((1,), (1,)), ((), ())), preferred_element_type=jnp.float32
    )


def head_view(matrix, head_count):
    return matrix.reshape(matrix.shape[0], head_count, matrix.shape[1] // head_count)


def scores_of(query_heads, key_heads, score_scale):
    return (
        jnp.einsum("qhd,khd->hqk", query_heads, key_heads, preferred_element_type=jnp.float32)
        * score_scale
    )


def weights_of(scores, visible, logsum):
    return jnp.where(visible[None], jnp.exp(scores - logsum[:, :, None]), 0.0)


def shards(
    inputs, crops, ln1_gain, ln1_bias, w_qkv, w_proj, ln2_gain, ln2_bias, w_fc1, w_fc2, cotangent
):
    row_count = inputs.shape[1]
    model_width = inputs.shape[2]
    head_count = HEADS
    score_scale = 1.0 / math.sqrt(model_width // head_count)
    seq_crops = crops[0]
    seq_len = seq_crops.shape[0]
    key_block = min(1024, seq_len)
    block_count = seq_len // key_block
    block_ids = jnp.arange(block_count)
    own_crops = lax.dynamic_slice_in_dim(seq_crops, lax.axis_index("blk") * row_count, row_count, 0)
    residual = inputs[0].astype(jnp.float32)
    normed_one_low = layer_norm(residual, ln1_gain, ln1_bias).astype(jnp.bfloat16)
    qkv_low = jnp.dot(normed_one_low, w_qkv, preferred_element_type=jnp.float32).astype(
        jnp.bfloat16
    )
    query_own = qkv_low[:, :model_width]
    key_own = qkv_low[:, model_width : 2 * model_width]
    value_own = qkv_low[:, 2 * model_width :]
    keys_all, values_all = (
        lax.all_gather(key_own, "blk", axis=0, tiled=True),
        lax.all_gather(value_own, "blk", axis=0, tiled=True),
    )
    query_heads = head_view(query_own, head_count)

    def block_inputs(block_index):
        key_heads = head_view(
            lax.dynamic_slice_in_dim(keys_all, block_index * key_block, key_block, 0), head_count
        )
        value_heads = head_view(
            lax.dynamic_slice_in_dim(values_all, block_index * key_block, key_block, 0), head_count
        )
        crop_block = lax.dynamic_slice_in_dim(seq_crops, block_index * key_block, key_block, 0)
        visible = own_crops[:, None] == crop_block[None, :]
        return (key_heads, value_heads, visible)

    def stats_step(carried, block_index):
        old_max, summed = carried
        key_heads, value_heads, visible = block_inputs(block_index)
        scores = jnp.where(visible[None], scores_of(query_heads, key_heads, score_scale), MASKED)
        new_max = jnp.maximum(old_max, jnp.max(scores, axis=-1))
        exp_terms = jnp.where(visible[None], jnp.exp(scores - new_max[:, :, None]), 0.0)
        return ((new_max, summed * jnp.exp(old_max - new_max) + jnp.sum(exp_terms, axis=-1)), None)

    start_max = jnp.full((head_count, row_count), MASKED, jnp.float32)
    start_sum = jnp.zeros((head_count, row_count), jnp.float32)
    (row_max, summed), _ = lax.scan(stats_step, (start_max, start_sum), block_ids)
    logsum = row_max + jnp.log(summed)

    def output_step(running, block_index):
        key_heads, value_heads, visible = block_inputs(block_index)
        attn_probs = weights_of(
            scores_of(query_heads, key_heads, score_scale), visible, logsum
        ).astype(jnp.bfloat16)
        return (
            running
            + jnp.einsum(
                "hqk,khd->qhd", attn_probs, value_heads, preferred_element_type=jnp.float32
            ),
            None,
        )

    attended, _ = lax.scan(output_step, jnp.zeros(query_heads.shape, jnp.float32), block_ids)
    attended_low = attended.reshape(row_count, model_width).astype(jnp.bfloat16)
    mixed_rows = residual + jnp.dot(attended_low, w_proj, preferred_element_type=jnp.float32)
    normed_two_low = layer_norm(mixed_rows, ln2_gain, ln2_bias).astype(jnp.bfloat16)
    hidden_pre = jnp.dot(normed_two_low, w_fc1, preferred_element_type=jnp.float32)
    active, gelu_back = jax.vjp(jax.nn.gelu, hidden_pre)
    active_low = active.astype(jnp.bfloat16)
    result = mixed_rows + jnp.dot(active_low, w_fc2, preferred_element_type=jnp.float32)
    output = result.astype(jnp.bfloat16)[None]
    grad_out_low = cotangent[0]
    grad_fc2 = contract_rows(active_low, grad_out_low)
    grad_active = against_weight(grad_out_low, w_fc2)
    grad_hidden_low = gelu_back(grad_active)[0].astype(jnp.bfloat16)
    grad_fc1 = contract_rows(normed_two_low, grad_hidden_low)
    grad_normed_two = against_weight(grad_hidden_low, w_fc1)
    _, norm_two_back = jax.vjp(layer_norm, mixed_rows, ln2_gain, ln2_bias)
    grad_mixed_part, grad_gain_two, grad_bias_two = norm_two_back(grad_normed_two)
    grad_mixed = grad_out_low.astype(jnp.float32) + grad_mixed_part
    grad_mixed_low = grad_mixed.astype(jnp.bfloat16)
    grad_proj = contract_rows(attended_low, grad_mixed_low)
    grad_attended_low = against_weight(grad_mixed_low, w_proj).astype(jnp.bfloat16)
    grad_heads = head_view(grad_attended_low, head_count)

    def delta_step(running, block_index):
        key_heads, value_heads, visible = block_inputs(block_index)
        attn_probs = weights_of(scores_of(query_heads, key_heads, score_scale), visible, logsum)
        grad_probs = jnp.einsum(
            "qhd,khd->hqk", grad_heads, value_heads, preferred_element_type=jnp.float32
        )
        return (running + jnp.sum(attn_probs * grad_probs, axis=-1), None)

    row_delta, _ = lax.scan(delta_step, jnp.zeros((head_count, row_count), jnp.float32), block_ids)

    def score_grads(
        query_part, grad_part, logsum_part, delta_part, key_heads, value_heads, visible
    ):
        attn_probs = weights_of(scores_of(query_part, key_heads, score_scale), visible, logsum_part)
        grad_probs = jnp.einsum(
            "qhd,khd->hqk", grad_part, value_heads, preferred_element_type=jnp.float32
        )
        grad_scores = (attn_probs * (grad_probs - delta_part[:, :, None])).astype(jnp.bfloat16)
        return (attn_probs, grad_scores)

    def pair_step(running, block_index):
        key_heads, value_heads, visible = block_inputs(block_index)
        attn_probs, grad_scores = score_grads(
            query_heads, grad_heads, logsum, row_delta, key_heads, value_heads, visible
        )
        key_term = (
            jnp.einsum("hqk,qhd->khd", grad_scores, query_heads, preferred_element_type=jnp.float32)
            * score_scale
        )
        value_term = jnp.einsum(
            "hqk,qhd->khd",
            attn_probs.astype(jnp.bfloat16),
            grad_heads,
            preferred_element_type=jnp.float32,
        )
        joined = jnp.concatenate(
            [key_term.reshape(key_block, model_width), value_term.reshape(key_block, model_width)],
            axis=1,
        )
        step_query = jnp.einsum(
            "hqk,khd->qhd", grad_scores, key_heads, preferred_element_type=jnp.float32
        )
        return (running + step_query, joined)

    grad_query, key_terms = lax.scan(
        pair_step, jnp.zeros(query_heads.shape, jnp.float32), block_ids
    )
    key_sums = lax.psum_scatter(
        key_terms.reshape(seq_len, 2 * model_width).astype(jnp.bfloat16),
        "blk",
        scatter_dimension=0,
        tiled=True,
    ).astype(jnp.float32)
    grad_key = key_sums[:, :model_width]
    grad_value = key_sums[:, model_width:]
    grad_query = grad_query.reshape(row_count, model_width) * score_scale
    grad_qkv_low = jnp.concatenate([grad_query, grad_key, grad_value], axis=1).astype(jnp.bfloat16)
    grad_wqkv = contract_rows(normed_one_low, grad_qkv_low)
    grad_normed_one = against_weight(grad_qkv_low, w_qkv)
    _, norm_one_back = jax.vjp(layer_norm, residual, ln1_gain, ln1_bias)
    grad_resid, grad_gain_one, grad_bias_one = norm_one_back(grad_normed_one)
    grad_input = (grad_mixed + grad_resid).astype(jnp.bfloat16)[None]
    (
        fc1_share,
        fc2_share,
        qkv_share,
        proj_share,
        gain_one_share,
        bias_one_share,
        gain_two_share,
        bias_two_share,
    ) = (
        lax.psum_scatter(
            grad_fc1.astype(jnp.bfloat16), "blk", scatter_dimension=0, tiled=True
        ).astype(jnp.float32),
        lax.psum_scatter(
            grad_fc2.astype(jnp.bfloat16), "blk", scatter_dimension=0, tiled=True
        ).astype(jnp.float32),
        lax.psum_scatter(
            grad_wqkv.astype(jnp.bfloat16), "blk", scatter_dimension=0, tiled=True
        ).astype(jnp.float32),
        lax.psum_scatter(
            grad_proj.astype(jnp.bfloat16), "blk", scatter_dimension=0, tiled=True
        ).astype(jnp.float32),
        lax.psum_scatter(
            grad_gain_one.astype(jnp.bfloat16), "blk", scatter_dimension=0, tiled=True
        ).astype(jnp.float32),
        lax.psum_scatter(
            grad_bias_one.astype(jnp.bfloat16), "blk", scatter_dimension=0, tiled=True
        ).astype(jnp.float32),
        lax.psum_scatter(
            grad_gain_two.astype(jnp.bfloat16), "blk", scatter_dimension=0, tiled=True
        ).astype(jnp.float32),
        lax.psum_scatter(
            grad_bias_two.astype(jnp.bfloat16), "blk", scatter_dimension=0, tiled=True
        ).astype(jnp.float32),
    )
    totals = (
        lax.psum(qkv_share.astype(jnp.bfloat16), "dp").astype(jnp.float32),
        lax.psum(proj_share.astype(jnp.bfloat16), "dp").astype(jnp.float32),
        lax.psum(fc1_share.astype(jnp.bfloat16), "dp").astype(jnp.float32),
        lax.psum(fc2_share.astype(jnp.bfloat16), "dp").astype(jnp.float32),
        lax.psum(gain_one_share.astype(jnp.bfloat16), "dp").astype(jnp.float32),
        lax.psum(bias_one_share.astype(jnp.bfloat16), "dp").astype(jnp.float32),
        lax.psum(gain_two_share.astype(jnp.bfloat16), "dp").astype(jnp.float32),
        lax.psum(bias_two_share.astype(jnp.bfloat16), "dp").astype(jnp.float32),
    )
    return (
        output,
        grad_input,
        totals[0],
        totals[1],
        totals[2],
        totals[3],
        totals[4],
        totals[5],
        totals[6],
        totals[7],
    )


MESH = pl.DeviceIdType.MESH
F32 = jnp.float32
BF16 = jnp.bfloat16
RUN_ROWS = 128
HEAD = 64
SKEW = 2


def mm(left, right):
    return lax.dot_general(left, right, (((1,), (0,)), ((), ())), preferred_element_type=F32)


def mm_nt(left, right):
    return lax.dot_general(left, right, (((1,), (1,)), ((), ())), preferred_element_type=F32)


def mm_tn(left, right):
    return lax.dot_general(left, right, (((0,), (0,)), ((), ())), preferred_element_type=F32)


def norm_parts(rows):
    centred = rows - jnp.mean(rows, axis=-1, keepdims=True)
    inv_std = lax.rsqrt(jnp.mean(centred * centred, axis=-1, keepdims=True) + EPSILON)
    return centred * inv_std, inv_std


def norm_back(grad_rows, hat, inv_std, gain):
    grad_hat = grad_rows * gain
    return inv_std * (
        grad_hat
        - jnp.mean(grad_hat, axis=-1, keepdims=True)
        - hat * jnp.mean(grad_hat * hat, axis=-1, keepdims=True)
    )


def gelu_pair(u):
    inner = 0.7978845608028654 * (u + 0.044715 * u * u * u)
    t = jnp.tanh(inner)
    half = 0.5 * (1.0 + t)
    slope = half + 0.5 * u * (1.0 - t * t) * (0.7978845608028654 * (1.0 + 0.134145 * u * u))
    return u * half, slope


def layer_kernel(Z, names, *refs):
    r = dict(zip(names, refs, strict=True))
    z = lax.axis_index("dp")
    b = lax.axis_index("blk")
    e = lax.rem(b, 2)
    chip = b // 2
    cx = lax.rem(chip, 2)
    cy = chip // 2
    scale = HEAD**-0.5

    def chip_at(delta):
        dx, dy = delta % 2, delta // 2
        return 2 * (cy + dy - 2 * cy * dy) + (cx + dx - 2 * cx * dx)

    def dev(delta):
        return (z, 2 * chip_at(delta) + e)

    other = (z, b + 1 - 2 * e)

    def remote(src, dst, send_sem, recv_sem, device):
        sems = [s[0].at[s[1]] if isinstance(s, tuple) else s for s in (send_sem, recv_sem)]
        return pltpu.make_async_remote_copy(
            src_ref=src, dst_ref=dst, send_sem=sems[0], recv_sem=sems[1],
            device_id=device, device_id_type=MESH,
        )

    loads = {}

    def load(name, src, dst):
        loads[name] = pltpu.make_async_copy(src, dst, r["ld_sem"].at[len(loads)])
        loads[name].start()

    load("x", r["x"], r["xb"].at[b])

    bar = pltpu.get_barrier_semaphore()
    for target in (other, dev(1), dev(2), dev(3)):
        pl.semaphore_signal(bar, inc=1, device_id=target, device_id_type=MESH)

    @pl.when(z > 0)
    def _():
        pl.semaphore_signal(bar, inc=1, device_id=(z - 1, b), device_id_type=MESH)

    @pl.when(z < Z - 1)
    def _():
        pl.semaphore_signal(bar, inc=1, device_id=(z + 1, b), device_id_type=MESH)

    pl.semaphore_wait(bar, 4 + jnp.minimum(z, 1) + jnp.minimum(Z - 1 - z, 1))

    class Gather:
        def __init__(self, buf, ss, rs):
            self.buf, self.ss, self.rs = buf, ss, rs

        def slot(self, m):
            return 2 * chip_at(m // 2) + (e if m % 2 == 0 else 1 - e)

        def copy(self, src, at, place, device):
            return remote(src, self.buf.at[at], (self.ss, place), (self.rs, place), device)

        def hop(self, delta, part, src=None):
            rows = pl.ds(64 * part, 64)
            at = (self.slot(2 * delta) if src is None else b, rows)
            return self.copy(self.buf.at[at] if src is None else src.at[rows], at, 2 * delta + part, dev(delta))

        def turn(self, part, delta):
            at = (self.slot(2 * delta), pl.ds(64 * part, 64))
            return self.copy(self.buf.at[at], at, 6 + part, dev(2 - part))

        def core(self, delta, src=None):
            at = self.slot(2 * delta) if src is None else b
            return self.copy(self.buf.at[at] if src is None else src, at, (0, 8, 9)[delta], other)

        def core_half(self, part):
            at = (self.slot(6), pl.ds(64 * part, 64))
            return self.copy(self.buf.at[at], at, 10 + part, other)

        def send(self, src):
            for part in (0, 1):
                self.hop(1, part, src).start()
                self.hop(2, 1 - part, src).start()
            self.core(0, src).start()

        def pass_first(self):
            self.hop(1, 0).wait_recv()
            self.turn(0, 1).start()
            self.hop(2, 1).wait_recv()
            self.turn(1, 2).start()

        def pass_second(self):
            self.hop(1, 1).wait_recv()
            self.core(1).start()
            self.hop(2, 0).wait_recv()
            self.core(2).start()

        def pass_diagonal(self):
            for part in (0, 1):
                self.turn(part, 3).wait_recv()
                self.core_half(part).start()

        def wait_core(self, delta):
            at = self.slot(2 * delta + 1)
            if delta < 3:
                self.copy(self.buf.at[at], at, (0, 8, 9)[delta], other).wait_recv()
            else:
                for part in (0, 1):
                    half = (at, pl.ds(64 * part, 64))
                    self.copy(self.buf.at[half], half, 10 + part, other).wait_recv()

        def finish(self, src):
            self.core(0, src).wait_send()
            for part in (0, 1):
                self.hop(1, part, src).wait_send()
                self.hop(2, part, src).wait_send()
                self.turn(part, 1 + part).wait_send()
                self.core(1 + part).wait_send()
                self.core_half(part).wait_send()

    gx = Gather(r["xb"], r["gx_s"], r["gx_r"])
    gdy = Gather(r["dyb"], r["gdy_s"], r["gdy_r"])

    class Chain:
        def __init__(self, name, K, dtype, sink, place):
            self.K, self.dtype, self.sink, self.place = K, dtype, sink, place
            for part in ("own", "rl", "rr", "tu", "td", "su", "sd", "ru", "rd"):
                setattr(self, part, r[name + "_" + part])

        def up(self, src, k):
            return remote(src, self.rl.at[k], (self.su, k), (self.ru, k), (z + 1, b))

        def down(self, src, k):
            return remote(src, self.rr.at[k], (self.sd, k), (self.rd, k), (z - 1, b))

        def prime(self, k):
            if Z == 1:
                return

            @pl.when(z == 0)
            def _():
                self.up(self.own.at[k], k).start()

            @pl.when(z == Z - 1)
            def _():
                self.down(self.own.at[k], k).start()

        def tick(self, i):
            ku = i - 1 - SKEW * (z - 1)

            @pl.when((z > 0) & (z < Z - 1) & (ku >= 0) & (ku < self.K))
            def _():
                self.up(self.own.at[ku], ku).wait_recv()
                self.tu[ku] = (self.own[ku].astype(F32) + self.rl[ku].astype(F32)).astype(self.dtype)
                self.up(self.tu.at[ku], ku).start()

            kd = i - 1 - SKEW * (Z - 2 - z)

            @pl.when((z > 0) & (z < Z - 1) & (kd >= 0) & (kd < self.K))
            def _():
                self.down(self.own.at[kd], kd).wait_recv()
                self.td[kd] = (self.own[kd].astype(F32) + self.rr[kd].astype(F32)).astype(self.dtype)
                self.down(self.td.at[kd], kd).start()

            k = i - 1 - SKEW * max(Z - 2, 0)
            if 0 <= k < self.K:

                @pl.when(z == 0)
                def _():
                    if Z > 1:
                        self.down(self.own.at[k], k).wait_recv()
                    self.sink(k, self.own[k].astype(F32) + self.rr[k].astype(F32))

                @pl.when((z == Z - 1) & (z > 0))
                def _():
                    self.up(self.own.at[k], k).wait_recv()
                    self.sink(k, self.own[k].astype(F32) + self.rl[k].astype(F32))

                @pl.when((z > 0) & (z < Z - 1))
                def _():
                    self.sink(
                        k,
                        self.own[k].astype(F32) + self.rl[k].astype(F32) + self.rr[k].astype(F32),
                    )

                leave(*self.place(k))

        def finish(self):
            @pl.when(z < Z - 1)
            def _():
                for k in range(self.K):
                    self.up(self.own.at[k], k).wait_send()

            @pl.when(z > 0)
            def _():
                for k in range(self.K):
                    self.down(self.own.at[k], k).wait_send()

    leaving = []

    def leave(name, at):
        copy = pltpu.make_async_copy(r["s_" + name].at[at], r["o_" + name].at[at], r["out_sem"].at[len(leaving)])
        copy.start()
        leaving.append(copy)

    def place_a(k):
        if k < 8:
            return "fc2", (pl.ds(96 * (k // 2), 96), pl.ds(384 * (k % 2), 384))
        src = chip_at((k - 8) // 2)
        return "fc1", (slice(None), pl.ds(pl.multiple_of(768 * src + 384 * (k % 2), 128), 384))

    def place_b(k):
        return "qkv", (chip_at(k),)

    def place_p(k):
        return "proj", (slice(None), pl.ds(384 * k, 384))

    def sink_to(place):
        def sink(k, total):
            name, at = place(k)
            r["s_" + name][at] = total.astype(BF16)

        return sink

    def place_c(k):
        return "ln", (slice(None),)

    def sink_c(k, total):
        for i in range(8):
            r["lnc"][i] = total[:, 96 * i : 96 * i + 96]
        r["s_ln"][...] = r["lnc"][b]

    ca = Chain("ca", 16, BF16, sink_to(place_a), place_a)
    cb = Chain("cb", 4, BF16, sink_to(place_b), place_b)
    cp = Chain("cp", 2, BF16, sink_to(place_p), place_p)
    cc = Chain("cc", 1, F32, sink_c, place_c)
    line = ((ca, 0), (cb, 16), (cp, 20))
    beats = [0]

    def beat(count=1):
        for _ in range(count):
            beats[0] += 1
            for chain, first in line:
                if 1 <= beats[0] - first <= chain.K + SKEW * max(Z - 2, 0):
                    chain.tick(beats[0] - first)

    gx.send(r["x"])
    load("w_qkv", r["w_qkv"], r["wq"])
    load("w_proj", r["w_proj"], r["wp"])
    load("dy", r["dy"], r["dyb"].at[b])
    load("w_fc1", r["w_fc1"], r["w1"])
    load("w_fc2", r["w_fc2"], r["w2"])

    crop = [r["crops"][0, RUN_ROWS * i] for i in range(8)]
    places = []
    for i in range(8):
        place = 2 * crop[i]
        for h in range(i):
            place = place + jnp.where(crop[h] == crop[i], 1, 0)
        places.append(place)
        r["inv"][i] = place
    for s in range(8):
        run = jnp.int32(0)
        for i in range(8):
            run = run + jnp.where(places[i] == s, i, 0)
        r["perm"][s] = run

    g1, b1 = r["ln1_gain"][...].reshape(1, 768), r["ln1_bias"][...].reshape(1, 768)
    g2, b2 = r["ln2_gain"][...].reshape(1, 768), r["ln2_bias"][...].reshape(1, 768)

    loads["x"].wait()
    loads["w_qkv"].wait()

    def project(delta):
        gx.wait_core(delta)
        pair = pl.ds(2 * chip_at(delta), 2)
        hat, _ = norm_parts(r["xb"][pair].reshape(256, 768).astype(F32))
        normed = (hat * g1 + b1).astype(BF16)
        r["n1"][pair] = normed.reshape(2, 128, 768)
        for t in range(3):
            out = mm(normed, r["wq"][:, pl.ds(pl.multiple_of(768 * t + 384 * e, 128), 384)])
            out = out * scale if t == 0 else out
            r["qkv"][pair, :, 384 * t : 384 * t + 384] = out.astype(BF16).reshape(2, 128, 384)

    project(0)
    gx.pass_first()
    gdy.send(r["dy"])
    gx.pass_second()
    project(1)
    project(2)
    gx.pass_diagonal()
    project(3)

    low_lanes = lax.broadcasted_iota(jnp.int32, (1, 128), 1) < HEAD

    def stack(two):
        none = jnp.zeros_like(two)
        return jnp.concatenate([jnp.where(low_lanes, two, none), jnp.where(low_lanes, none, two)], axis=0)

    def o_core(at):
        place = (e, pl.ds(2 * at, 2))
        return remote(r["ob"].at[place], r["ob"].at[place], (r["o_s"], at), (r["o_r"], at), other)

    def attend(at, carry):
        run0, run1 = r["perm"][2 * at], r["perm"][2 * at + 1]
        outs = []
        for h in range(3):
            q, k, v = [
                jnp.concatenate(
                    [r["qkv"][run, :, 384 * t + 128 * h : 384 * t + 128 * h + 128] for run in (run0, run1)],
                    axis=0,
                )
                for t in range(3)
            ]
            s = mm_nt(stack(q), k)
            p = jnp.exp(s - jnp.max(s, axis=-1, keepdims=True))
            o = mm(p.astype(BF16), jnp.concatenate([v, jnp.ones_like(v)], axis=1))
            o = o[:, 0:128] / o[:, 128:256]
            outs.append(jnp.where(low_lanes, o[0:256], o[256:512]))
        low = jnp.concatenate(outs, axis=1).astype(BF16)
        r["ob"][e, pl.ds(2 * at, 2)] = low.reshape(2, 128, 384)
        o_core(at).start()
        return carry

    def by_perm(buf, first, count):
        return jnp.concatenate([buf[r["perm"][first + i]] for i in range(count)], axis=0)

    own_hidden = pl.ds(pl.multiple_of(384 * b, 128), 384)

    def feed(at):
        place = (1 - e, pl.ds(2 * at, 2))
        remote(r["ob"].at[place], r["ob"].at[place], (r["o_s"], at), (r["o_r"], at), other).wait_recv()
        pair = pl.ds(2 * at, 2)
        o = jnp.concatenate([r["ob"][i, pair].reshape(256, 384) for i in range(2)], axis=1)
        x1 = by_perm(r["xb"], 2 * at, 2).astype(F32) + mm(o, r["wp"][...])
        r["x1"][pair] = x1.reshape(2, 128, 768)
        hat, _ = norm_parts(x1)
        n2 = (hat * g2 + b2).astype(BF16)
        r["n2"][pair] = n2.reshape(2, 128, 768)
        u = mm(n2, r["w1"][:, own_hidden])
        r["u"][pair] = u.reshape(2, 128, 384)
        r["act"][pair] = gelu_pair(u)[0].astype(BF16).reshape(2, 128, 384)

    attend(0, 0)
    gdy.pass_first()
    attend(1, 0)
    for name in ("w_proj", "w_fc1", "w_fc2", "dy"):
        loads[name].wait()
    feed(0)
    gdy.pass_second()
    attend(2, 0)
    feed(1)
    attend(3, 0)
    feed(2)
    gdy.pass_diagonal()
    feed(3)
    for delta in range(4):
        gdy.wait_core(delta)

    grad = mm_tn(r["act"][...].reshape(1024, 384), by_perm(r["dyb"], 0, 8)).astype(BF16)
    for k in range(8):
        ca.own[k] = grad[96 * (k // 2) : 96 * (k // 2) + 96, 384 * (k % 2) : 384 * (k % 2) + 384]
        ca.prime(k)

    place_own = r["inv"][b]
    dy_own = r["dyb"][b]
    r["y"][...] = r["x1"][place_own]
    r["dn2"][...] = jnp.zeros((128, 768), F32)

    def own_rows(i, carry):
        part = pl.ds(768 * i, 768)
        act, slope = gelu_pair(mm(r["n2"][place_own], r["w1"][:, part]))
        du = (mm_nt(r["dyb"][b], r["w2"][part]) * slope).astype(BF16)
        r["dn2"][...] += mm_nt(du, r["w1"][:, part])
        r["y"][...] += mm(act.astype(BF16), r["w2"][part])
        return carry

    for i in range(4):
        own_rows(i, 0)
        if i == 2:
            beat()
    r["s_y"][...] = r["y"][...].astype(BF16)
    leave("y", (slice(None),))

    dn2 = r["dn2"][...]
    hat, inv_std = norm_parts(r["x1"][place_own])
    r["lnp"][2:3] = jnp.sum(dn2 * hat, axis=0, keepdims=True)
    r["lnp"][3:4] = jnp.sum(dn2, axis=0, keepdims=True)
    dx1 = dy_own.astype(F32) + norm_back(dn2, hat, inv_std, g2)
    r["dx1"][...] = dx1
    low = dx1.astype(BF16)
    do = mm_nt(low, r["wp"][...]).astype(BF16)
    for i in range(4):
        r["dos"][i] = do[:, 192 * i : 192 * i + 192]

    def do_send(delta):
        return remote(r["dos"].at[chip_at(delta)], r["dob"].at[b], (r["do_s"], 2 * delta), (r["do_r"], 2 * delta), dev(delta))

    def do_slot(m):
        return 2 * chip_at(m // 2) + (e if m % 2 == 0 else 1 - e)

    def do_core(delta):
        src = r["dos"].at[chip] if delta == 0 else r["dob"].at[do_slot(2 * delta)]
        return remote(src, r["dob"].at[do_slot(2 * delta)], (r["do_s"], 2 * delta + 1), (r["do_r"], 2 * delta + 1), other)

    for delta in (3, 2, 1):
        do_send(delta).start()
    do_core(0).start()
    r["dob"][b] = r["dos"][chip]
    beat()

    def back_hidden(c, carry):
        pair = pl.ds(2 * c, 2)
        da = mm_nt(by_perm(r["dyb"], 2 * c, 2), r["w2"][own_hidden])
        slope = gelu_pair(r["u"][pair].reshape(256, 384))[1]
        r["du"][pair] = (da * slope).astype(BF16).reshape(2, 128, 384)
        return carry

    for c in range(4):
        back_hidden(c, 0)
    beat()
    grad = mm_tn(r["n2"][...].reshape(1024, 768), r["du"][...].reshape(1024, 384)).astype(BF16)
    for i in range(8):
        r["t1"][i % 2, i // 2] = grad[96 * i : 96 * i + 96]
    t1_core = remote(r["t1"].at[1 - e], r["t1x"], r["t1_cs"], r["t1_cr"], other)
    t1_core.start()
    beat()

    def t1_send(delta, half):
        src = r["t1"].at[e, chip_at(delta)] if half == 0 else r["t1x"].at[chip_at(delta)]
        hidden_core = e if half == 0 else 1 - e
        at = 2 * delta + half
        return remote(src, ca.own.at[8 + 2 * delta + hidden_core], (r["t1_s"], at), (r["t1_r"], at), dev(delta))

    o = jnp.concatenate([r["ob"][i, place_own] for i in range(2)], axis=1)
    grad = mm_tn(o, low).astype(BF16)
    for i in range(8):
        r["tp"][i % 2, i // 2] = grad[96 * i : 96 * i + 96]
    tp_core = remote(r["tp"].at[1 - e], r["tpx"], r["tp_cs"], r["tp_cr"], other)
    tp_core.start()

    def tp_send(delta):
        return remote(r["tps"].at[delta], r["tpr"].at[delta], (r["tp_s"], delta), (r["tp_r"], delta), dev(delta))

    t1_core.wait_recv()
    for delta in (1, 2, 3):
        for half in (0, 1):
            t1_send(delta, half).start()
    ca.own[8 + e] = r["t1"][e, chip]
    ca.own[9 - e] = r["t1x"][chip]
    ca.prime(8)
    ca.prime(9)
    beat()

    for s in range(4):
        r["n1s"][s] = r["n1"][r["perm"][4 * e + s]]
    odd = lax.rem(chip, 2) == 1
    for t in range(3):
        first = pl.multiple_of(768 * t + 192 * chip - 64 * lax.rem(chip, 2), 128)
        four = mm(r["n1s"][...].reshape(512, 768), r["wq"][:, pl.ds(first, 256)])
        three = jnp.where(odd, four[:, 64:256], four[:, 0:192]).astype(BF16)
        r["qo"][:, :, 128 * t : 128 * t + 128] = three[:, 0:128].reshape(2, 256, 128)
        r["qo"][:, :, 384 + 64 * t : 448 + 64 * t] = three[:, 128:192].reshape(2, 256, 64)

    for delta in (1, 2, 3):
        do_send(delta).wait_recv()
        do_core(delta).start()
    for delta in range(4):
        at = do_slot(2 * delta + 1)
        remote(r["dob"].at[at], r["dob"].at[at], (r["do_s"], 2 * delta + 1), (r["do_r"], 2 * delta + 1), other).wait_recv()

    beat()

    def t1_arrive(delta):
        for half in (0, 1):
            t1_send(delta, half).wait_recv()
        ca.prime(8 + 2 * delta)
        ca.prime(9 + 2 * delta)

    def attend_back(at, heads):
        runs = [r["perm"][4 * e + 2 * at + i] for i in range(2)]
        if heads == 2:
            g = jnp.concatenate([r["dob"][run, :, 0:128] for run in runs], axis=0)
            q, k, v = [r["qo"][at, :, 128 * t : 128 * t + 128] for t in range(3)]
            q, g = stack(q), stack(g)
        else:
            g = jnp.concatenate([r["dob"][run, :, 128:192] for run in runs], axis=0)
            q, k, v = [r["qo"][at, :, 384 + 64 * t : 448 + 64 * t] for t in range(3)]
        q = (q.astype(F32) * scale).astype(BF16)
        s = mm_nt(q, k)
        p = jnp.exp(s - jnp.max(s, axis=-1, keepdims=True))
        p = p / jnp.sum(p, axis=-1, keepdims=True)
        dp = mm_nt(g, v)
        ds = (p * (dp - jnp.sum(p * dp, axis=-1, keepdims=True))).astype(BF16)
        dq = mm(ds, k) * scale
        dk = mm_tn(ds, q)
        dv = mm_tn(p.astype(BF16), g)
        mine = pl.ds(2 * (2 * e + at), 2)
        if heads == 2:
            dq = jnp.where(low_lanes, dq[0:256], dq[256:512])
        first, wide = (0, 128) if heads == 2 else (384, 64)
        for t, part in enumerate((dq, dk, dv)):
            r["dq"][mine, :, first + wide * t : first + wide * t + wide] = part.astype(BF16).reshape(2, 128, wide)

    attend_back(0, 2)
    beat()
    attend_back(0, 1)
    t1_arrive(1)
    beat()
    attend_back(1, 2)
    t1_arrive(2)
    attend_back(1, 1)

    dq_core = remote(r["dq"].at[pl.ds(4 * e, 4)], r["dq"].at[pl.ds(4 * e, 4)], r["dq_cs"], r["dq_cr"], other)
    dq_core.start()
    grad = mm_tn(r["n1s"][...].reshape(512, 768), r["dq"][pl.ds(4 * e, 4)].reshape(512, 576))
    for i in range(8):
        r["tq"][i % 2, i // 2] = grad[96 * i : 96 * i + 96].astype(BF16)
    tq_core = remote(r["tq"].at[1 - e], r["tqx"], r["tq_cs"], r["tq_cr"], other)
    tq_core.start()

    def tq_send(delta):
        return remote(r["tqs"].at[delta], cb.own.at[delta], (r["tq_s"], delta), (r["tq_r"], delta), dev(delta))

    def dq_send(delta, landing=None):
        landing = chip if landing is None else landing
        return remote(r["dqs"].at[delta], r["dqr"].at[landing], (r["dq_s"], delta), (r["dq_r"], delta), dev(delta))

    beat()

    t1_arrive(3)
    tq_core.wait_recv()
    for delta in (3, 2, 1, 0):
        c = chip_at(delta)
        total = (r["tq"][e, c].astype(F32) + r["tqx"][c].astype(F32)).astype(BF16)
        if delta == 0:
            cb.own[0] = total
        else:
            r["tqs"][delta] = total
            tq_send(delta).start()
    beat()
    at = pl.ds(4 - 4 * e, 4)
    remote(r["dq"].at[at], r["dq"].at[at], r["dq_cs"], r["dq_cr"], other).wait_recv()
    for delta in (3, 2, 1):
        r["dqs"][delta] = r["dq"][r["inv"][2 * chip_at(delta) + e]]
        dq_send(delta).start()
    tp_core.wait_recv()
    for delta in (3, 2, 1, 0):
        c = chip_at(delta)
        r["tps"][delta] = (r["tp"][e, c].astype(F32) + r["tpx"][c].astype(F32)).astype(BF16)
        if delta > 0:
            tp_send(delta).start()

    def beat_to(count):
        beat(count - beats[0])

    beat_to(12)
    cb.prime(0)
    beat_to(15)
    for delta in (1, 2, 3):
        tq_send(delta).wait_recv()
        cb.prime(delta)
    beat_to(18)
    r["dqr"][chip] = r["dq"][r["inv"][b]]
    for delta in (1, 2, 3):
        dq_send(delta, chip_at(delta)).wait_recv()
    for i in range(4):
        for t in range(3):
            first = 768 * t + 192 * i
            r["dnat"][:, first : first + 128] = r["dqr"][i, :, 128 * t : 128 * t + 128]
            r["dnat"][:, first + 128 : first + 192] = r["dqr"][i, :, 384 + 64 * t : 448 + 64 * t]
    dn1 = mm_nt(r["dnat"][...], r["wq"][...])
    hat, inv_std = norm_parts(r["xb"][b].astype(F32))
    r["lnp"][0:1] = jnp.sum(dn1 * hat, axis=0, keepdims=True)
    r["lnp"][1:2] = jnp.sum(dn1, axis=0, keepdims=True)
    r["lnp"][4:8] = jnp.zeros((4, 768), F32)
    r["s_gin"][...] = (r["dx1"][...] + norm_back(dn1, hat, inv_std, g1)).astype(BF16)
    leave("gin", (slice(None),))
    ln_core = remote(r["lnp"], r["lnx"].at[0], (r["ln_s"], 0), (r["ln_r"], 0), other)
    ln_core.start()
    beat_to(19)
    ln_core.wait_recv()
    r["lns"][...] = r["lnp"][...] + r["lnx"][0]

    def ln_send(delta):
        return remote(r["lns"], r["lnx"].at[delta], (r["ln_s"], delta), (r["ln_r"], delta), dev(delta))

    for delta in (3, 2, 1):
        ln_send(delta).start()
    beat_to(20)
    total = r["tps"][0].astype(F32)
    for delta in (1, 2, 3):
        tp_send(delta).wait_recv()
        total += r["tpr"][delta].astype(F32)
    for k in range(2):
        cp.own[k] = total[:, 384 * k : 384 * k + 384].astype(BF16)
        cp.prime(k)
    total = r["lns"][...]
    for delta in (1, 2, 3):
        ln_send(delta).wait_recv()
        total += r["lnx"][delta]
    cc.own[0] = total
    cc.prime(0)
    beat_to(22)
    cc.tick(1)
    beat_to(22 + SKEW)
    cc.tick(1 + SKEW)
    beat_to(22 + SKEW * max(Z - 2, 0))
    for hop in range(2, max(Z - 2, 0) + 1):
        cc.tick(1 + SKEW * hop)

    gx.finish(r["x"])
    gdy.finish(r["dy"])
    for at in range(4):
        o_core(at).wait_send()
    for copy in (t1_core, tp_core, tq_core, dq_core, ln_core, do_core(0)):
        copy.wait_send()
    for delta in (1, 2, 3):
        do_send(delta).wait_send()
        do_core(delta).wait_send()
        t1_send(delta, 0).wait_send()
        t1_send(delta, 1).wait_send()
        tp_send(delta).wait_send()
        tq_send(delta).wait_send()
        dq_send(delta).wait_send()
        ln_send(delta).wait_send()
    ca.finish()
    cb.finish()
    cp.finish()
    cc.finish()
    for copy in leaving:
        copy.wait()


def widen_kernel(*refs):
    sources, results, held, wide = refs[:7], refs[7:17], refs[17:24], refs[24:32]
    sem_in, sem_out = refs[32:]
    every = slice(None)
    pieces = [(4, (every, pl.ds(1024 * i, 1024))) for i in range(3)]
    pieces += [(5, (pl.ds(128 * i, 128), every)) for i in range(3)]
    pieces += [(2, (every,)), (3, (every,)), (6, (every,)), (0, (every,)), (1, (every,))]
    copies = []
    for n, (i, at) in enumerate(pieces):
        copies.append(pltpu.make_async_copy(sources[i].at[at], held[i].at[at], sem_in.at[n]))
        copies[-1].start()
    leaving = []

    def leave(src, dst):
        copy = pltpu.make_async_copy(src, dst, sem_out.at[len(leaving)])
        copy.start()
        leaving.append(copy)

    for (i, at), copy in zip(pieces, copies):
        copy.wait()
        part = held[i]
        if i < 2:
            leave(part, results[i])
        elif i == 2:
            for t in range(3):
                parts = []
                for c in range(4):
                    parts.append(part[c, :, 128 * t : 128 * t + 128])
                    parts.append(part[c, :, 384 + 64 * t : 448 + 64 * t])
                cols = (every, pl.ds(768 * t, 768))
                wide[0][cols] = jnp.concatenate(parts, axis=1).astype(F32)
                leave(wide[0].at[cols], results[2].at[cols])
        elif i < 6:
            wide[i - 2][at] = part[at].astype(F32)
            leave(wide[i - 2].at[at], results[i].at[at])
        else:
            for t in range(4):
                wide[4 + t][...] = part[t, :]
                leave(wide[4 + t], results[6 + t])
    for copy in leaving:
        copy.wait()


def fast_shards(
    Z, inputs, crops, ln1_gain, ln1_bias, w_qkv, w_proj, ln2_gain, ln2_bias, w_fc1, w_fc2, cotangent
):
    V, D = pltpu.VMEM, pltpu.SemaphoreType.DMA
    anyspace = pl.BlockSpec(memory_space=pl.ANY)
    vmem = pl.BlockSpec(memory_space=pltpu.VMEM)
    smem = pl.BlockSpec(memory_space=pltpu.SMEM)
    arguments = dict(
        x=(inputs[0], anyspace),
        crops=(crops, smem),
        ln1_gain=(ln1_gain, vmem),
        ln1_bias=(ln1_bias, vmem),
        w_qkv=(w_qkv, anyspace),
        w_proj=(w_proj, anyspace),
        ln2_gain=(ln2_gain, vmem),
        ln2_bias=(ln2_bias, vmem),
        w_fc1=(w_fc1, anyspace),
        w_fc2=(w_fc2, anyspace),
        dy=(cotangent[0], anyspace),
    )
    results = dict(
        o_y=((128, 768), BF16),
        o_gin=((128, 768), BF16),
        o_qkv=((4, 96, 576), BF16),
        o_proj=((96, 768), BF16),
        o_fc1=((96, 3072), BF16),
        o_fc2=((384, 768), BF16),
        o_ln=((8, 96), F32),
    )
    scratch = dict(
        ld_sem=D((6,)),
        perm=pltpu.SMEM((8,), jnp.int32),
        inv=pltpu.SMEM((8,), jnp.int32),
        xb=V((8, 128, 768), BF16), gx_s=D((12,)), gx_r=D((12,)),
        dyb=V((8, 128, 768), BF16), gdy_s=D((12,)), gdy_r=D((12,)),
        dob=V((8, 128, 192), BF16), dos=V((4, 128, 192), BF16), do_s=D((8,)), do_r=D((8,)),
        wq=V((768, 2304), BF16), dnat=V((128, 2304), BF16), wp=V((768, 768), BF16),
        w1=V((768, 3072), BF16), w2=V((3072, 768), BF16),
        n1=V((8, 128, 768), BF16), n1s=V((4, 128, 768), BF16), qkv=V((8, 128, 1152), BF16),
        ob=V((2, 8, 128, 384), BF16), o_s=D((4,)), o_r=D((4,)),
        x1=V((8, 128, 768), F32), n2=V((8, 128, 768), BF16),
        act=V((8, 128, 384), BF16), u=V((8, 128, 384), F32), du=V((8, 128, 384), BF16),
        y=V((128, 768), F32), dn2=V((128, 768), F32), dx1=V((128, 768), F32),
        t1=V((2, 4, 96, 384), BF16), t1x=V((4, 96, 384), BF16),
        t1_cs=D, t1_cr=D, t1_s=D((8,)), t1_r=D((8,)),
        tp=V((2, 4, 96, 768), BF16), tpx=V((4, 96, 768), BF16), tps=V((4, 96, 768), BF16), tpr=V((4, 96, 768), BF16),
        tp_cs=D, tp_cr=D, tp_s=D((4,)), tp_r=D((4,)),
        qo=V((2, 256, 576), BF16), dq=V((8, 128, 576), BF16),
        tq=V((2, 4, 96, 576), BF16), tqx=V((4, 96, 576), BF16), tqs=V((4, 96, 576), BF16),
        tq_cs=D, tq_cr=D, tq_s=D((4,)), tq_r=D((4,)),
        dqs=V((4, 128, 576), BF16), dqr=V((4, 128, 576), BF16),
        dq_cs=D, dq_cr=D, dq_s=D((4,)), dq_r=D((4,)),
        lnp=V((8, 768), F32), lns=V((8, 768), F32), lnx=V((4, 8, 768), F32), lnc=V((8, 8, 96), F32),
        ln_s=D((4,)), ln_r=D((4,)),
    )
    for name, K, shape, dtype in (
        ("ca", 16, (96, 384), BF16), ("cb", 4, (96, 576), BF16), ("cp", 2, (96, 384), BF16), ("cc", 1, (8, 768), F32)
    ):
        for part in ("own", "rl", "rr", "tu", "td"):
            scratch[name + "_" + part] = V((K, *shape), dtype)
        for part in ("su", "sd", "ru", "rd"):
            scratch[name + "_" + part] = D((K,))
    scratch.update({"s" + name[1:]: V(*shape) for name, shape in results.items()}, out_sem=D((25,)))
    names = (*arguments, *results, *scratch)
    narrow = pl.pallas_call(
        functools.partial(layer_kernel, Z, names),
        out_shape=[jax.ShapeDtypeStruct(*shape) for shape in results.values()],
        in_specs=[spec for _, spec in arguments.values()],
        out_specs=[anyspace] * len(results),
        scratch_shapes=list(scratch.values()),
        compiler_params=pltpu.CompilerParams(
            collective_id=0, has_side_effects=True, vmem_limit_bytes=60 * 2**20
        ),
    )(*[array for array, _ in arguments.values()])
    wide = [((128, 768), BF16), ((128, 768), BF16), ((96, 2304), F32), ((96, 768), F32), ((96, 3072), F32), ((384, 768), F32)]
    wide += [((96,), F32)] * 4
    y, gin, *grads = pl.pallas_call(
        widen_kernel,
        out_shape=[jax.ShapeDtypeStruct(*shape) for shape in wide],
        in_specs=[anyspace] * len(narrow),
        out_specs=[anyspace] * len(wide),
        scratch_shapes=[V(*shape) for shape in results.values()]
        + [V(*shape) for shape in wide[2:6]]
        + [V((96,), F32)] * 4
        + [D((11,)), D((16,))],
        compiler_params=pltpu.CompilerParams(vmem_limit_bytes=62 * 2**20),
    )(*narrow)
    return (y[None], gin[None], *grads)


def solution(mesh):
    placed = (
        P("dp", "blk", None),
        P("dp", None),
        P(),
        P(),
        P(),
        P(),
        P(),
        P(),
        P(),
        P(),
        P("dp", "blk", None),
    )
    def whole(*arrays):
        one_run = arrays[0].shape[1] == 8 * RUN_ROWS and mesh.shape["blk"] == 8
        body = functools.partial(fast_shards, mesh.shape["dp"]) if one_run else shards
        return placed_call(body)(*arrays)

    placed_call = lambda body: jax.shard_map(
        body,
        mesh=mesh,
        in_specs=placed,
        out_specs=(
            P("dp", "blk", None),
            P("dp", "blk", None),
            P("blk", None),
            P("blk", None),
            P("blk", None),
            P("blk", None),
            P("blk"),
            P("blk"),
            P("blk"),
            P("blk"),
        ),
        check_vma=False,
    )
    return whole
```
